32 devices in a mesh: seq: 8 (over y, x, core), stream: 4 (over z).
Axes of the slice: x: 2, y: 2, z: 4, core: 2. Of those that a mesh axis runs over, the one named last changes fastest.
Arguments:
- tokens: bfloat16 [32, 1024, 768], P('seq', 'stream'), may hold values from -6 to 6
- source_len: int32 [32], P('seq'), may hold values from 1 to 512, as said below
- target_len: int32 [32], P('seq'), may hold values from 1 to 512, as said below
- timesteps: int32 [32], P('seq'), may hold values from 0 to 1999
- cotangent: bfloat16 [32, 1024, 768], P('seq', 'stream'), may hold values from -6 to 6
- query_weight: float32 [768, 768], P(('seq', 'stream')), may hold values from -0.21875 to 0.21875
- query_bias: float32 [768], P(('seq', 'stream')), may hold values from -3 to 3
- key_weight: float32 [768, 768], P(('seq', 'stream')), may hold values from -0.21875 to 0.21875
- value_weight: float32 [768, 768], P(('seq', 'stream')), may hold values from -0.21875 to 0.21875
- value_bias: float32 [768], P(('seq', 'stream')), may hold values from -0.3 to 0.3
- out_weight: float32 [768, 768], P(('seq', 'stream')), may hold values from -3.5 to 3.5
- out_bias: float32 [768], P(('seq', 'stream')), may hold values from -3 to 3
- attn_gain: float32 [768], P(('seq', 'stream')), may hold values from 0.5 to 1.5
- attn_shift: float32 [768], P(('seq', 'stream')), may hold values from -2 to 2
- up_weight: float32 [768, 3072], P(('seq', 'stream')), may hold values from -0.21875 to 0.21875
- up_bias: float32 [3072], P(('seq', 'stream')), may hold values from -3 to 3
- down_weight: float32 [3072, 768], P(('seq', 'stream')), may hold values from -0.109375 to 0.109375
- down_bias: float32 [768], P(('seq', 'stream')), may hold values from -3 to 3
- ffn_gain: float32 [768], P(('seq', 'stream')), may hold values from 0.5 to 1.5
- ffn_shift: float32 [768], P(('seq', 'stream')), may hold values from -2 to 2
- stamp_weight: float32 [128, 768], P(('seq', 'stream')), may hold values from -0.5 to 0.5
- stamp_bias: float32 [768], P(('seq', 'stream')), may hold values from -3 to 3
- embed_weight: float32 [768, 768], P(('seq', 'stream')), may hold values from -0.21875 to 0.21875
- embed_bias: float32 [768], P(('seq', 'stream')), may hold values from -3 to 3
Outputs:
- output: bfloat16 [32, 1024, 768], P('seq', 'stream')
- token_grad: float32 [32, 1024, 768], P('seq', 'stream')
- query_weight_grad: float32 [768, 768], P(('seq', 'stream'))
- query_bias_grad: float32 [768], P(('seq', 'stream'))
- key_weight_grad: float32 [768, 768], P(('seq', 'stream'))
- value_weight_grad: float32 [768, 768], P(('seq', 'stream'))
- value_bias_grad: float32 [768], P(('seq', 'stream'))
- out_weight_grad: float32 [768, 768], P(('seq', 'stream'))
- out_bias_grad: float32 [768], P(('seq', 'stream'))
- attn_gain_grad: float32 [768], P(('seq', 'stream'))
- attn_shift_grad: float32 [768], P(('seq', 'stream'))
- up_weight_grad: float32 [768, 3072], P(('seq', 'stream'))
- up_bias_grad: float32 [3072], P(('seq', 'stream'))
- down_weight_grad: float32 [3072, 768], P(('seq', 'stream'))
- down_bias_grad: float32 [768], P(('seq', 'stream'))
- ffn_gain_grad: float32 [768], P(('seq', 'stream'))
- ffn_shift_grad: float32 [768], P(('seq', 'stream'))
- stamp_weight_grad: float32 [128, 768], P(('seq', 'stream'))
- stamp_bias_grad: float32 [768], P(('seq', 'stream'))
- embed_weight_grad: float32 [768, 768], P(('seq', 'stream'))
- embed_bias_grad: float32 [768], P(('seq', 'stream'))
The draws below stay inside these ranges and needn't reach their ends.
Inputs may be any that keep to these rules, and one draw needn't show every extreme that they name: `source_len`: in each aligned block of 4 sequences (those of one index of seq) one, chosen by the seed, has the full source length 512. `target_len`: in each aligned block of 4 sequences (those of one index of seq) one, chosen by the seed, has the full target length 512.
All inputs are finite; a program needn't handle non-finite values.
Results may differ from the reference program's by a relative error of at most 0.015.
The reference program's roundings to bfloat16 on the way count: a program that leaves them out, or rounds other values in their place, can miss the bound.
Values may be sent and summed in bfloat16 or wider, within the bound.
No kernel may reach another device: no remote copies, remote signals or barrier semaphores. Data moves between devices by JAX's collectives and lax.ppermute only.
A program may use at most 384 MiB of HBM per device.

```python
import math
from functools import partial
import jax
import jax.numpy as jnp
from jax import lax

D = 768
HEAD = 64
FF = 3072
TDIM = 128
SEQS = 4
SEQUENCES = 32
LENGTH = 1024
HALF_LEN = 512


def length_draw(key):
    group_count = SEQUENCES // SEQS
    chosen_index = jax.random.randint(jax.random.fold_in(key, 7), (group_count, 1), 0, SEQS)
    lengths_drawn = jax.random.randint(jax.random.fold_in(key, 11), (group_count, SEQS), 1, HALF_LEN + 1)
    chosen = jnp.arange(SEQS)[None, :] == chosen_index
    return jnp.where(chosen, HALF_LEN, lengths_drawn).reshape(SEQUENCES).astype(jnp.int32)


def draw_source_len(key, part):
    return length_draw(jax.random.fold_in(key, 1))


def draw_target_len(key, part):
    return length_draw(jax.random.fold_in(key, 2))


def with_ends(array, own_key, smallest, top_value):
    shape = array.shape
    index_at = [jax.random.randint(jax.random.fold_in(own_key, axis), (), 0, shape[axis]) for axis in range(len(shape))]
    array = array.at[tuple(index_at)].set(smallest)
    longest = shape.index(max(shape))
    index_at[longest] = (index_at[longest] + 1) % shape[longest]
    return array.at[tuple(index_at)].set(top_value)


def level_of(stream_key, dims, cuts, least, high):
    level, own = 1.0, jax.random.fold_in(stream_key, 6)
    for axis_at, blocks in cuts:
        steps = jnp.exp(jax.random.uniform(jax.random.fold_in(own, axis_at), (blocks,), jnp.float32, least / len(cuts), high / len(cuts)))
        level = level * jnp.repeat(steps, dims[axis_at] // blocks).reshape([-1 if axis == axis_at else 1 for axis in range(len(dims))])
    return level


def scatter_about(stream_key, dims, width, bound, shards=(), held_as=jnp.bfloat16):
    drawn = width * jax.random.normal(stream_key, dims, jnp.float32)
    if shards:
        drawn = drawn * level_of(stream_key, dims, shards, -0.22, 0.18)
    return jnp.clip(drawn, -bound, bound).astype(held_as)


def setup_inputs(seed: int = 0) -> dict:
    streams_of = jax.random.split(jax.random.key(seed), 25)
    return {
        "tokens": scatter_about(streams_of[0], (SEQUENCES, LENGTH, D), 1.0, 6.0, ((0, 8), (1, 4))),
        "source_len": draw_source_len(jax.random.fold_in(streams_of[24], 71), 0),
        "target_len": draw_target_len(jax.random.fold_in(streams_of[24], 71), 0),
        "timesteps": with_ends(jax.random.randint(streams_of[3], (SEQUENCES,), 0, 2000), jax.random.fold_in(streams_of[3], 1), 0, 1999).astype(jnp.int32),
        "cotangent": scatter_about(streams_of[4], (SEQUENCES, LENGTH, D), 1.0, 6.0, ((0, 8), (1, 4))),
        "query_weight": scatter_about(streams_of[5], (D, D), D ** -0.5, 0.21875, ((0, 32),), jnp.float32),
        "query_bias": scatter_about(streams_of[6], (D,), 0.5, 3.0, ((0, 32),), jnp.float32),
        "key_weight": scatter_about(streams_of[7], (D, D), D ** -0.5, 0.21875, ((0, 32),), jnp.float32),
        "value_weight": scatter_about(streams_of[8], (D, D), D ** -0.5, 0.21875, ((0, 32),), jnp.float32),
        "value_bias": scatter_about(streams_of[9], (D,), 0.05, 0.3, ((0, 32),), jnp.float32),
        "out_weight": scatter_about(streams_of[10], (D, D), 3 ** -0.5, 3.5, ((0, 32),), jnp.float32),
        "out_bias": scatter_about(streams_of[11], (D,), 0.5, 3.0, ((0, 32),), jnp.float32),
        "attn_gain": jnp.clip(1.0 + 0.1 * jax.random.normal(streams_of[12], (D,), jnp.float32), 0.5, 1.5),
        "attn_shift": scatter_about(streams_of[13], (D,), 0.3, 2.0, ((0, 32),), jnp.float32),
        "up_weight": scatter_about(streams_of[14], (D, FF), D ** -0.5, 0.21875, ((0, 32),), jnp.float32),
        "up_bias": scatter_about(streams_of[15], (FF,), 0.5, 3.0, ((0, 32),), jnp.float32),
        "down_weight": scatter_about(streams_of[16], (FF, D), FF ** -0.5, 0.109375, ((0, 32),), jnp.float32),
        "down_bias": scatter_about(streams_of[17], (D,), 0.5, 3.0, ((0, 32),), jnp.float32),
        "ffn_gain": jnp.clip(1.0 + 0.1 * jax.random.normal(streams_of[18], (D,), jnp.float32), 0.5, 1.5),
        "ffn_shift": scatter_about(streams_of[19], (D,), 0.3, 2.0, ((0, 32),), jnp.float32),
        "stamp_weight": scatter_about(streams_of[20], (TDIM, D), TDIM ** -0.5, 0.5, ((0, 32),), jnp.float32),
        "stamp_bias": scatter_about(streams_of[21], (D,), 0.5, 3.0, ((0, 32),), jnp.float32),
        "embed_weight": scatter_about(streams_of[22], (D, D), D ** -0.5, 0.21875, ((0, 32),), jnp.float32),
        "embed_bias": scatter_about(streams_of[23], (D,), 0.5, 3.0, ((0, 32),), jnp.float32),
    }


@jax.custom_vjp
def low(v):
    return lax.optimization_barrier(v.astype(jnp.bfloat16)).astype(jnp.float32)

@jax.custom_vjp
def low_back(v):
    return v

def low_keep(v):
    return (low(v), None)

def low_pass(kept, grad):
    return (grad,)

def back_keep(v):
    return (v, None)

def back_low(kept, grad):
    return (low(grad),)
low.defvjp(low_keep, low_pass)
low_back.defvjp(back_keep, back_low)

def both_ways(value):
    return low(low_back(value))

def product(left, right):
    return jnp.dot(left, right, precision=lax.Precision.HIGHEST)

def layer_norm(values, gain, shift):
    average = lax.optimization_barrier(jnp.mean(values, -1, keepdims=True))
    centred = values - average
    spread = lax.optimization_barrier(jnp.mean(centred * centred, -1, keepdims=True))
    return centred * lax.rsqrt(spread + 1e-05) * gain + shift

def stamp_features(stamps, feature_width):
    halfway = feature_width // 2
    rates = jnp.exp(-math.log(10000.0) * jnp.arange(halfway, dtype=jnp.float32) / halfway)
    angles = stamps.astype(jnp.float32)[..., None] * rates
    return jnp.concatenate([jnp.sin(angles), jnp.cos(angles)], axis=-1)

def sequence_layer(params, tokens, source_len, target_len, stamp):
    query_weight, query_bias, key_weight, value_weight, value_bias, out_weight, out_bias, attn_gain, attn_shift, up_weight, up_bias, down_weight, down_bias, ffn_gain, ffn_shift, stamp_weight, stamp_bias, embed_weight, embed_bias = params
    length = tokens.shape[0]
    halfway = length // 2
    head_count = query_weight.shape[1] // HEAD
    score_scale = 1.0 / math.sqrt(HEAD)
    places = jnp.arange(length)
    live = jnp.where(places < halfway, places < source_len, places - halfway < target_len)
    target = (places >= halfway).astype(jnp.float32)
    features = low(stamp_features(stamp, stamp_weight.shape[0]))
    stamp_hidden = low(jax.nn.silu(product(features[None, :], stamp_weight) + stamp_bias))
    embedded = product(stamp_hidden, embed_weight) + embed_bias
    mixed_in = tokens + target[:, None] * embedded
    inputs = low(mixed_in)
    queries = both_ways(product(inputs, query_weight) + query_bias).reshape(length, head_count, HEAD)
    key_rows = both_ways(product(inputs, key_weight)).reshape(length, head_count, HEAD)
    value_rows = both_ways(product(inputs, value_weight) + value_bias).reshape(length, head_count, HEAD)
    raw_scores = jnp.einsum('qhe,khe->hqk', queries, key_rows, precision=lax.Precision.HIGHEST) * score_scale
    scores = jnp.where(live[None, None, :], low_back(raw_scores), -1e+30)
    row_peak = lax.optimization_barrier(jnp.max(scores, -1, keepdims=True))
    powered = jnp.exp(scores - row_peak)
    attn_probs = powered / lax.optimization_barrier(jnp.sum(powered, -1, keepdims=True))
    attended = jnp.einsum('hqk,khe->qhe', low(attn_probs), value_rows, precision=lax.Precision.HIGHEST)
    attended = both_ways(attended.reshape(length, head_count * HEAD))
    branch = low_back(product(attended, out_weight) + out_bias)
    normed = layer_norm(mixed_in + branch, attn_gain, attn_shift)
    up_pre = low_back(product(low(normed), up_weight) + up_bias)
    gelued = low(jax.nn.gelu(up_pre, approximate=False))
    down_out = low_back(product(gelued, down_weight) + down_bias)
    result = layer_norm(normed + down_out, ffn_gain, ffn_shift)
    return result * live[:, None].astype(jnp.float32)

def reference(tokens, source_len, target_len, timesteps, cotangent, query_weight, query_bias, key_weight, value_weight, value_bias, out_weight, out_bias, attn_gain, attn_shift, up_weight, up_bias, down_weight, down_bias, ffn_gain, ffn_shift, stamp_weight, stamp_bias, embed_weight, embed_bias):
    masters = (query_weight, query_bias, key_weight, value_weight, value_bias, out_weight, out_bias, attn_gain, attn_shift, up_weight, up_bias, down_weight, down_bias, ffn_gain, ffn_shift, stamp_weight, stamp_bias, embed_weight, embed_bias)
    sequence_count = tokens.shape[0]
    group_size = 4 if sequence_count % 4 == 0 else 1
    blocks = sequence_count // group_size

    def forward(token_values, master_values):
        rounded = tuple((low(master) for master in master_values))
        per_group = jax.vmap(partial(sequence_layer, rounded))

        def one_group(packed):
            return per_group(packed[0], packed[1], packed[2], packed[3])
        packed = (token_values.reshape(blocks, group_size, token_values.shape[1], token_values.shape[2]), source_len.reshape(blocks, group_size), target_len.reshape(blocks, group_size), timesteps.reshape(blocks, group_size))
        outcome = lax.map(jax.checkpoint(one_group), packed)
        return outcome.reshape(token_values.shape)
    outputs, pullback = jax.vjp(forward, tokens.astype(jnp.float32), masters)
    token_grad, weight_grads = pullback(cotangent.astype(jnp.float32))
    return (outputs.astype(jnp.bfloat16), token_grad, weight_grads[0], weight_grads[1], weight_grads[2], weight_grads[3], weight_grads[4], weight_grads[5], weight_grads[6], weight_grads[7], weight_grads[8], weight_grads[9], weight_grads[10], weight_grads[11], weight_grads[12], weight_grads[13], weight_grads[14], weight_grads[15], weight_grads[16], weight_grads[17], weight_grads[18])
```

```python
import functools
import math

import jax
import jax.numpy as jnp
from jax import lax
from jax.experimental import pallas as pl
from jax.experimental.pallas import tpu as pltpu
from jax.sharding import PartitionSpec as P

F32=jnp.float32; BF=jnp.bfloat16
NT=(((1,),(1,)),((),())); NN=(((1,),(0,)),((),())); TN=(((0,),(0,)),((),()))
def mm(a,b,dims): return lax.dot_general(a,b,dims,preferred_element_type=F32)
def lanes(shape): return lax.broadcasted_iota(jnp.int32,shape,len(shape)-1)
def split3(x):
    hi=x.astype(BF).astype(F32); r=x-hi
    mid=r.astype(BF).astype(F32); lo=r-mid
    return hi,mid,lo
QB=256
def fwd_kernel(q_ref,k_ref,v_ref,auxk_ref,o_ref,auxq_ref,kaug,vm):
    i=pl.program_id(1)
    @pl.when(i==0)
    def _():
        k=k_ref[...]; v=v_ref[...]; ln=lanes(k.shape)
        z=jnp.zeros_like(k)
        for e in range(2):
            sel=(ln<64) if e==0 else (ln>=64)
            kaug[e,:,:128]=jnp.where(sel,k,z)
            kaug[e,:,128:]=auxk_ref[...]
            vm[e]=jnp.where(sel,v,z)
    q=q_ref[...]
    one=jnp.where(lanes(q.shape)==64,1.0,0.0).astype(BF)
    qa=jnp.concatenate([q,one],axis=1)
    out=None; ln=lanes((QB,128)); aux=jnp.where(ln==64,1.0,0.0)
    for e in range(2):
        s=mm(qa,kaug[e],NT)
        m=jnp.max(s,axis=1,keepdims=True)
        p=jnp.exp(s-m)
        l=jnp.sum(p,axis=1,keepdims=True)
        o=mm(p.astype(BF),vm[e],NN)*(1.0/l)
        out=o if out is None else out+o
        hi,mid,lo=split3(-(m+jnp.log(l)))
        aux=jnp.where(ln==3*e,hi,aux); aux=jnp.where(ln==3*e+1,mid,aux); aux=jnp.where(ln==3*e+2,lo,aux)
    o_ref[...]=out.astype(BF)
    auxq_ref[...]=aux.astype(BF)[None]
def attn_fwd(q,k,v,auxk,p0,np_):
    L=q.shape[0]
    return pl.pallas_call(fwd_kernel,grid=(np_,L//QB),
      in_specs=[pl.BlockSpec((QB,128),lambda p,i:(i,p0+p)),pl.BlockSpec((L,128),lambda p,i:(0,p0+p)),
        pl.BlockSpec((L,128),lambda p,i:(0,p0+p)),pl.BlockSpec((L,128),lambda p,i:(0,0))],
      out_specs=[pl.BlockSpec((QB,128),lambda p,i:(i,p)),pl.BlockSpec((1,QB,128),lambda p,i:(p,i,0))],
      out_shape=[jax.ShapeDtypeStruct((L,128*np_),BF),jax.ShapeDtypeStruct((np_,L,128),BF)],
      scratch_shapes=[pltpu.VMEM((2,L,256),BF),pltpu.VMEM((2,L,128),BF)],
      compiler_params=pltpu.CompilerParams(vmem_limit_bytes=56*2**20),
      cost_estimate=pl.CostEstimate(flops=np_*2*L*L*64*4,bytes_accessed=np_*L*128*2*5,transcendentals=np_*2*L*L),
      name="attn_fwd")(q,k,v,auxk)
def bwd_kernel(p0,q_ref,k_ref,v_ref,do_ref,auxk_ref,auxq_ref,auxd_ref,dq_ref,dk_ref,dv_ref,kaug,vaug,qa,doa,qm,dom,dk_acc,dv_acc):
    pair=p0+pl.program_id(0)
    L=q_ref.shape[0]
    k=k_ref[...]; v=v_ref[...]; q=q_ref[...]; do=do_ref[...]
    ln=lanes(k.shape); z=jnp.zeros_like(k); auxk=auxk_ref[...]
    qa[:,:128]=q; qa[:,128:]=auxq_ref[0]
    doa[:,:128]=do; doa[:,128:]=auxd_ref[...]
    for e in range(2):
        sel=(ln<64) if e==0 else (ln>=64)
        on=(ln>=3*e)&(ln<3*e+3)
        kaug[e,:,:128]=jnp.where(sel,k,z)
        kaug[e,:,128:]=jnp.where(on,jnp.ones_like(k),auxk)
        vaug[e,:,:128]=jnp.where(sel,v,z)
        b=6*pair+3*e
        vaug[e,:,128:]=jnp.where((ln>=b)&(ln<b+3),jnp.ones_like(k),z)
        qm[e]=jnp.where(sel,q,z)
        dom[e]=jnp.where(sel,do,z)
    for i in range(L//QB):
        r=pl.ds(i*QB,QB)
        dq=None
        for e in range(2):
            p=jnp.exp(mm(kaug[e],qa[r,:],NT))
            dp=mm(vaug[e],doa[r,:],NT)
            ds=(p*dp).astype(BF)
            dv=mm(p.astype(BF),dom[e,r,:],NN)
            dk=mm(ds,qm[e,r,:],NN)
            if i==0 and e==0: dv_acc[...]=dv; dk_acc[...]=dk
            else: dv_acc[...]+=dv; dk_acc[...]+=dk
            d=mm(ds,kaug[e,:,:128],TN)
            dq=d if dq is None else dq+d
        dq_ref[r,:]=(dq*0.125).astype(BF)
    dk_ref[...]=dk_acc[...].astype(BF)
    dv_ref[...]=dv_acc[...].astype(BF)
def attn_bwd(q,k,v,do,auxk,auxq,auxd,p0,np_):
    L=q.shape[0]
    col=lambda: pl.BlockSpec((L,128),lambda p:(0,p0+p))
    con=lambda: pl.BlockSpec((L,128),lambda p:(0,0))
    oc=lambda: pl.BlockSpec((L,128),lambda p:(0,p))
    return pl.pallas_call(functools.partial(bwd_kernel,p0),grid=(np_,),
      in_specs=[col(),col(),col(),col(),con(),pl.BlockSpec((1,L,128),lambda p:(p,0,0)),con()],
      out_specs=[oc(),oc(),oc()],
      out_shape=[jax.ShapeDtypeStruct((L,128*np_),BF)]*3,
      scratch_shapes=[pltpu.VMEM((2,L,256),BF),pltpu.VMEM((2,L,256),BF),pltpu.VMEM((L,256),BF),pltpu.VMEM((L,256),BF),
        pltpu.VMEM((2,L,128),BF),pltpu.VMEM((2,L,128),BF),pltpu.VMEM((L,128),F32),pltpu.VMEM((L,128),F32)],
      compiler_params=pltpu.CompilerParams(vmem_limit_bytes=56*2**20),
      cost_estimate=pl.CostEstimate(flops=np_*2*L*L*64*10,bytes_accessed=np_*L*128*2*9,transcendentals=np_*2*L*L),
      name="attn_bwd")(q,k,v,do,auxk,auxq,auxd)

Q_B,V_B,STAMP_B,EMBED_B=0,1,8,9
ORDER=(0,2,4,6,1,3,5,7)
def rows_at(me,t,n):
    return pl.ds(pl.multiple_of(jnp.bitwise_xor(me,ORDER[t])*n,n),n)
def sds(*a): return jax.ShapeDtypeStruct(*a)
def once(s): return pl.BlockSpec(s.shape,lambda i:(0,)*len(s.shape),pipeline_mode=pl.Buffered(1))
def smem(): return pl.BlockSpec(memory_space=pltpu.SMEM)
def anyw(): return pl.BlockSpec(memory_space=pl.ANY)
def load_weights(me,pieces,base,n,dst,sem):
    return [pltpu.make_async_copy(p.at[pl.ds(base,n),:],dst.at[rows_at(me,t,n),:],sem) for t,p in enumerate(pieces)]
def in_kernel(nt,me_ref,info_ref,feat_ref,vec_ref,*rest):
    toks=rest[:nt]; pieces=rest[nt:nt+8]
    mixed_ref,inp_ref,q_ref,k_ref,v_ref,auxk_ref,pre_ref,hid_ref, tok,wq,wk,wv,we,ws,emb,sems=rest[nt+8:]
    i=pl.program_id(0); me=me_ref[0]
    D=wq.shape[0]; n=D//8; ns=ws.shape[0]//8
    tcp=[pltpu.make_async_copy(t,tok.at[c],sems.at[5+c]) for c,t in enumerate(toks)]
    scp=[pltpu.make_async_copy(p.at[pl.ds(4*n,ns),:],ws.at[pl.ds(t*ns,ns),:],sems.at[0]) for t,p in enumerate(pieces)]
    wcp=[load_weights(me,pieces,w*n,n,dst,sems.at[1+w]) for w,dst in enumerate((wq,wk,wv,we))]
    vec=lambda r: vec_ref[pl.ds(r,1),:].astype(F32)
    @pl.when(i==0)
    def _():
        for c in scp+wcp[3]+tcp[:1]+wcp[0]+wcp[1]+wcp[2]+tcp[1:]: c.start()
        for c in scp: c.wait()
        pre=mm(feat_ref[...],ws[...],NN)+vec(STAMP_B)
        pre_ref[...]=pre
        hid=(pre/(1.0+jnp.exp(-pre))).astype(BF)
        hid_ref[...]=hid
        for c in wcp[3]: c.wait()
        emb[...]=mm(hid,we[...],NN)+vec(EMBED_B)
    for c in range(nt):
        @pl.when(i==c)
        def _(): tcp[c].wait()
    flag=info_ref[i,0].astype(F32); nlive=info_ref[i,1]
    x=tok[i].astype(F32)+flag*emb[pl.ds(0,1),:]
    mixed_ref[...]=x
    xb=x.astype(BF); inp_ref[...]=xb
    R=x.shape[0]
    ln=lanes((R,128)); row=lax.broadcasted_iota(jnp.int32,(R,128),0)
    auxk_ref[...]=jnp.where((ln==64)&(row>=nlive),-1e30,0.0).astype(BF)
    @pl.when(i==0)
    def _():
        for w in range(3):
            for c in wcp[w]: c.wait()
    q=(mm(xb,wq[...],NN)+vec(Q_B)).astype(BF)
    q_ref[...]=(q.astype(F32)*0.125).astype(BF)
    k_ref[...]=mm(xb,wk[...],NN).astype(BF)
    v_ref[...]=(mm(xb,wv[...],NN)+vec(V_B)).astype(BF)
def project(me,info,feat,vec,toks,pieces):
    nt=len(toks); R,D=toks[0].shape; n=D//8; ns=pieces[0].shape[0]-4*n; L=nt*R
    row=lambda w: pl.BlockSpec((R,w),lambda i:(i,0))
    full=lambda a: pl.BlockSpec(a.shape,lambda i:(0,)*a.ndim)
    outs=[sds((L,D),F32)]+[sds((L,D),BF)]*4+[sds((L,128),BF),sds((8,D),F32),sds((8,D),BF)]
    return pl.pallas_call(functools.partial(in_kernel,nt),grid=(nt,),
      in_specs=[smem(),smem(),full(feat),full(vec)]+[anyw()]*(nt+8),
      out_specs=[row(D)]*5+[row(128),once(outs[6]),once(outs[7])],
      out_shape=outs,
      scratch_shapes=[pltpu.VMEM((nt,R,D),BF)]+[pltpu.VMEM((D,D),BF)]*4+[pltpu.VMEM((8*ns,D),BF),pltpu.VMEM((8,D),F32),pltpu.SemaphoreType.DMA((5+nt,))],
      compiler_params=pltpu.CompilerParams(vmem_limit_bytes=48*2**20),
      cost_estimate=pl.CostEstimate(flops=2*L*D*D*3,bytes_accessed=20_000_000,transcendentals=0),
      name="project")(me,info,feat,vec,*toks,*pieces)

def token_kernel(nc,me_ref,info_ref,ga_ref,*rest):
    dq=rest[:nc]; dk=rest[nc:2*nc]; dv=rest[2*nc:3*nc]; pieces=rest[3*nc:3*nc+8]
    tg_ref,ge_ref,wq,wk,wv,sems=rest[3*nc+8:]
    i=pl.program_id(0); me=me_ref[0]
    D=wq.shape[0]; n=D//8
    wcp=[load_weights(me,pieces,w*n,n,dst,sems.at[w]) for w,dst in enumerate((wq,wk,wv))]
    @pl.when(i==0)
    def _():
        for w in wcp:
            for c in w: c.start()
        ge_ref[...]=jnp.zeros_like(ge_ref)
    g=ga_ref[...]
    for w,(src,dst) in enumerate(((dq,wq),(dk,wk),(dv,wv))):
        @pl.when(i==0)
        def _():
            for c in wcp[w]: c.wait()
        g=g+mm(jnp.concatenate([s[...] for s in src],axis=1),dst[...],NT)
    tg_ref[0]=g.astype(BF)
    ge_ref[pl.ds(0,1),:]+=info_ref[i,0].astype(F32)*jnp.sum(g,axis=0,keepdims=True)
def token_grads(me,info,ga,dq,dk,dv,pieces,R):
    L,D=ga.shape; nt=L//R; nc=len(dq); W=dq[0].shape[1]
    outs=[sds((nt,R,D),BF),sds((8,D),F32)]
    return pl.pallas_call(functools.partial(token_kernel,nc),grid=(nt,),
      in_specs=[smem(),smem(),pl.BlockSpec((R,D),lambda i:(i,0))]+[pl.BlockSpec((R,W),lambda i:(i,0))]*(3*nc)+[anyw()]*8,
      out_specs=[pl.BlockSpec((1,R,D),lambda i:(i,0,0)),once(outs[1])],
      out_shape=outs,
      scratch_shapes=[pltpu.VMEM((D,D),BF)]*3+[pltpu.SemaphoreType.DMA((3,))],
      compiler_params=pltpu.CompilerParams(vmem_limit_bytes=48*2**20),
      cost_estimate=pl.CostEstimate(flops=2*L*D*D*3,bytes_accessed=15_000_000,transcendentals=0),
      name="token_grads")(me,info,ga,*dq,*dk,*dv,*pieces)

def spread3(row):
    hi,mid,lo=split3(row)
    r=lax.broadcasted_iota(jnp.int32,(8,row.shape[1]),0)
    return jnp.where(r==0,hi,jnp.where(r==1,mid,jnp.where(r==2,lo,0.0))).astype(BF)
def three(rows):
    r=lax.broadcasted_iota(jnp.int32,rows.shape,0)
    return jnp.where(r<3,jnp.broadcast_to(rows[0:1,:].astype(F32),rows.shape),0.0).astype(BF)
def weight_kernel(nc,me_ref,inp_ref,ge_ref,pre_ref,hid_ref,feat_ref,*rest):
    dq=rest[:nc]; dk=rest[nc:2*nc]; dv=rest[2*nc:3*nc]; pieces=rest[3*nc:3*nc+8]
    mine_ref,theirs_ref,small_ref,dvec_ref,we,scr,sem=rest[3*nc+8:]
    me=me_ref[0]; D=we.shape[0]; n=D//8
    cps=load_weights(me,pieces,3*n,n,we,sem.at[0])
    for c in cps: c.start()
    def put(w,val):
        scr[...]=val
        for t in range(8):
            dst=mine_ref if t<4 else theirs_ref
            dst[t%4,w*n:(w+1)*n,:]=scr[rows_at(me,t,n),:].astype(BF)
    x=inp_ref[...]
    dvec_ref[...]=jnp.zeros_like(dvec_ref)
    for w,src in enumerate((dq,dk,dv)):
        y=jnp.concatenate([s[...] for s in src],axis=1)
        if w!=1: dvec_ref[pl.ds(w//2,1),:]=jnp.sum(y.astype(F32),axis=0,keepdims=True)
        put(w,mm(x,y,TN))
    ge=ge_ref[0:1,:]
    put(3,mm(three(hid_ref[...]),spread3(ge),TN))
    for c in cps: c.wait()
    gh=jnp.sum(mm(spread3(ge),we[...],NT),axis=0,keepdims=True)
    pre=pre_ref[0:1,:]
    sg=1.0/(1.0+jnp.exp(-pre))
    gs=gh*(sg*(1.0+pre*(1.0-sg)))
    dvec_ref[pl.ds(2,1),:]=gs
    dvec_ref[pl.ds(3,1),:]=ge
    small_ref[...]=mm(three(feat_ref[...]),spread3(gs),TN)
def weight_grads(me,inp,ge,pre,hid,feat,dq,dk,dv,pieces):
    L,D=inp.shape; n=D//8; nc=len(dq)
    outs=[sds((4,4*n,D),BF),sds((4,4*n,D),BF),sds((feat.shape[1],D),F32),sds((8,D),F32)]
    vm=pl.BlockSpec(memory_space=pltpu.VMEM)
    return pl.pallas_call(functools.partial(weight_kernel,nc),
      in_specs=[smem()]+[vm]*(5+3*nc)+[anyw()]*8,
      out_specs=[vm]*4,out_shape=outs,
      scratch_shapes=[pltpu.VMEM((D,D),BF),pltpu.VMEM((D,D),F32),pltpu.SemaphoreType.DMA((1,))],
      compiler_params=pltpu.CompilerParams(vmem_limit_bytes=48*2**20),
      cost_estimate=pl.CostEstimate(flops=2*L*D*D*3,bytes_accessed=12_000_000,transcendentals=0),
      name="weight_grads")(me,inp,ge,pre,hid,feat,*dq,*dk,*dv,*pieces)

INV_SQRT2=0.7071067811865476; INV_SQRT2PI=0.3989422804014327
HEAD=64
RB=256; FC=512
def norm_stats(x):
    mu=jnp.mean(x,axis=1,keepdims=True); c=x-mu
    r=lax.rsqrt(jnp.mean(c*c,axis=1,keepdims=True)+1e-5)
    return c*r,r
def norm_back(e,n,r):
    return r*(e-jnp.mean(e,axis=1,keepdims=True)-n*jnp.mean(e*n,axis=1,keepdims=True))
def colsum(x): return jnp.sum(x,axis=0,keepdims=True)
OUT_B,ATT_G,ATT_S,DOWN_B,FFN_G,FFN_S=2,3,4,5,6,7
def mid_kernel(nblk,me_ref,info_ref,mix_ref,cot_ref,att_refs,vec_ref,upb_ref,wod_p,wu_p,
        out_ref,gas_ref,gatt_ref,auxd_ref,dwod_m,dwod_t,dwu_m,dwu_t,dvec_ref,dupb_ref,
        wo,wd,wu,awo,awd,awu,gel,dgel,sems):
    i=pl.program_id(0); nb=pl.num_programs(0)
    D=wo.shape[0]; FF=wd.shape[0]; ro=D//nblk; rd=FF//nblk
    me=me_ref[0]
    cps=[load_weights(me,wod_p,0,ro,wo,sems.at[0]),load_weights(me,wu_p,0,ro,wu,sems.at[1]),
        load_weights(me,wod_p,ro,rd,wd,sems.at[2])]
    def wait(which):
        @pl.when(i==0)
        def _():
            for c in cps[which]: c.wait()
    @pl.when(i==0)
    def _():
        for w in cps:
            for c in w: c.start()
        awo[...]=jnp.zeros_like(awo); awd[...]=jnp.zeros_like(awd); awu[...]=jnp.zeros_like(awu)
        dvec_ref[...]=jnp.zeros_like(dvec_ref); dupb_ref[...]=jnp.zeros_like(dupb_ref)
    vec=lambda r: vec_ref[pl.ds(r,1),:].astype(F32)
    nlive=info_ref[i,1]
    x0=mix_ref[...]
    live=(lax.broadcasted_iota(jnp.int32,(RB,1),0)<nlive).astype(F32)
    wait(0)
    att=jnp.concatenate([a[...] for a in att_refs],axis=1)
    asum=x0+(mm(att,wo[...],NN)+vec(OUT_B))
    n1,r1=norm_stats(asum)
    normed=n1*vec(ATT_G)+vec(ATT_S)
    hid=normed.astype(BF)
    wait(1); wait(2)
    down=None
    for f in range(FF//FC):
        c=slice(f*FC,(f+1)*FC)
        u=mm(hid,wu[:,c],NN)+upb_ref[:,c].astype(F32)
        ph=0.5+0.5*lax.erf(u*INV_SQRT2)
        pd=jnp.exp(u*u*-0.5)*INV_SQRT2PI
        g=(u*ph).astype(BF)
        gel[:,c]=g
        dgel[:,c]=ph+u*pd
        t=mm(g,wd[c,:],NN)
        down=t if down is None else down+t
    fsum=normed+(down+vec(DOWN_B))
    n2,r2=norm_stats(fsum)
    g2=vec(FFN_G)
    out_ref[0]=((n2*g2+vec(FFN_S))*live).astype(BF)
    og=cot_ref[0].astype(F32)*live
    dvec_ref[pl.ds(FFN_G,1),:]+=colsum(og*n2)
    dvec_ref[pl.ds(FFN_S,1),:]+=colsum(og)
    gf=norm_back(og*g2,n2,r2)
    gd=gf.astype(BF)
    dvec_ref[pl.ds(DOWN_B,1),:]+=colsum(gd.astype(F32))
    gn=gf
    for f in range(FF//FC):
        c=slice(f*FC,(f+1)*FC)
        gu=(mm(gd,wd[c,:],NT)*dgel[:,c]).astype(BF)
        dupb_ref[:,c]+=colsum(gu.astype(F32))
        awd[c,:]+=mm(gel[:,c],gd,TN)
        awu[:,c]+=mm(hid,gu,TN)
        gn=gn+mm(gu,wu[:,c],NT)
    dvec_ref[pl.ds(ATT_G,1),:]+=colsum(gn*n1)
    dvec_ref[pl.ds(ATT_S,1),:]+=colsum(gn)
    ga=norm_back(gn*vec(ATT_G),n1,r1)
    gas_ref[...]=ga
    gb=ga.astype(BF)
    dvec_ref[pl.ds(OUT_B,1),:]+=colsum(gb.astype(F32))
    awo[...]+=mm(att,gb,TN)
    gatt=mm(gb,wo[...],NT).astype(BF)
    gatt_ref[...]=gatt
    pr=-(gatt.astype(F32)*att.astype(F32))
    hi,mid,lo=split3(pr)
    hrow=lax.broadcasted_iota(jnp.int32,(D,128),0)//64
    hcol=lax.broadcasted_iota(jnp.int32,(D,128),1)
    ind=((hcol>=3*hrow)&(hcol<3*hrow+3)).astype(BF)
    dl=mm(hi.astype(BF),ind,NN)+mm(mid.astype(BF),ind,NN)
    h2,m2,l2=split3(dl)
    ln=lanes(dl.shape)%3
    auxd_ref[...]=jnp.where(ln==0,h2,jnp.where(ln==1,m2,l2)).astype(BF)
    @pl.when(i==nb-1)
    def _():
        for t in range(nblk):
            dod,du=(dwod_m,dwu_m) if t<4 else (dwod_t,dwu_t)
            dod[t%4,:ro,:]=awo[rows_at(me,t,ro),:].astype(BF)
            dod[t%4,ro:,:]=awd[rows_at(me,t,rd),:].astype(BF)
            du[t%4]=awu[rows_at(me,t,ro),:].astype(BF)
def middle(me,info,mixed,cot,atts,vec,upb,wod_p,wu_p):
    nblk=8; L,D=mixed.shape; FF=upb.shape[1]; ro=D//8; rd=FF//8
    nb=L//RB; na=len(atts)
    def kern(me_ref,info_ref,mix_ref,cot_ref,*rest):
        att=rest[:na]; rest=rest[na:]
        mid_kernel(nblk,me_ref,info_ref,mix_ref,cot_ref,att,rest[0],rest[1],rest[2:10],rest[10:18],*rest[18:])
    full=lambda a: pl.BlockSpec(a.shape,lambda i:(0,)*a.ndim)
    blk=pl.BlockSpec((1,RB,D),lambda i:(i,0,0)); row=pl.BlockSpec((RB,D),lambda i:(i,0))
    outs=[sds((nb,RB,D),BF),sds((L,D),F32),sds((L,D),BF),sds((L,128),BF)]+[sds((4,ro+rd,D),BF)]*2+[sds((4,ro,FF),BF)]*2+[sds((16,D),F32),sds((1,FF),F32)]
    return pl.pallas_call(kern,grid=(nb,),
      in_specs=[smem(),smem(),row,blk]+[pl.BlockSpec((RB,a.shape[1]),lambda i:(i,0)) for a in atts]+[full(vec),full(upb)]+[anyw()]*16,
      out_specs=[blk,row,row,pl.BlockSpec((RB,128),lambda i:(i,0))]+[once(s) for s in outs[4:]],
      out_shape=outs,
      scratch_shapes=[pltpu.VMEM((D,D),BF),pltpu.VMEM((FF,D),BF),pltpu.VMEM((D,FF),BF),
        pltpu.VMEM((D,D),F32),pltpu.VMEM((FF,D),F32),pltpu.VMEM((D,FF),F32),
        pltpu.VMEM((RB,FF),BF),pltpu.VMEM((RB,FF),F32),pltpu.SemaphoreType.DMA((3,))],
      compiler_params=pltpu.CompilerParams(vmem_limit_bytes=61*2**20),
      cost_estimate=pl.CostEstimate(flops=2*L*D*(3*D+6*FF),bytes_accessed=60_000_000,transcendentals=2*L*FF),
      name="middle")(me,info,mixed,cot,*atts,vec,upb,*wod_p,*wu_p)

GROUPS=8
AXES=("seq","stream")
def flip(x,mask,total):
    return lax.ppermute(x,AXES,[(i,i^mask) for i in range(total)])
def by_index(pieces,index):
    x=jnp.stack(pieces); n=x.shape[0]; bit=1
    while bit<n:
        turned=jnp.concatenate([x[k^bit][None] for k in range(n)])
        x=jnp.where((index&bit)!=0,turned,x); bit*=2
    return x
def spread(own,unit,total,via):
    across=lambda x,g: flip(x,g*unit,total)
    bx=across(own,2); by=across(own,4)
    bd=across(by,2) if via==2 else across(bx,4)
    near=[own,bx,by,bd]
    return near+[across(x,1) for x in near]
def collect(mine,theirs,unit,total,via):
    across=lambda x,g: flip(x,g*unit,total)
    got=across(theirs,1)
    add=lambda *xs: sum(x.astype(F32) for x in xs)
    d=add(mine[3],got[3]).astype(BF)
    d=across(d,via)
    extra=(2,1) if via==2 else (1,2)
    x=[None,mine[1],mine[2]]
    fx=add(mine[1],got[1],*([d] if extra[0]==1 else [])).astype(BF)
    fy=add(mine[2],got[2],*([d] if extra[0]==2 else [])).astype(BF)
    return add(mine[0],got[0],across(fx,2),across(fy,4))
def finish(part,inner,count,total):
    low=part.astype(BF)
    out=lax.dynamic_index_in_dim(part,inner,0,keepdims=False)
    for k in range(1,count):
        out=out+flip(lax.dynamic_index_in_dim(low,inner^k,0,keepdims=False),k,total).astype(F32)
    return out

def on_device(tokens,source_len,target_len,timesteps,cotangent,query_weight,query_bias,key_weight,value_weight,value_bias,
        out_weight,out_bias,attn_gain,attn_shift,up_weight,up_bias,down_weight,down_bias,ffn_gain,ffn_shift,
        stamp_weight,stamp_bias,embed_weight,embed_bias):
    seqs,R,D=tokens.shape
    streams=lax.axis_size("stream"); seq_size=lax.axis_size("seq"); total=seq_size*streams
    s0=lax.axis_index("stream"); flat=lax.axis_index("seq")*streams+s0
    unit=total//GROUPS
    inner=flat%unit; group=flat//unit
    me=group.astype(jnp.int32).reshape(1)
    n=D//GROUPS; shard=D//total; stamp_rows=stamp_weight.shape[0]; FF=up_weight.shape[1]; ff_shard=FF//total
    vecs=(query_bias,value_bias,out_bias,attn_gain,attn_shift,down_bias,ffn_gain,ffn_shift,stamp_bias,embed_bias)
    nv=len(vecs)
    packed=jnp.concatenate(vecs+(up_bias,)); width=packed.shape[0]
    packed=jnp.pad(packed,(0,D-width))[None]
    small=jnp.concatenate([stamp_weight,packed,jnp.zeros((7-stamp_rows,D),F32)])
    first=jnp.concatenate([query_weight,key_weight,value_weight,embed_weight,small]).astype(BF)
    second=jnp.concatenate([out_weight,down_weight]).astype(BF)
    third=up_weight.astype(BF)
    def along(x): return by_index([x]+[flip(x,k,total) for k in range(1,unit)],inner)
    def rowwise(x,sizes):
        at=0; out=[]
        for count,size in sizes:
            part=x[:,at:at+count*size].reshape(unit,count,size,x.shape[2])
            out.append(part.transpose(1,0,2,3).reshape(count*unit*size,x.shape[2])); at+=count*size
        return jnp.concatenate(out) if len(out)>1 else out[0]
    first=rowwise(along(first),((4,shard),(1,8)))
    toks=[]
    for k in range(streams):
        part=lax.dynamic_index_in_dim(tokens,s0^k,0,keepdims=False)
        toks.append(part if k==0 else flip(part,k,total))
    second=rowwise(along(second),((1,shard),(1,ff_shard)))
    third=along(third).reshape(n,FF)
    p1=spread(first,unit,total,2)
    p2=spread(second,unit,total,4)
    p3=spread(third,unit,total,2)
    cots=[]
    for k in range(streams):
        part=lax.dynamic_index_in_dim(cotangent,s0^k,0,keepdims=False)
        cots.append(part if k==0 else flip(part,k,total))
    cot=jnp.stack(cots)
    order=jnp.asarray(ORDER,jnp.int32)
    smalls=jnp.stack([p[4*n:].reshape(unit,8,D)[:,stamp_rows,:width].reshape(unit*width) for p in p1])
    pick=(jnp.arange(GROUPS)[:,None]==(order^group)[None,:]).astype(BF)
    smalls=jnp.dot(pick,smalls,preferred_element_type=F32).astype(BF).reshape(total,width)
    vec=smalls[:,:nv*shard].reshape(total,nv,shard).transpose(1,0,2).reshape(nv,D)
    vec=jnp.pad(vec,((0,16-nv),(0,0))).astype(F32)
    upb=smalls[:,nv*shard:].reshape(1,FF).astype(F32)
    source=source_len[s0]; target=target_len[s0]; stamp=timesteps[s0]
    half=R*streams//2
    place=(s0^jnp.arange(streams))*R
    flag=(place>=half).astype(jnp.int32)
    nlive=jnp.clip(jnp.where(flag==1,target-(place-half),source-place),0,R).astype(jnp.int32)
    info=jnp.stack([flag,nlive],1)
    tdim=stamp_rows*total; halfway=tdim//2
    t_ids=(((order^group)[:,None,None]*unit+jnp.arange(unit)[None,:,None])*stamp_rows+jnp.arange(8)[None,None,:])
    valid=(jnp.arange(8)<stamp_rows)[None,None,:]
    t_ids=jnp.where(valid,t_ids,0).reshape(-1)
    rates=jnp.exp(-math.log(10000.0)*(t_ids%halfway).astype(F32)/halfway)
    angle=stamp.astype(F32)*rates
    feats=jnp.where(t_ids<halfway,jnp.sin(angle),jnp.cos(angle))
    feats=jnp.where(jnp.broadcast_to(valid,(GROUPS,unit,8)).reshape(-1),feats,0.0)
    feat=jnp.broadcast_to(feats.astype(BF)[None],(8,feats.shape[0]))
    mixed,inputs,q,k,v,auxk,pre,hid=project(me,info,feat,vec,toks,p1)
    parts=3; pairs=D//(2*HEAD); per=pairs//parts
    atts=[];auxq=[]
    for c in range(parts):
        a,x=attn_fwd(q,k,v,auxk,c*per,per); atts.append(a); auxq.append(x)
    output,ga,gatt,auxd,dwod_m,dwod_t,dwu_m,dwu_t,dvec,dupb=middle(me,info,mixed,cot,atts,vec,upb,p2,p3)
    g2=collect(dwod_m,dwod_t,unit,total,4)
    g3=collect(dwu_m,dwu_t,unit,total,2)
    dq=[];dk=[];dv=[]
    for c in range(parts):
        a,b,d=attn_bwd(q,k,v,gatt,auxk,auxq[c],auxd,c*per,per); dq.append(a);dk.append(b);dv.append(d)
    def back(chunks,dtype):
        out=jnp.zeros((seqs,R,D),dtype)
        for kk in range(streams):
            part=chunks[kk] if kk==0 else flip(chunks[kk],kk,total)
            out=lax.dynamic_update_index_in_dim(out,part.astype(dtype),s0^kk,0)
        return out
    output=back(output,BF)
    tg,ge=token_grads(me,info,ga,dq,dk,dv,p1,R)
    token_grad=back(tg,F32)
    m1,t1,dsmall,dvec2=weight_grads(me,inputs,ge,pre,hid,feat,dq,dk,dv,p1)
    g1=collect(m1,t1,unit,total,2)
    rows=jnp.concatenate([dvec2[0:2],dvec[2:8],dvec2[2:4]])
    packed=jnp.concatenate([rows.reshape(nv,total,shard).transpose(1,0,2).reshape(total,nv*shard),dupb.reshape(total,ff_shard)],1)
    packed=packed.reshape(GROUPS,unit*width)
    packed=jnp.dot(pick.astype(F32).T,packed,precision=lax.Precision.HIGHEST).reshape(GROUPS,unit,1,width)
    packed=jnp.pad(packed,((0,0),(0,0),(stamp_rows,7-stamp_rows),(0,D-width)))
    gs=(dsmall.reshape(GROUPS,unit,8,D)+packed).astype(BF)
    gs=finish(collect(gs[:4],gs[4:],unit,total,4),inner,unit,total)
    h1=finish(g1.reshape(4,unit,shard,D).transpose(1,0,2,3).reshape(unit,4*shard,D),inner,unit,total)
    g2=jnp.concatenate([g2[:n].reshape(unit,shard,D),g2[n:].reshape(unit,ff_shard,D)],1)
    h2=finish(g2,inner,unit,total)
    h3=finish(g3.reshape(unit,shard,FF),inner,unit,total)
    pv=gs[stamp_rows]
    gv=[pv[j*shard:(j+1)*shard] for j in range(nv)]
    cut=lambda j: h1[j*shard:(j+1)*shard]
    return (output,token_grad,cut(0),gv[0],cut(1),cut(2),gv[1],h2[:shard],gv[2],gv[3],gv[4],h3,pv[nv*shard:width],h2[shard:],gv[5],gv[6],gv[7],
        gs[:stamp_rows],gv[8],cut(3),gv[9])

def solution(mesh):
    cells=P("seq","stream",None); per=P("seq"); mat=P(("seq","stream"),None); row=P(("seq","stream"))
    return jax.shard_map(on_device,mesh=mesh,
        in_specs=(cells,per,per,per,cells,mat,row,mat,mat,row,mat,row,row,row,mat,row,mat,row,row,row,mat,row,mat,row),
        out_specs=(cells,cells,mat,row,mat,mat,row,mat,row,row,row,mat,row,mat,row,row,row,mat,row,mat,row),
        check_vma=False)
```

```python
import functools
import math

import jax
import jax.numpy as jnp
from jax import lax
from jax.experimental import pallas as pl
from jax.experimental.pallas import tpu as pltpu
from jax.sharding import PartitionSpec as P

F32=jnp.float32; BF=jnp.bfloat16
NT=(((1,),(1,)),((),())); NN=(((1,),(0,)),((),())); TN=(((0,),(0,)),((),()))
def mm(a,b,dims): return lax.dot_general(a,b,dims,preferred_element_type=F32)
def lanes(shape): return lax.broadcasted_iota(jnp.int32,shape,len(shape)-1)
def split3(x):
    hi=x.astype(BF).astype(F32); r=x-hi
    mid=r.astype(BF).astype(F32); lo=r-mid
    return hi,mid,lo
QB=256
def fwd_kernel(q_ref,k_ref,v_ref,auxk_ref,o_ref,auxq_ref,kaug,vm):
    i=pl.program_id(1)
    @pl.when(i==0)
    def _():
        k=k_ref[...]; v=v_ref[...]; ln=lanes(k.shape)
        z=jnp.zeros_like(k)
        for e in range(2):
            sel=(ln<64) if e==0 else (ln>=64)
            kaug[e,:,:128]=jnp.where(sel,k,z)
            kaug[e,:,128:]=auxk_ref[...]
            vm[e]=jnp.where(sel,v,z)
    q=q_ref[...]
    one=jnp.where(lanes(q.shape)==64,1.0,0.0).astype(BF)
    qa=jnp.concatenate([q,one],axis=1)
    out=None; ln=lanes((QB,128)); aux=jnp.where(ln==64,1.0,0.0)
    for e in range(2):
        s=mm(qa,kaug[e],NT)
        m=jnp.max(s,axis=1,keepdims=True)
        p=jnp.exp(s-m)
        l=jnp.sum(p,axis=1,keepdims=True)
        o=mm(p.astype(BF),vm[e],NN)*(1.0/l)
        out=o if out is None else out+o
        hi,mid,lo=split3(-(m+jnp.log(l)))
        aux=jnp.where(ln==3*e,hi,aux); aux=jnp.where(ln==3*e+1,mid,aux); aux=jnp.where(ln==3*e+2,lo,aux)
    o_ref[...]=out.astype(BF)
    auxq_ref[...]=aux.astype(BF)[None]
def attn_fwd(q,k,v,auxk,p0,np_):
    L=q.shape[0]
    return pl.pallas_call(fwd_kernel,grid=(np_,L//QB),
      in_specs=[pl.BlockSpec((QB,128),lambda p,i:(i,p0+p)),pl.BlockSpec((L,128),lambda p,i:(0,p0+p)),
        pl.BlockSpec((L,128),lambda p,i:(0,p0+p)),pl.BlockSpec((L,128),lambda p,i:(0,0))],
      out_specs=[pl.BlockSpec((QB,128),lambda p,i:(i,p)),pl.BlockSpec((1,QB,128),lambda p,i:(p,i,0))],
      out_shape=[jax.ShapeDtypeStruct((L,128*np_),BF),jax.ShapeDtypeStruct((np_,L,128),BF)],
      scratch_shapes=[pltpu.VMEM((2,L,256),BF),pltpu.VMEM((2,L,128),BF)],
      compiler_params=pltpu.CompilerParams(vmem_limit_bytes=60*2**20),
      cost_estimate=pl.CostEstimate(flops=np_*2*L*L*64*4,bytes_accessed=np_*L*128*2*5,transcendentals=np_*2*L*L),
      name="attn_fwd")(q,k,v,auxk)
def bwd_kernel(p0,q_ref,k_ref,v_ref,do_ref,auxk_ref,auxq_ref,auxd_ref,dq_ref,dk_ref,dv_ref,kaug,vaug,qa,doa,qm,dom,dk_acc,dv_acc):
    pair=p0+pl.program_id(0)
    L=q_ref.shape[0]
    k=k_ref[...]; v=v_ref[...]; q=q_ref[...]; do=do_ref[...]
    ln=lanes(k.shape); z=jnp.zeros_like(k); auxk=auxk_ref[...]
    qa[:,:128]=q; qa[:,128:]=auxq_ref[0]
    doa[:,:128]=do; doa[:,128:]=auxd_ref[...]
    for e in range(2):
        sel=(ln<64) if e==0 else (ln>=64)
        on=(ln>=3*e)&(ln<3*e+3)
        kaug[e,:,:128]=jnp.where(sel,k,z)
        kaug[e,:,128:]=jnp.where(on,jnp.ones_like(k),auxk)
        vaug[e,:,:128]=jnp.where(sel,v,z)
        b=6*pair+3*e
        vaug[e,:,128:]=jnp.where((ln>=b)&(ln<b+3),jnp.ones_like(k),z)
        qm[e]=jnp.where(sel,q,z)
        dom[e]=jnp.where(sel,do,z)
    for i in range(L//QB):
        r=pl.ds(i*QB,QB)
        dq=None
        for e in range(2):
            p=jnp.exp(mm(kaug[e],qa[r,:],NT))
            dp=mm(vaug[e],doa[r,:],NT)
            ds=(p*dp).astype(BF)
            dv=mm(p.astype(BF),dom[e,r,:],NN)
            dk=mm(ds,qm[e,r,:],NN)
            if i==0 and e==0: dv_acc[...]=dv; dk_acc[...]=dk
            else: dv_acc[...]+=dv; dk_acc[...]+=dk
            d=mm(ds,kaug[e,:,:128],TN)
            dq=d if dq is None else dq+d
        dq_ref[r,:]=(dq*0.125).astype(BF)
    dk_ref[...]=dk_acc[...].astype(BF)
    dv_ref[...]=dv_acc[...].astype(BF)
def attn_bwd(q,k,v,do,auxk,auxq,auxd,p0,np_):
    L=q.shape[0]
    col=lambda: pl.BlockSpec((L,128),lambda p:(0,p0+p))
    con=lambda: pl.BlockSpec((L,128),lambda p:(0,0))
    oc=lambda: pl.BlockSpec((L,128),lambda p:(0,p))
    return pl.pallas_call(functools.partial(bwd_kernel,p0),grid=(np_,),
      in_specs=[col(),col(),col(),col(),con(),pl.BlockSpec((1,L,128),lambda p:(p,0,0)),con()],
      out_specs=[oc(),oc(),oc()],
      out_shape=[jax.ShapeDtypeStruct((L,128*np_),BF)]*3,
      scratch_shapes=[pltpu.VMEM((2,L,256),BF),pltpu.VMEM((2,L,256),BF),pltpu.VMEM((L,256),BF),pltpu.VMEM((L,256),BF),
        pltpu.VMEM((2,L,128),BF),pltpu.VMEM((2,L,128),BF),pltpu.VMEM((L,128),F32),pltpu.VMEM((L,128),F32)],
      compiler_params=pltpu.CompilerParams(vmem_limit_bytes=60*2**20),
      cost_estimate=pl.CostEstimate(flops=np_*2*L*L*64*10,bytes_accessed=np_*L*128*2*9,transcendentals=np_*2*L*L),
      name="attn_bwd")(q,k,v,do,auxk,auxq,auxd)

SMALL=16; Q_B,V_B,OUT_B,ATT_G,ATT_S,DOWN_B,FFN_G,FFN_S,STAMP_B,EMBED_B=range(4,14); UP_B=14
def owner_of(rows,me,unit,width):
    r=lax.shift_right_logical(lax.broadcasted_iota(jnp.int32,(rows,width),0),SMALL.bit_length()-1)
    shift=unit.bit_length()-1
    t=lax.shift_right_logical(r,shift)
    g=jnp.bitwise_xor(jnp.bitwise_or(jnp.bitwise_and(t*2,7),lax.shift_right_logical(t,2)),me)
    return g*unit+jnp.bitwise_and(r,unit-1)
def repeats(width,shard):
    l=lax.broadcasted_iota(jnp.int32,(128,width),0).astype(F32); d=lax.broadcasted_iota(jnp.int32,(128,width),1).astype(F32)
    return (d-shard*jnp.floor((d+0.5)*(1.0/shard))==l).astype(BF)
def owned(owner,shard):
    d=lax.broadcasted_iota(jnp.int32,owner.shape,1)
    return (d>=owner*shard)&(d<owner*shard+shard)
def pack_kernel(*refs):
    *ins,first_ref,second_ref,scr=refs
    wq,wk,wv,we,st,wo,wd,wu=ins[:8]; vecs=ins[8:]
    scr[...]=jnp.zeros_like(scr)
    scr[:st.shape[0],:]=st[...]
    for r,v in enumerate(vecs):
        scr[4+r:5+r,:v.shape[0]]=v[...].reshape(1,-1)
    D=wq.shape[1]
    first_ref[...]=jnp.concatenate([wq[...],wk[...],wv[...],we[...],scr[...]],axis=0).astype(BF)
    up=[wu[:,c*D:(c+1)*D] for c in range(wu.shape[1]//D)]
    second_ref[...]=jnp.concatenate([wo[...],wd[...]]+up,axis=0).astype(BF)
def pack(mats,vecs):
    wq,wk,wv,we,st,wo,wd,wu=mats; n,D=wq.shape
    vm=pl.BlockSpec(memory_space=pltpu.VMEM)
    second=n+wd.shape[0]+n*(wu.shape[1]//D)
    if n%8:
        small=jnp.concatenate([st]+[jnp.zeros((4-st.shape[0],D),F32)]+[jnp.pad(v,(0,D-v.shape[0]))[None] for v in vecs]+[jnp.zeros((SMALL-4-len(vecs),D),F32)])
        up=[wu[:,c*D:(c+1)*D] for c in range(wu.shape[1]//D)]
        return jnp.concatenate([wq,wk,wv,we,small]).astype(BF),jnp.concatenate([wo,wd]+up).astype(BF)
    return pl.pallas_call(pack_kernel,in_specs=[vm]*(8+len(vecs)),out_specs=[vm]*2,
      out_shape=[sds((4*n+SMALL,D),BF),sds((second,D),BF)],scratch_shapes=[pltpu.VMEM((SMALL,D),F32)],name="pack")(*mats,*vecs)
ORDER=(0,2,4,6,1,3,5,7)
def rows_at(me,t,n):
    return pl.ds(pl.multiple_of(jnp.bitwise_xor(me,ORDER[t])*n,n),n)
def sds(*a): return jax.ShapeDtypeStruct(*a)
def once(s): return pl.BlockSpec(s.shape,lambda i:(0,)*len(s.shape),pipeline_mode=pl.Buffered(1))
def smem(): return pl.BlockSpec(memory_space=pltpu.SMEM)
def anyw(): return pl.BlockSpec(memory_space=pl.ANY)
def load_weights(me,pieces,base,n,dst,sem):
    return [pltpu.make_async_copy(p.at[pl.ds(base,n),:],dst.at[rows_at(me,t,n),:],sem) for t,p in enumerate(pieces)]
def in_kernel(nt,unit,me_ref,info_ref,feat_ref,*rest):
    toks=rest[:nt]; pieces=rest[nt:nt+8]
    mixed_ref,inp_ref,q_ref,k_ref,v_ref,auxk_ref,pre_ref,hid_ref,vec_ref,upb_ref,tok,wq,wk,wv,we,ws,emb,sems=rest[nt+8:]
    i=pl.program_id(0); me=me_ref[0]
    D=wq.shape[0]; n=D//8; ns=ws.shape[0]//8
    tcp=[pltpu.make_async_copy(t,tok.at[c],sems.at[5+c]) for c,t in enumerate(toks)]
    scp=[pltpu.make_async_copy(p.at[pl.ds(4*n,ns),:],ws.at[pl.ds(t*ns,ns),:],sems.at[0]) for t,p in enumerate(pieces)]
    wcp=[load_weights(me,pieces,w*n,n,dst,sems.at[1+w]) for w,dst in enumerate((wq,wk,wv,we))]
    vec=lambda r: vec_ref[pl.ds(r,1),:]
    @pl.when(i==0)
    def _():
        for c in scp+wcp[3]+tcp[:1]+wcp[0]+wcp[1]+wcp[2]+tcp[1:]: c.start()
        for c in scp: c.wait()
        rows=8*ns; total=8*unit; FF=upb_ref.shape[1]
        lead=ws[:,:128]
        spread=mm(lead,repeats(D,D//total),NN)
        spread=jnp.where(owned(owner_of(rows,me,unit,D),D//total),spread,0.0)
        vec_ref[...]=jnp.sum(spread.reshape(total,SMALL,D),axis=0)
        ups=lead.astype(F32).reshape(total,SMALL,128)[:,UP_B,:].astype(BF)
        ups=mm(ups,repeats(FF,FF//total),NN)
        own=owner_of(rows,me,unit,128).reshape(total,SMALL,128)[:,0,:1]
        upb_ref[...]=jnp.sum(jnp.where(owned(jnp.broadcast_to(own,(total,FF)),FF//total),ups,0.0),axis=0,keepdims=True)
        pre=mm(feat_ref[...],ws[...],NN)+vec(STAMP_B)
        pre_ref[...]=pre
        hid=(pre/(1.0+jnp.exp(-pre))).astype(BF)
        hid_ref[...]=hid
        for c in wcp[3]: c.wait()
        emb[...]=mm(hid,we[...],NN)+vec(EMBED_B)
    for c in range(nt):
        @pl.when(i==c)
        def _(): tcp[c].wait()
    flag=info_ref[i,0].astype(F32); nlive=info_ref[i,1]
    x=tok[i].astype(F32)+flag*emb[pl.ds(0,1),:]
    mixed_ref[...]=x
    xb=x.astype(BF); inp_ref[...]=xb
    R=x.shape[0]
    ln=lanes((R,128)); row=lax.broadcasted_iota(jnp.int32,(R,128),0)
    auxk_ref[...]=jnp.where((ln==64)&(row>=nlive),-1e30,0.0).astype(BF)
    @pl.when(i==0)
    def _():
        for w in range(3):
            for c in wcp[w]: c.wait()
    q=(mm(xb,wq[...],NN)+vec(Q_B)).astype(BF)
    q_ref[...]=(q.astype(F32)*0.125).astype(BF)
    k_ref[...]=mm(xb,wk[...],NN).astype(BF)
    v_ref[...]=(mm(xb,wv[...],NN)+vec(V_B)).astype(BF)
def project(me,info,feat,toks,pieces,unit,FF):
    nt=len(toks); R,D=toks[0].shape; n=D//8; ns=pieces[0].shape[0]-4*n; L=nt*R
    row=lambda w: pl.BlockSpec((R,w),lambda i:(i,0))
    full=lambda a: pl.BlockSpec(a.shape,lambda i:(0,)*a.ndim)
    outs=[sds((L,D),F32)]+[sds((L,D),BF)]*4+[sds((L,128),BF),sds((8,D),F32),sds((8,D),BF),sds((SMALL,D),F32),sds((1,FF),F32)]
    return pl.pallas_call(functools.partial(in_kernel,nt,unit),grid=(nt,),
      in_specs=[smem(),smem(),full(feat)]+[anyw()]*(nt+8),
      out_specs=[row(D)]*5+[row(128)]+[once(o) for o in outs[6:]],
      out_shape=outs,
      scratch_shapes=[pltpu.VMEM((nt,R,D),BF)]+[pltpu.VMEM((D,D),BF)]*4+[pltpu.VMEM((8*ns,D),BF),pltpu.VMEM((8,D),F32),pltpu.SemaphoreType.DMA((5+nt,))],
      compiler_params=pltpu.CompilerParams(vmem_limit_bytes=60*2**20),
      cost_estimate=pl.CostEstimate(flops=2*L*D*D*3,bytes_accessed=20_000_000,transcendentals=0),
      name="project")(me,info,feat,*toks,*pieces)

def spread3(row):
    hi,mid,lo=split3(row)
    r=lax.broadcasted_iota(jnp.int32,(8,row.shape[1]),0)
    return jnp.where(r==0,hi,jnp.where(r==1,mid,jnp.where(r==2,lo,0.0))).astype(BF)
def three(rows):
    r=lax.broadcasted_iota(jnp.int32,rows.shape,0)
    return jnp.where(r<3,jnp.broadcast_to(rows[0:1,:].astype(F32),rows.shape),0.0).astype(BF)
def token_kernel(nc,unit,me_ref,info_ref,ga_ref,pre_ref,hid_ref,feat_ref,dvec_ref,dupb_ref,*rest):
    dq=rest[:nc]; dk=rest[nc:2*nc]; dv=rest[2*nc:3*nc]; pieces=rest[3*nc:3*nc+8]
    tg_ref,mine_ref,theirs_ref,wq,wk,wv,we,rows_ref,acc,sems=rest[3*nc+8:]
    i=pl.program_id(0); me=me_ref[0]
    D=wq.shape[0]; n=D//8; rows=feat_ref.shape[1]; ns=rows//8
    wcp=[load_weights(me,pieces,w*n,n,dst,sems.at[w]) for w,dst in enumerate((wq,wk,wv,we))]
    @pl.when(i==0)
    def _():
        for w in wcp:
            for c in w: c.start()
        rows_ref[...]=jnp.zeros_like(rows_ref)
    g=ga_ref[...]
    for w,(src,dst) in enumerate(((dq,wq),(dk,wk),(dv,wv))):
        y=jnp.concatenate([s[...] for s in src],axis=1)
        if w!=1: rows_ref[pl.ds(w//2,1),:]+=jnp.sum(y.astype(F32),axis=0,keepdims=True)
        @pl.when(i==0)
        def _():
            for c in wcp[w]: c.wait()
        g=g+mm(y,dst[...],NT)
    tg_ref[0]=g.astype(BF)
    rows_ref[pl.ds(3,1),:]+=info_ref[i,0].astype(F32)*jnp.sum(g,axis=0,keepdims=True)
    @pl.when(i==pl.num_programs(0)-1)
    def _():
        for c in wcp[3]: c.wait()
        ge=rows_ref[pl.ds(3,1),:]
        gh=jnp.sum(mm(spread3(ge),we[...],NT),axis=0,keepdims=True)
        pre=pre_ref[0:1,:]
        sg=1.0/(1.0+jnp.exp(-pre))
        gs=gh*(sg*(1.0+pre*(1.0-sg)))
        rows_ref[pl.ds(2,1),:]=gs
        acc[...]=mm(three(hid_ref[...]),spread3(ge),TN)
        total=8*unit; FF=dupb_ref.shape[1]
        r=lax.broadcasted_iota(jnp.int32,(SMALL,D),0)
        vec=dvec_ref[...]
        for at,row in ((Q_B,0),(V_B,1),(STAMP_B,2),(EMBED_B,3)):
            vec=jnp.where(r==at,rows_ref[pl.ds(row,1),:],vec)
        vec=jnp.broadcast_to(vec[None],(total,SMALL,D)).reshape(rows,D)
        vec=jnp.where(owned(owner_of(rows,me,unit,D),D//total),vec,0.0).astype(BF)
        vec=mm(vec,repeats(D,D//total),NT)
        own=owner_of(rows,me,unit,128).reshape(total,SMALL,128)[:,0,:1]
        ups=jnp.where(owned(jnp.broadcast_to(own,(total,FF)),FF//total),dupb_ref[...],0.0).astype(BF)
        ups=mm(ups,repeats(FF,FF//total),NT)
        line=jnp.bitwise_and(lax.broadcasted_iota(jnp.int32,(rows,128),0),SMALL-1)
        ups=jnp.broadcast_to(ups[:,None,:],(total,SMALL,128)).reshape(rows,128)
        vec=jnp.where(line==UP_B,ups,jnp.where((line>=4)&(line<UP_B),vec,0.0))
        small=mm(three(feat_ref[...]),spread3(gs),TN)
        small=small+jnp.concatenate([vec,jnp.zeros((rows,D-128),F32)],axis=1)
        small=small.astype(BF)
        for t in range(8):
            dst=mine_ref if t<4 else theirs_ref
            dst[t%4,:n,:]=acc[rows_at(me,t,n),:].astype(BF)
            dst[t%4,n:,:]=small[t*ns:(t+1)*ns]
def token_grads(me,info,ga,pre,hid,feat,dvec,dupb,dq,dk,dv,pieces,unit,R):
    L,D=ga.shape; nt=L//R; nc=len(dq); W=dq[0].shape[1]; n=D//8
    outs=[sds((nt,R,D),BF)]+[sds((4,n+feat.shape[1]//8,D),BF)]*2
    full=lambda a: pl.BlockSpec(a.shape,lambda i:(0,)*a.ndim)
    return pl.pallas_call(functools.partial(token_kernel,nc,unit),grid=(nt,),
      in_specs=[smem(),smem(),pl.BlockSpec((R,D),lambda i:(i,0))]+[full(a) for a in (pre,hid,feat,dvec,dupb)]+[pl.BlockSpec((R,W),lambda i:(i,0))]*(3*nc)+[anyw()]*8,
      out_specs=[pl.BlockSpec((1,R,D),lambda i:(i,0,0))]+[once(o) for o in outs[1:]],
      out_shape=outs,
      scratch_shapes=[pltpu.VMEM((D,D),BF)]*4+[pltpu.VMEM((8,D),F32),pltpu.VMEM((D,D),F32),pltpu.SemaphoreType.DMA((4,))],
      compiler_params=pltpu.CompilerParams(vmem_limit_bytes=60*2**20),
      cost_estimate=pl.CostEstimate(flops=2*L*D*D*3,bytes_accessed=15_000_000,transcendentals=0),
      name="token_grads")(me,info,ga,pre,hid,feat,dvec,dupb,*dq,*dk,*dv,*pieces)
def weight_kernel(nc,me_ref,inp_ref,*rest):
    dq=rest[:nc]; dk=rest[nc:2*nc]; dv=rest[2*nc:3*nc]
    mine_ref,theirs_ref,acc=rest[3*nc:]
    i=pl.program_id(0); me=me_ref[0]; D=inp_ref.shape[1]; n=D//8
    grads=mm(inp_ref[...],jnp.concatenate([s[...] for s in dq+dk+dv],axis=1),TN)
    @pl.when(i==0)
    def _(): acc[...]=grads
    @pl.when(i>0)
    def _(): acc[...]+=grads
    @pl.when(i==pl.num_programs(0)-1)
    def _():
        for t in range(8):
            dst=mine_ref if t<4 else theirs_ref
            for w in range(3):
                dst[t%4,w*n:(w+1)*n,:]=acc[rows_at(me,t,n),w*D:(w+1)*D].astype(BF)
def weight_grads(me,inp,dq,dk,dv,R):
    L,D=inp.shape; n=D//8; nc=len(dq); W=dq[0].shape[1]
    outs=[sds((4,3*n,D),BF)]*2
    return pl.pallas_call(functools.partial(weight_kernel,nc),grid=(L//R,),
      in_specs=[smem(),pl.BlockSpec((R,D),lambda i:(i,0))]+[pl.BlockSpec((R,W),lambda i:(i,0))]*(3*nc),
      out_specs=[once(o) for o in outs],out_shape=outs,
      scratch_shapes=[pltpu.VMEM((D,3*D),F32)],
      compiler_params=pltpu.CompilerParams(vmem_limit_bytes=60*2**20),
      cost_estimate=pl.CostEstimate(flops=2*L*D*D*3,bytes_accessed=12_000_000,transcendentals=0),
      name="weight_grads")(me,inp,*dq,*dk,*dv)
def last1_kernel(keep_ref,got_ref,*outs):
    x=keep_ref[...]+got_ref[...].astype(F32)
    *mats,st=outs[:5]; n=mats[0].shape[0]
    for w,o in enumerate(mats): o[...]=x[w*n:(w+1)*n]
    st[...]=x[4*n:4*n+st.shape[0]]
    for r,o in enumerate(outs[5:]):
        o[...]=x[4*n+4+r:4*n+5+r,:o.shape[0]].reshape(o.shape)
def last1(keep,got,n,stamp_rows,sizes):
    D=keep.shape[1]
    vm=pl.BlockSpec(memory_space=pltpu.VMEM)
    outs=[sds((n,D),F32)]*4+[sds((stamp_rows,D),F32)]+[sds((k,),F32) for k in sizes]
    if n%8:
        x=keep+got.astype(F32)
        return [x[w*n:(w+1)*n] for w in range(4)]+[x[4*n:4*n+stamp_rows]]+[x[4*n+4+r,:k] for r,k in enumerate(sizes)]
    return pl.pallas_call(last1_kernel,in_specs=[vm]*2,out_specs=[vm]*len(outs),out_shape=outs,name="last_attn")(keep,got)
def last2_kernel(keep_ref,got_ref,wo,wd,wu):
    x=keep_ref[...]+got_ref[...].astype(F32); n,D=wo.shape; m=wd.shape[0]
    wo[...]=x[:n]; wd[...]=x[n:n+m]
    for c in range(wu.shape[1]//D): wu[:,c*D:(c+1)*D]=x[n+m+c*n:n+m+(c+1)*n]
def last2(keep,got,n,m,FF):
    D=keep.shape[1]
    vm=pl.BlockSpec(memory_space=pltpu.VMEM)
    outs=[sds((n,D),F32),sds((m,D),F32),sds((n,FF),F32)]
    if n%8:
        x=keep+got.astype(F32)
        return x[:n],x[n:n+m],jnp.concatenate([x[n+m+c*n:n+m+(c+1)*n] for c in range(FF//D)],1)
    return pl.pallas_call(last2_kernel,in_specs=[vm]*2,out_specs=[vm]*3,out_shape=outs,name="last_ffn")(keep,got)

INV_SQRT2=0.7071067811865476; INV_SQRT2PI=0.3989422804014327
HEAD=64
RB=256; FC=512
def norm_stats(x):
    mu=jnp.mean(x,axis=1,keepdims=True); c=x-mu
    r=lax.rsqrt(jnp.mean(c*c,axis=1,keepdims=True)+1e-5)
    return c*r,r
def norm_back(e,n,r):
    return r*(e-jnp.mean(e,axis=1,keepdims=True)-n*jnp.mean(e*n,axis=1,keepdims=True))
def colsum(x): return jnp.sum(x,axis=0,keepdims=True)
def mid_kernel(nblk,me_ref,info_ref,mix_ref,cot_ref,att_refs,vec_ref,upb_ref,pieces,
        out_ref,gas_ref,gatt_ref,auxd_ref,mine_ref,theirs_ref,dvec_ref,dupb_ref,
        wo,wd,wu,awo,awd,awu,gel,dgel,sems):
    i=pl.program_id(0); nb=pl.num_programs(0)
    D=wo.shape[0]; FF=wd.shape[0]; ro=D//nblk; rd=FF//nblk
    me=me_ref[0]
    cps=[load_weights(me,pieces,0,ro,wo,sems.at[0]),
        sum((load_weights(me,pieces,ro+rd+b*ro,ro,wu.at[:,pl.ds(b*D,D)],sems.at[1]) for b in range(FF//D)),[]),
        load_weights(me,pieces,ro,rd,wd,sems.at[2])]
    def wait(which):
        @pl.when(i==0)
        def _():
            for c in cps[which]: c.wait()
    @pl.when(i==0)
    def _():
        for w in cps:
            for c in w: c.start()
        awo[...]=jnp.zeros_like(awo); awd[...]=jnp.zeros_like(awd); awu[...]=jnp.zeros_like(awu)
        dvec_ref[...]=jnp.zeros_like(dvec_ref); dupb_ref[...]=jnp.zeros_like(dupb_ref)
    vec=lambda r: vec_ref[pl.ds(r,1),:].astype(F32)
    nlive=info_ref[i,1]
    x0=mix_ref[...]
    live=(lax.broadcasted_iota(jnp.int32,(RB,1),0)<nlive).astype(F32)
    wait(0)
    att=jnp.concatenate([a[...] for a in att_refs],axis=1)
    asum=x0+(mm(att,wo[...],NN)+vec(OUT_B))
    n1,r1=norm_stats(asum)
    normed=n1*vec(ATT_G)+vec(ATT_S)
    hid=normed.astype(BF)
    wait(1); wait(2)
    down=None
    for f in range(FF//FC):
        c=slice(f*FC,(f+1)*FC)
        u=mm(hid,wu[:,c],NN)+upb_ref[:,c].astype(F32)
        ph=0.5+0.5*lax.erf(u*INV_SQRT2)
        pd=jnp.exp(u*u*-0.5)*INV_SQRT2PI
        g=(u*ph).astype(BF)
        gel[:,c]=g
        dgel[:,c]=ph+u*pd
        t=mm(g,wd[c,:],NN)
        down=t if down is None else down+t
    fsum=normed+(down+vec(DOWN_B))
    n2,r2=norm_stats(fsum)
    g2=vec(FFN_G)
    out_ref[0]=((n2*g2+vec(FFN_S))*live).astype(BF)
    og=cot_ref[0].astype(F32)*live
    dvec_ref[pl.ds(FFN_G,1),:]+=colsum(og*n2)
    dvec_ref[pl.ds(FFN_S,1),:]+=colsum(og)
    gf=norm_back(og*g2,n2,r2)
    gd=gf.astype(BF)
    dvec_ref[pl.ds(DOWN_B,1),:]+=colsum(gd.astype(F32))
    gn=gf
    for f in range(FF//FC):
        c=slice(f*FC,(f+1)*FC)
        gu=(mm(gd,wd[c,:],NT)*dgel[:,c]).astype(BF)
        dupb_ref[:,c]+=colsum(gu.astype(F32))
        awd[c,:]+=mm(gel[:,c],gd,TN)
        awu[:,c]+=mm(hid,gu,TN)
        gn=gn+mm(gu,wu[:,c],NT)
    dvec_ref[pl.ds(ATT_G,1),:]+=colsum(gn*n1)
    dvec_ref[pl.ds(ATT_S,1),:]+=colsum(gn)
    ga=norm_back(gn*vec(ATT_G),n1,r1)
    gas_ref[...]=ga
    gb=ga.astype(BF)
    dvec_ref[pl.ds(OUT_B,1),:]+=colsum(gb.astype(F32))
    awo[...]+=mm(att,gb,TN)
    gatt=mm(gb,wo[...],NT).astype(BF)
    gatt_ref[...]=gatt
    pr=-(gatt.astype(F32)*att.astype(F32))
    hi,mid,lo=split3(pr)
    hrow=lax.broadcasted_iota(jnp.int32,(D,128),0)//64
    hcol=lax.broadcasted_iota(jnp.int32,(D,128),1)
    ind=((hcol>=3*hrow)&(hcol<3*hrow+3)).astype(BF)
    dl=mm(hi.astype(BF),ind,NN)+mm(mid.astype(BF),ind,NN)
    h2,m2,l2=split3(dl)
    ln=lanes(dl.shape)%3
    auxd_ref[...]=jnp.where(ln==0,h2,jnp.where(ln==1,m2,l2)).astype(BF)
    @pl.when(i==nb-1)
    def _():
        for t in range(nblk):
            dst=mine_ref if t<4 else theirs_ref
            dst[t%4,:ro,:]=awo[rows_at(me,t,ro),:].astype(BF)
            dst[t%4,ro:ro+rd,:]=awd[rows_at(me,t,rd),:].astype(BF)
            for b in range(FF//D):
                dst[t%4,ro+rd+b*ro:ro+rd+(b+1)*ro,:]=awu[rows_at(me,t,ro),b*D:(b+1)*D].astype(BF)
def middle(me,info,mixed,cot,atts,vec,upb,pieces):
    nblk=8; L,D=mixed.shape; FF=upb.shape[1]; ro=D//8; rd=FF//8
    nb=L//RB; na=len(atts)
    def kern(me_ref,info_ref,mix_ref,cot_ref,*rest):
        att=rest[:na]; rest=rest[na:]
        mid_kernel(nblk,me_ref,info_ref,mix_ref,cot_ref,att,rest[0],rest[1],rest[2:10],*rest[10:])
    full=lambda a: pl.BlockSpec(a.shape,lambda i:(0,)*a.ndim)
    blk=pl.BlockSpec((1,RB,D),lambda i:(i,0,0)); row=pl.BlockSpec((RB,D),lambda i:(i,0))
    outs=[sds((nb,RB,D),BF),sds((L,D),F32),sds((L,D),BF),sds((L,128),BF)]+[sds((4,)+pieces[0].shape,BF)]*2+[sds((16,D),F32),sds((1,FF),F32)]
    return pl.pallas_call(kern,grid=(nb,),
      in_specs=[smem(),smem(),row,blk]+[pl.BlockSpec((RB,a.shape[1]),lambda i:(i,0)) for a in atts]+[full(vec),full(upb)]+[anyw()]*8,
      out_specs=[blk,row,row,pl.BlockSpec((RB,128),lambda i:(i,0))]+[once(s) for s in outs[4:]],
      out_shape=outs,
      scratch_shapes=[pltpu.VMEM((D,D),BF),pltpu.VMEM((FF,D),BF),pltpu.VMEM((D,FF),BF),
        pltpu.VMEM((D,D),F32),pltpu.VMEM((FF,D),F32),pltpu.VMEM((D,FF),F32),
        pltpu.VMEM((RB,FF),BF),pltpu.VMEM((RB,FF),F32),pltpu.SemaphoreType.DMA((3,))],
      compiler_params=pltpu.CompilerParams(vmem_limit_bytes=61*2**20),
      cost_estimate=pl.CostEstimate(flops=2*L*D*(3*D+6*FF),bytes_accessed=60_000_000,transcendentals=2*L*FF),
      name="middle")(me,info,mixed,cot,*atts,vec,upb,*pieces)

GROUPS=8
AXES=("seq","stream")
def flip(x,mask,total):
    return lax.ppermute(x,AXES,[(i,i^mask) for i in range(total)])
def far_first(count):
    bits=[]; bit=count//2
    while bit: bits.append(bit); bit//=2
    return bits
def widen(x,bit,total): return jnp.concatenate([x,flip(x,bit,total)])
def settle(x,inner,count):
    ids=[0]
    for bit in far_first(count): ids=ids+[i^bit for i in ids]
    return in_order(jnp.stack([x[ids.index(k)] for k in range(count)]),inner)
def in_order(x,index):
    n=x.shape[0]; bit=1
    while bit<n:
        turned=jnp.concatenate([x[k^bit][None] for k in range(n)])
        x=jnp.where((index&bit)!=0,turned,x); bit*=2
    return x
def after(x,*deps):
    return lax.optimization_barrier((x,)+deps)[0]
def spread_start(own,unit,total):
    across=lambda x,g: flip(x,g*unit,total)
    return [own,across(own,2),across(own,4)]
def spread_diag(near,unit,total):
    across=lambda x,g: flip(x,g*unit,total)
    own,bx,by=near; cut=own.shape[0]//2
    return across(by[:cut],2),across(bx[cut:],4),[across(x,1) for x in near]
def spread_end(near,low,high,far,unit,total):
    bd=jnp.concatenate([low,high])
    return near+[bd]+far+[flip(bd,unit,total)]
def add(*xs): return sum(x.astype(F32) for x in xs)
def collect_diag(mine,got,unit,total):
    cut=mine.shape[1]//2
    low=flip(add(mine[3,:cut],got[3,:cut]).astype(BF),2*unit,total)
    high=flip(add(mine[3,cut:],got[3,cut:]).astype(BF),4*unit,total)
    return low,high
def collect_near(mine,got,low,high,unit,total):
    cut=mine.shape[1]//2
    fx=jnp.concatenate([add(mine[1,:cut],got[1,:cut]),add(mine[1,cut:],got[1,cut:],high)]).astype(BF)
    fy=jnp.concatenate([add(mine[2,:cut],got[2,:cut],low),add(mine[2,cut:],got[2,cut:])]).astype(BF)
    return flip(fx,2*unit,total),flip(fy,4*unit,total)
def split_send(x,bit,total):
    send=jnp.stack([x[j] for j in range(1,x.shape[0],2)]).astype(BF)
    return jnp.stack([x[j] for j in range(0,x.shape[0],2)]),flip(send,bit,total)
def finish2(keep,got,total):
    bit=2
    while keep.shape[0]>1:
        keep,got=split_send(keep+got.astype(F32),bit,total); bit*=2
    return keep[0],got[0]
def finish(x,total): return finish2(*split_send(x,1,total),total)

def on_device(tokens,source_len,target_len,timesteps,cotangent,query_weight,query_bias,key_weight,value_weight,value_bias,
        out_weight,out_bias,attn_gain,attn_shift,up_weight,up_bias,down_weight,down_bias,ffn_gain,ffn_shift,
        stamp_weight,stamp_bias,embed_weight,embed_bias):
    seqs,R,D=tokens.shape
    streams=lax.axis_size("stream"); seq_size=lax.axis_size("seq"); total=seq_size*streams
    s0=lax.axis_index("stream"); flat=lax.axis_index("seq")*streams+s0
    unit=total//GROUPS
    inner=flat%unit; group=flat//unit
    me=group.astype(jnp.int32).reshape(1)
    n=D//GROUPS; shard=D//total; stamp_rows=stamp_weight.shape[0]; FF=up_weight.shape[1]; ff_shard=FF//total
    vecs=(query_bias,value_bias,out_bias,attn_gain,attn_shift,down_bias,ffn_gain,ffn_shift,stamp_bias,embed_bias,up_bias)
    first,second=pack((query_weight,key_weight,value_weight,embed_weight,stamp_weight,out_weight,down_weight,up_weight),vecs)
    def rowwise(x,sizes):
        at=0; out=[]
        for count,size in sizes:
            part=x[:,at:at+count*size].reshape(unit,count,size,x.shape[2])
            out.append(part.transpose(1,0,2,3).reshape(count*unit*size,x.shape[2])); at+=count*size
        return jnp.concatenate(out) if len(out)>1 else out[0]
    def exchange(chunks):
        return [x if c==0 else flip(x,c,total) for c,x in enumerate(chunks)]
    def chunks_of(x): return [lax.dynamic_index_in_dim(x,s0^c,0,keepdims=False) for c in range(streams)]
    bits=far_first(unit)
    first=widen(first[None],bits[0],total)
    second=widen(after(second[None],first),bits[0],total)
    for bit in bits[1:]: first=widen(first,bit,total)
    first=rowwise(settle(first,inner,unit),((4,shard),(1,SMALL)))
    n1=spread_start(first,unit,total)
    cells=chunks_of(after(tokens,second))
    for bit in bits[1:]: second=widen(second,bit,total)
    second=rowwise(settle(second,inner,unit),((1,shard),(1,ff_shard),(FF//D,shard)))
    toks=[cells[0]]+[None]*(streams-1)
    tail=streams-2
    toks[tail]=flip(cells[tail],tail,total)
    n1x,n1y,second,toks[tail]=lax.optimization_barrier((n1[1],n1[2],second,toks[tail]))
    n1=[n1[0],n1x,n1y]
    d1=spread_diag(n1,unit,total)
    n2=spread_start(second,unit,total)
    for c in range(1,streams):
        if c!=tail: toks[c]=flip(after(cells[c],toks[tail]),c,total)
    p1=spread_end(n1,*d1,unit,total)
    order=jnp.asarray(ORDER,jnp.int32)
    source=source_len[s0]; target=target_len[s0]; stamp=timesteps[s0]
    half=R*streams//2
    place=(s0^jnp.arange(streams))*R
    flag=(place>=half).astype(jnp.int32)
    nlive=jnp.clip(jnp.where(flag==1,target-(place-half),source-place),0,R).astype(jnp.int32)
    info=jnp.stack([flag,nlive],1)
    tdim=stamp_rows*total; halfway=tdim//2
    t_ids=(((order^group)[:,None,None]*unit+jnp.arange(unit)[None,:,None])*stamp_rows+jnp.arange(SMALL)[None,None,:])
    valid=(jnp.arange(SMALL)<stamp_rows)[None,None,:]
    t_ids=jnp.where(valid,t_ids,0).reshape(-1)
    rates=jnp.exp(-math.log(10000.0)*(t_ids%halfway).astype(F32)/halfway)
    angle=stamp.astype(F32)*rates
    feats=jnp.where(t_ids<halfway,jnp.sin(angle),jnp.cos(angle))
    feats=jnp.where(jnp.broadcast_to(valid,(GROUPS,unit,SMALL)).reshape(-1),feats,0.0)
    feat=jnp.broadcast_to(feats.astype(BF)[None],(8,feats.shape[0]))
    mixed,inputs,q,k,v,auxk,pre,hid,vec,upb=project(me,info,feat,toks,p1,unit,FF)
    parts=3; pairs=D//(2*HEAD); per=pairs//parts
    atts=[];auxq=[]
    def forward(c,q):
        a,x=attn_fwd(q,k,v,auxk,c*per,per); atts.append(a); auxq.append(x)
    cots=exchange(chunks_of(after(cotangent,*toks)))
    q,n2x,n2y=lax.optimization_barrier((q,n2[1],n2[2]))
    n2=[n2[0],n2x,n2y]
    d2=spread_diag(n2,unit,total)
    forward(0,q)
    forward(1,q)
    low,high,far0,far1,far2,q2,_=lax.optimization_barrier((d2[0],d2[1],*d2[2],q,atts[1]))
    forward(2,q2)
    p2=spread_end(n2,low,high,[far0,far1,far2],unit,total)
    *cots,_=lax.optimization_barrier((*cots,atts[2]))
    cot=jnp.stack(cots)
    output,ga,gatt,auxd,mine2,theirs2,dvec,dupb=middle(me,info,mixed,cot,atts,vec,upb,p2)
    dq=[];dk=[];dv=[]
    def backward(c,q):
        a,b,d=attn_bwd(q,k,v,gatt,auxk,auxq[c],auxd,c*per,per); dq.append(a);dk.append(b);dv.append(d)
    got=flip(theirs2,unit,total)
    backs=exchange([output[c] for c in range(streams)])
    backward(0,q)
    got,q3,_,backs[1]=lax.optimization_barrier((got,q,dq[0],backs[1]))
    low,high=collect_diag(mine2,got,unit,total)
    backward(1,q3)
    low,high,q4,_,backs[2]=lax.optimization_barrier((low,high,q3,dq[1],backs[2]))
    fx,fy=collect_near(mine2,got,low,high,unit,total)
    backward(2,q4)
    def place(chunks,dtype):
        out=jnp.zeros((seqs,R,D),dtype)
        for c,part in enumerate(chunks):
            out=lax.dynamic_update_index_in_dim(out,part.astype(dtype),s0^c,0)
        return out
    mine1,theirs1=weight_grads(me,inputs,dq,dk,dv,R)
    got1=flip(theirs1,unit,total)
    ga,theirs1,fx,fy,backs[3]=lax.optimization_barrier((ga,theirs1,fx,fy,backs[3]))
    at=n+FF//GROUPS
    g2=add(mine2[0],got[0],fx,fy)
    g2=jnp.concatenate([g2[:n].reshape(unit,shard,D),g2[n:at].reshape(unit,ff_shard,D)]
        +[g2[at+c*n:at+(c+1)*n].reshape(unit,shard,D) for c in range(FF//D)],1)
    keep2,got2=split_send(in_order(g2,inner),1,total)
    ga,keep2=lax.optimization_barrier((ga,keep2))
    tg,mines,theirss=token_grads(me,info,ga,pre,hid,feat,dvec,dupb,dq,dk,dv,p1,unit,R)
    got1,got2,_=lax.optimization_barrier((got1,got2,tg))
    gots=flip(theirss,unit,total)
    tgs=exchange([tg[c] for c in range(streams)])
    mine1=jnp.concatenate([mine1,mines],1); got1=jnp.concatenate([got1,gots],1)
    a1=add(mine1,got1).astype(BF)
    fx,fy,fd=flip(a1[1],2*unit,total),flip(a1[2],4*unit,total),flip(a1[3],6*unit,total)
    keep2,got2=finish2(keep2,got2,total)
    tgs[1],fx,fy=lax.optimization_barrier((tgs[1],fx,fy))
    output=place(backs,BF)
    dwo,dwd,dwu=last2(keep2,got2,shard,ff_shard,FF)
    g1=add(a1[0],fx,fy,fd)
    g1=jnp.concatenate([g1[c*n:(c+1)*n].reshape(unit,shard,D) for c in range(4)]+[g1[4*n:].reshape(unit,SMALL,D)],1)
    keep1,got1=finish(in_order(g1,inner),total)
    dwq,dwk,dwv,dwe,dws,bq,bv,bo,ag,as_,bd,fg,fs,bs,be,bu=last1(keep1,got1,shard,stamp_rows,[shard]*10+[ff_shard])
    token_grad=place(tgs,F32)
    return (output,token_grad,dwq,bq,dwk,dwv,bv,dwo,bo,ag,as_,dwu,bu,dwd,bd,fg,fs,dws,bs,dwe,be)

def solution(mesh):
    cells=P("seq","stream",None); per=P("seq"); mat=P(("seq","stream"),None); row=P(("seq","stream"))
    return jax.shard_map(on_device,mesh=mesh,
        in_specs=(cells,per,per,per,cells,mat,row,mat,mat,row,mat,row,row,row,mat,row,mat,row,row,row,mat,row,mat,row),
        out_specs=(cells,cells,mat,row,mat,mat,row,mat,row,row,row,mat,row,mat,row,row,row,mat,row,mat,row),
        check_vma=False)
```

```python
import functools
import math

import jax
import jax.numpy as jnp
from jax import lax
from jax.experimental import pallas as pl
from jax.experimental.pallas import tpu as pltpu
from jax.sharding import PartitionSpec as P

F32=jnp.float32; BF=jnp.bfloat16
NT=(((1,),(1,)),((),())); NN=(((1,),(0,)),((),())); TN=(((0,),(0,)),((),()))
def mm(a,b,dims): return lax.dot_general(a,b,dims,preferred_element_type=F32)
def lanes(shape): return lax.broadcasted_iota(jnp.int32,shape,len(shape)-1)
def split3(x):
    hi=x.astype(BF).astype(F32); r=x-hi
    mid=r.astype(BF).astype(F32); lo=r-mid
    return hi,mid,lo
QB=256
def fwd_kernel(q_ref,k_ref,v_ref,auxk_ref,o_ref,auxq_ref,kaug,vm):
    L=q_ref.shape[0]
    k=k_ref[...]; v=v_ref[...]; ln=lanes(k.shape)
    for e in range(2):
        sel=(ln<64) if e==0 else (ln>=64)
        kaug[e,:,:128]=jnp.where(sel,k,jnp.zeros_like(k))
        kaug[e,:,128:]=auxk_ref[...]
        vm[e]=jnp.where(sel,v,(ln==64*(1-e)).astype(BF))
    ln=lanes((QB,128)); one=jnp.where(ln==64,1.0,0.0).astype(BF)
    steps=[(b,e) for b in range(L//QB) for e in range(2)]
    def score(b,e):
        return mm(jnp.concatenate([q_ref[pl.ds(b*QB,QB),:],one],axis=1),kaug[e],NT)
    s=score(*steps[0]); out=None; aux=None
    for t,(b,e) in enumerate(steps):
        later=score(*steps[t+1]) if t+1<len(steps) else None
        m=jnp.max(s,axis=1,keepdims=True)
        p=jnp.exp(s-m).astype(BF)
        o=mm(p,vm[e],NN)
        l=o[:,64*(1-e):64*(1-e)+1]
        o=jnp.where((ln<64) if e==0 else (ln>=64),o*(1.0/l),0.0)
        hi,mid,lo=split3(-(m+jnp.log(l)))
        if e==0: out=o; aux=jnp.where(ln==64,1.0,0.0)
        else: out=out+o
        aux=jnp.where(ln==3*e,hi,aux); aux=jnp.where(ln==3*e+1,mid,aux); aux=jnp.where(ln==3*e+2,lo,aux)
        if e==1:
            r=pl.ds(b*QB,QB)
            o_ref[r,:]=out.astype(BF); auxq_ref[0,r,:]=aux.astype(BF)
        s=later
def attn_fwd(q,k,v,auxk,p0,np_):
    L=q.shape[0]
    col=lambda: pl.BlockSpec((L,128),lambda p:(0,p0+p))
    return pl.pallas_call(fwd_kernel,grid=(np_,),
      in_specs=[col(),col(),col(),pl.BlockSpec((L,128),lambda p:(0,0))],
      out_specs=[pl.BlockSpec((L,128),lambda p:(0,p)),pl.BlockSpec((1,L,128),lambda p:(p,0,0))],
      out_shape=[jax.ShapeDtypeStruct((L,128*np_),BF),jax.ShapeDtypeStruct((np_,L,128),BF)],
      scratch_shapes=[pltpu.VMEM((2,L,256),BF),pltpu.VMEM((2,L,128),BF)],
      compiler_params=pltpu.CompilerParams(vmem_limit_bytes=60*2**20),
      cost_estimate=pl.CostEstimate(flops=np_*2*L*L*64*4,bytes_accessed=np_*L*128*2*5,transcendentals=np_*2*L*L),
      name="attn_fwd")(q,k,v,auxk)
def bwd_kernel(p0,q_ref,k_ref,v_ref,do_ref,auxk_ref,auxq_ref,auxd_ref,out_ref,kaug,vaug,qa,doa,qm,dom,dk_acc,dv_acc):
    pair=p0+pl.program_id(0)
    L=q_ref.shape[0]
    k=k_ref[...]; v=v_ref[...]; q=q_ref[...]; do=do_ref[...]
    ln=lanes(k.shape); z=jnp.zeros_like(k); auxk=auxk_ref[...]
    qa[:,:128]=q; qa[:,128:]=auxq_ref[0]
    doa[:,:128]=do; doa[:,128:]=auxd_ref[...]
    for e in range(2):
        sel=(ln<64) if e==0 else (ln>=64)
        on=(ln>=3*e)&(ln<3*e+3)
        kaug[e,:,:128]=jnp.where(sel,k,z)
        kaug[e,:,128:]=jnp.where(on,jnp.ones_like(k),auxk)
        vaug[e,:,:128]=jnp.where(sel,v,z)
        b=6*pair+3*e
        vaug[e,:,128:]=jnp.where((ln>=b)&(ln<b+3),jnp.ones_like(k),z)
        qm[e]=jnp.where(sel,q,z)
        dom[e]=jnp.where(sel,do,z)
    for i in range(L//QB):
        r=pl.ds(i*QB,QB)
        dq=None
        for e in range(2):
            p=jnp.exp(mm(kaug[e],qa[r,:],NT))
            dp=mm(vaug[e],doa[r,:],NT)
            ds=(p*dp).astype(BF)
            dv=mm(p.astype(BF),dom[e,r,:],NN)
            dk=mm(ds,qm[e,r,:],NN)
            if i==0 and e==0: dv_acc[...]=dv; dk_acc[...]=dk
            else: dv_acc[...]+=dv; dk_acc[...]+=dk
            d=mm(ds,kaug[e,:,:128],TN)
            dq=d if dq is None else dq+d
        out_ref[0,r,:]=(dq*0.125).astype(BF)
    out_ref[1]=dk_acc[...].astype(BF)
    out_ref[2]=dv_acc[...].astype(BF)
def attn_bwd(q,k,v,do,auxk,auxq,auxd,p0,np_,a0):
    L=q.shape[0]
    col=lambda: pl.BlockSpec((L,128),lambda p:(0,p0+p))
    con=lambda: pl.BlockSpec((L,128),lambda p:(0,0))
    return pl.pallas_call(functools.partial(bwd_kernel,p0),grid=(np_,),
      in_specs=[col(),col(),col(),col(),con(),pl.BlockSpec((1,L,128),lambda p:(a0+p,0,0)),con()],
      out_specs=pl.BlockSpec((3,L,128),lambda p:(0,0,p)),
      out_shape=jax.ShapeDtypeStruct((3,L,128*np_),BF),
      scratch_shapes=[pltpu.VMEM((2,L,256),BF),pltpu.VMEM((2,L,256),BF),pltpu.VMEM((L,256),BF),pltpu.VMEM((L,256),BF),
        pltpu.VMEM((2,L,128),BF),pltpu.VMEM((2,L,128),BF),pltpu.VMEM((L,128),F32),pltpu.VMEM((L,128),F32)],
      compiler_params=pltpu.CompilerParams(vmem_limit_bytes=60*2**20),
      cost_estimate=pl.CostEstimate(flops=np_*2*L*L*64*10,bytes_accessed=np_*L*128*2*9,transcendentals=np_*2*L*L),
      name="attn_bwd")(q,k,v,do,auxk,auxq,auxd)

SMALL=16; Q_B,V_B,OUT_B,ATT_G,ATT_S,DOWN_B,FFN_G,FFN_S,STAMP_B,EMBED_B=range(4,14); UP_B=14
def owner_of(rows,me,unit,width):
    r=lax.shift_right_logical(lax.broadcasted_iota(jnp.int32,(rows,width),0),SMALL.bit_length()-1)
    shift=unit.bit_length()-1
    t=lax.shift_right_logical(r,shift)
    g=jnp.bitwise_xor(jnp.bitwise_or(jnp.bitwise_and(t*2,7),lax.shift_right_logical(t,2)),me)
    return g*unit+jnp.bitwise_and(r,unit-1)
def repeats(width,shard):
    l=lax.broadcasted_iota(jnp.int32,(128,width),0).astype(F32); d=lax.broadcasted_iota(jnp.int32,(128,width),1).astype(F32)
    return (d-shard*jnp.floor((d+0.5)*(1.0/shard))==l).astype(BF)
def owned(owner,shard):
    d=lax.broadcasted_iota(jnp.int32,owner.shape,1)
    return (d>=owner*shard)&(d<owner*shard+shard)
def pack_kernel(*refs):
    *ins,first_ref,second_ref,scr=refs
    wq,wk,wv,we,st,wo,wd,wu=ins[:8]; vecs=ins[8:]
    scr[...]=jnp.zeros_like(scr)
    scr[:st.shape[0],:]=st[...]
    for r,v in enumerate(vecs):
        scr[4+r:5+r,:v.shape[0]]=v[...].reshape(1,-1)
    D=wq.shape[1]
    first_ref[...]=jnp.concatenate([wq[...],wk[...],wv[...],we[...],scr[...]],axis=0).astype(BF)
    up=[wu[:,c*D:(c+1)*D] for c in range(wu.shape[1]//D)]
    second_ref[...]=jnp.concatenate([wo[...],wd[...]]+up,axis=0).astype(BF)
def pack(mats,vecs):
    wq,wk,wv,we,st,wo,wd,wu=mats; n,D=wq.shape
    vm=pl.BlockSpec(memory_space=pltpu.VMEM)
    second=n+wd.shape[0]+n*(wu.shape[1]//D)
    if n%8:
        small=jnp.concatenate([st]+[jnp.zeros((4-st.shape[0],D),F32)]+[jnp.pad(v,(0,D-v.shape[0]))[None] for v in vecs]+[jnp.zeros((SMALL-4-len(vecs),D),F32)])
        up=[wu[:,c*D:(c+1)*D] for c in range(wu.shape[1]//D)]
        return jnp.concatenate([wq,wk,wv,we,small]).astype(BF),jnp.concatenate([wo,wd]+up).astype(BF)
    return pl.pallas_call(pack_kernel,in_specs=[vm]*(8+len(vecs)),out_specs=[vm]*2,
      out_shape=[sds((4*n+SMALL,D),BF),sds((second,D),BF)],scratch_shapes=[pltpu.VMEM((SMALL,D),F32)],name="pack")(*mats,*vecs)
ORDER=(0,2,4,6,1,3,5,7)
def rows_at(me,t,n):
    return pl.ds(pl.multiple_of(jnp.bitwise_xor(me,ORDER[t])*n,n),n)
def sds(*a): return jax.ShapeDtypeStruct(*a)
def once(s): return pl.BlockSpec(s.shape,lambda i:(0,)*len(s.shape),pipeline_mode=pl.Buffered(1))
def smem(): return pl.BlockSpec(memory_space=pltpu.SMEM)
def anyw(): return pl.BlockSpec(memory_space=pl.ANY)
def load_weights(me,pieces,base,n,dst,sem):
    return [pltpu.make_async_copy(p.at[pl.ds(base,n),:],dst.at[rows_at(me,t,n),:],sem) for t,p in enumerate(pieces)]
def in_kernel(nt,unit,me_ref,info_ref,feat_ref,*rest):
    toks=rest[:nt]; pieces=rest[nt:nt+8]
    mixed_ref,inp_ref,q_ref,k_ref,v_ref,auxk_ref,pre_ref,hid_ref,vec_ref,upb_ref,tok,wq,wk,wv,we,ws,emb,sems=rest[nt+8:]
    i=pl.program_id(0); me=me_ref[0]
    D=wq.shape[0]; n=D//8; ns=ws.shape[0]//8
    tcp=[pltpu.make_async_copy(t,tok.at[c],sems.at[5+c]) for c,t in enumerate(toks)]
    scp=[pltpu.make_async_copy(p.at[pl.ds(4*n,ns),:],ws.at[pl.ds(t*ns,ns),:],sems.at[0]) for t,p in enumerate(pieces)]
    wcp=[load_weights(me,pieces,w*n,n,dst,sems.at[1+w]) for w,dst in enumerate((wq,wk,wv,we))]
    vec=lambda r: vec_ref[pl.ds(r,1),:]
    @pl.when(i==0)
    def _():
        for c in scp+wcp[3]+tcp[:1]+wcp[0]+wcp[1]+wcp[2]+tcp[1:]: c.start()
        for c in scp: c.wait()
        rows=8*ns; total=8*unit; FF=upb_ref.shape[1]
        lead=ws[:,:128]
        spread=mm(lead,repeats(D,D//total),NN)
        spread=jnp.where(owned(owner_of(rows,me,unit,D),D//total),spread,0.0)
        vec_ref[...]=jnp.sum(spread.reshape(total,SMALL,D),axis=0)
        ups=lead.astype(F32).reshape(total,SMALL,128)[:,UP_B,:].astype(BF)
        ups=mm(ups,repeats(FF,FF//total),NN)
        own=owner_of(rows,me,unit,128).reshape(total,SMALL,128)[:,0,:1]
        upb_ref[...]=jnp.sum(jnp.where(owned(jnp.broadcast_to(own,(total,FF)),FF//total),ups,0.0),axis=0,keepdims=True)
        pre=mm(feat_ref[...],ws[...],NN)+vec(STAMP_B)
        pre_ref[...]=pre
        hid=(pre/(1.0+jnp.exp(-pre))).astype(BF)
        hid_ref[...]=hid
        for c in wcp[3]: c.wait()
        emb[...]=mm(hid,we[...],NN)+vec(EMBED_B)
    for c in range(nt):
        @pl.when(i==c)
        def _(): tcp[c].wait()
    flag=info_ref[i,0].astype(F32); nlive=info_ref[i,1]
    x=tok[i].astype(F32)+flag*emb[pl.ds(0,1),:]
    mixed_ref[...]=x
    xb=x.astype(BF); inp_ref[...]=xb
    R=x.shape[0]
    ln=lanes((R,128)); row=lax.broadcasted_iota(jnp.int32,(R,128),0)
    auxk_ref[...]=jnp.where((ln==64)&(row>=nlive),-1e30,0.0).astype(BF)
    @pl.when(i==0)
    def _():
        for w in range(3):
            for c in wcp[w]: c.wait()
    q=(mm(xb,wq[...],NN)+vec(Q_B)).astype(BF)
    q_ref[...]=(q.astype(F32)*0.125).astype(BF)
    k_ref[...]=mm(xb,wk[...],NN).astype(BF)
    v_ref[...]=(mm(xb,wv[...],NN)+vec(V_B)).astype(BF)
def project(me,info,feat,toks,pieces,unit,FF):
    nt=len(toks); R,D=toks[0].shape; n=D//8; ns=pieces[0].shape[0]-4*n; L=nt*R
    row=lambda w: pl.BlockSpec((R,w),lambda i:(i,0))
    full=lambda a: pl.BlockSpec(a.shape,lambda i:(0,)*a.ndim)
    outs=[sds((L,D),F32)]+[sds((L,D),BF)]*4+[sds((L,128),BF),sds((8,D),F32),sds((8,D),BF),sds((SMALL,D),F32),sds((1,FF),F32)]
    return pl.pallas_call(functools.partial(in_kernel,nt,unit),grid=(nt,),
      in_specs=[smem(),smem(),full(feat)]+[anyw()]*(nt+8),
      out_specs=[row(D)]*5+[row(128)]+[once(o) for o in outs[6:]],
      out_shape=outs,
      scratch_shapes=[pltpu.VMEM((nt,R,D),BF)]+[pltpu.VMEM((D,D),BF)]*4+[pltpu.VMEM((8*ns,D),BF),pltpu.VMEM((8,D),F32),pltpu.SemaphoreType.DMA((5+nt,))],
      compiler_params=pltpu.CompilerParams(vmem_limit_bytes=60*2**20),
      cost_estimate=pl.CostEstimate(flops=2*L*D*D*3,bytes_accessed=20_000_000,transcendentals=0),
      name="project")(me,info,feat,*toks,*pieces)

def spread3(row):
    hi,mid,lo=split3(row)
    r=lax.broadcasted_iota(jnp.int32,(8,row.shape[1]),0)
    return jnp.where(r==0,hi,jnp.where(r==1,mid,jnp.where(r==2,lo,0.0))).astype(BF)
def three(rows):
    r=lax.broadcasted_iota(jnp.int32,rows.shape,0)
    return jnp.where(r<3,jnp.broadcast_to(rows[0:1,:].astype(F32),rows.shape),0.0).astype(BF)
def token_kernel(nc,me_ref,info_ref,ga_ref,pre_ref,*rest):
    grads=rest[:nc]; pieces=rest[nc:nc+8]
    tg_ref,rows_ref,wq,wk,wv,we,sems=rest[nc+8:]
    i=pl.program_id(0); me=me_ref[0]
    D=wq.shape[0]; n=D//8
    wcp=[load_weights(me,pieces,w*n,n,dst,sems.at[w]) for w,dst in enumerate((wq,wk,wv,we))]
    @pl.when(i==0)
    def _():
        for w in wcp:
            for c in w: c.start()
        rows_ref[...]=jnp.zeros_like(rows_ref)
    g=ga_ref[...]
    for w,dst in enumerate((wq,wk,wv)):
        y=jnp.concatenate([s[w] for s in grads],axis=1)
        if w!=1: rows_ref[pl.ds(w//2,1),:]+=jnp.sum(y.astype(F32),axis=0,keepdims=True)
        @pl.when(i==0)
        def _():
            for c in wcp[w]: c.wait()
        g=g+mm(y,dst[...],NT)
    tg_ref[0]=g.astype(BF)
    rows_ref[pl.ds(3,1),:]+=info_ref[i,0].astype(F32)*jnp.sum(g,axis=0,keepdims=True)
    @pl.when(i==pl.num_programs(0)-1)
    def _():
        for c in wcp[3]: c.wait()
        gh=jnp.sum(mm(spread3(rows_ref[pl.ds(3,1),:]),we[...],NT),axis=0,keepdims=True)
        pre=pre_ref[0:1,:]
        sg=1.0/(1.0+jnp.exp(-pre))
        rows_ref[pl.ds(2,1),:]=gh*(sg*(1.0+pre*(1.0-sg)))
def token_grads(me,info,ga,pre,grads,pieces,R):
    L,D=ga.shape; nt=L//R; nc=len(grads); W=grads[0].shape[2]
    outs=[sds((nt,R,D),BF),sds((8,D),F32)]
    return pl.pallas_call(functools.partial(token_kernel,nc),grid=(nt,),
      in_specs=[smem(),smem(),pl.BlockSpec((R,D),lambda i:(i,0)),pl.BlockSpec((8,D),lambda i:(0,0))]+[pl.BlockSpec((3,R,W),lambda i:(0,i,0))]*nc+[anyw()]*8,
      out_specs=[pl.BlockSpec((1,R,D),lambda i:(i,0,0)),once(outs[1])],
      out_shape=outs,
      scratch_shapes=[pltpu.VMEM((D,D),BF)]*4+[pltpu.SemaphoreType.DMA((4,))],
      compiler_params=pltpu.CompilerParams(vmem_limit_bytes=60*2**20),
      cost_estimate=pl.CostEstimate(flops=2*L*D*D*3,bytes_accessed=15_000_000,transcendentals=0),
      name="token_grads")(me,info,ga,pre,*grads,*pieces)
def weight_kernel(nc,unit,me_ref,inp_ref,rows_ref,hid_ref,feat_ref,dvec_ref,dupb_ref,*rest):
    grads=rest[:nc]
    mine_ref,theirs_ref,acc=rest[nc:]
    i=pl.program_id(0); me=me_ref[0]
    D=inp_ref.shape[1]; n=D//8; rows=feat_ref.shape[1]; ns=rows//8
    def to(t): return mine_ref if t<4 else theirs_ref
    @pl.when(i==0)
    def _():
        acc[:,3*D:]=mm(three(hid_ref[...]),spread3(rows_ref[3:4,:]),TN)
        total=8*unit; FF=dupb_ref.shape[1]
        r=lax.broadcasted_iota(jnp.int32,(SMALL,D),0)
        vec=dvec_ref[...]
        for at,row in ((Q_B,0),(V_B,1),(STAMP_B,2),(EMBED_B,3)):
            vec=jnp.where(r==at,rows_ref[row:row+1,:],vec)
        vec=jnp.broadcast_to(vec[None],(total,SMALL,D)).reshape(rows,D)
        vec=jnp.where(owned(owner_of(rows,me,unit,D),D//total),vec,0.0).astype(BF)
        vec=mm(vec,repeats(D,D//total),NT)
        own=owner_of(rows,me,unit,128).reshape(total,SMALL,128)[:,0,:1]
        ups=jnp.where(owned(jnp.broadcast_to(own,(total,FF)),FF//total),dupb_ref[...],0.0).astype(BF)
        ups=mm(ups,repeats(FF,FF//total),NT)
        line=jnp.bitwise_and(lax.broadcasted_iota(jnp.int32,(rows,128),0),SMALL-1)
        ups=jnp.broadcast_to(ups[:,None,:],(total,SMALL,128)).reshape(rows,128)
        vec=jnp.where(line==UP_B,ups,jnp.where((line>=4)&(line<UP_B),vec,0.0))
        small=mm(three(feat_ref[...]),spread3(rows_ref[2:3,:]),TN)
        small=small+jnp.concatenate([vec,jnp.zeros((rows,D-128),F32)],axis=1)
        small=small.astype(BF)
        for t in range(8): to(t)[t%4,4*n:,:]=small[t*ns:(t+1)*ns]
    part=mm(inp_ref[...],jnp.concatenate([s[w] for w in range(3) for s in grads],axis=1),TN)
    @pl.when(i==0)
    def _(): acc[:,:3*D]=part
    @pl.when(i>0)
    def _(): acc[:,:3*D]+=part
    @pl.when(i==pl.num_programs(0)-1)
    def _():
        for t in range(8):
            for w in range(4): to(t)[t%4,w*n:(w+1)*n,:]=acc[rows_at(me,t,n),w*D:(w+1)*D].astype(BF)
def weight_grads(me,inp,rows,hid,feat,dvec,dupb,grads,unit,R):
    L,D=inp.shape; n=D//8; nc=len(grads); W=grads[0].shape[2]
    outs=[sds((4,4*n+feat.shape[1]//8,D),BF)]*2
    full=lambda a: pl.BlockSpec(a.shape,lambda i:(0,)*a.ndim)
    return pl.pallas_call(functools.partial(weight_kernel,nc,unit),grid=(L//R,),
      in_specs=[smem(),pl.BlockSpec((R,D),lambda i:(i,0))]+[full(a) for a in (rows,hid,feat,dvec,dupb)]+[pl.BlockSpec((3,R,W),lambda i:(0,i,0))]*nc,
      out_specs=[once(o) for o in outs],out_shape=outs,
      scratch_shapes=[pltpu.VMEM((D,4*D),F32)],
      compiler_params=pltpu.CompilerParams(vmem_limit_bytes=60*2**20),
      cost_estimate=pl.CostEstimate(flops=2*L*D*D*3,bytes_accessed=12_000_000,transcendentals=0),
      name="weight_grads")(me,inp,rows,hid,feat,dvec,dupb,*grads)
LB=384
def take(k,R): return pl.BlockSpec((1,R,LB),lambda i:(k,0,i))
def flat(R): return pl.BlockSpec((R,LB),lambda i:(0,i))
def total_of(refs):
    out=refs[0].astype(F32)
    for r in refs[1:]: out=out+r.astype(F32)
    return out
def diag_kernel(cut,a,b,low,high):
    x=total_of((a[0],b[0])).astype(BF)
    low[...]=x[:cut]; high[...]=x[cut:]
def sum_diag(mine,got,cut):
    _,R,D=mine.shape
    return pl.pallas_call(functools.partial(diag_kernel,cut),grid=(D//LB,),in_specs=[take(3,R)]*2,out_specs=[flat(cut),flat(R-cut)],
      out_shape=[sds((cut,D),BF),sds((R-cut,D),BF)],name="sum_diag")(mine,got)
def near_kernel(cut,a1,b1,a2,b2,low,high,fx,fy):
    fx[:cut,:]=total_of((a1[0,:cut],b1[0,:cut])).astype(BF)
    fx[cut:,:]=total_of((a1[0,cut:],b1[0,cut:],high[...])).astype(BF)
    fy[:cut,:]=total_of((a2[0,:cut],b2[0,:cut],low[...])).astype(BF)
    fy[cut:,:]=total_of((a2[0,cut:],b2[0,cut:])).astype(BF)
def sum_near(mine,got,low,high):
    _,R,D=mine.shape; cut=low.shape[0]
    return pl.pallas_call(functools.partial(near_kernel,cut),grid=(D//LB,),in_specs=[take(1,R)]*2+[take(2,R)]*2+[flat(cut),flat(R-cut)],
      out_specs=[flat(R)]*2,out_shape=[sds((R,D),BF)]*2,name="sum_near")(mine,got,mine,got,low,high)
def three_kernel(a1,b1,a2,b2,a3,b3,o1,o2,o3):
    for a,b,o in ((a1,b1,o1),(a2,b2,o2),(a3,b3,o3)): o[...]=total_of((a[0],b[0])).astype(BF)
def sum_three(mine,got):
    _,R,D=mine.shape
    return pl.pallas_call(three_kernel,grid=(D//LB,),in_specs=[take(1,R)]*2+[take(2,R)]*2+[take(3,R)]*2,
      out_specs=[flat(R)]*3,out_shape=[sds((R,D),BF)]*3,name="sum_three")(mine,got,mine,got,mine,got)
def own_kernel(sizes,unit,nx,inner_ref,a,b,*rest):
    more=rest[:nx]; keep,send,scr=rest[nx:]
    inner=inner_ref[0]
    scr[...]=total_of((a[0],b[0])+tuple(x[...] for x in more))
    for j in range(unit):
        k=jnp.bitwise_xor(inner,j); at=0; out=0
        for count,size in sizes:
            for c in range(count):
                x=scr[pl.ds(pl.multiple_of(at+k*size,8),size),:]
                if j%2: send[j//2,out:out+size,:]=x.astype(BF)
                else: keep[j//2,out:out+size,:]=x
                at+=unit*size; out+=size
def sum_own(inner,mine,got,more,sizes,unit,total):
    _,R,D=mine.shape; rows=R//unit
    if any(size%8 for _,size in sizes):
        x=mine[0].astype(F32)+got[0].astype(F32)+sum(m.astype(F32) for m in more); at=0; parts=[]
        for count,size in sizes:
            for c in range(count):
                parts.append(x[at:at+unit*size].reshape(unit,size,D)); at+=unit*size
        return split_send(in_order(jnp.concatenate(parts,1),inner),1,total)
    blk=pl.BlockSpec((unit//2,rows,LB),lambda i:(0,0,i))
    keep,send=pl.pallas_call(functools.partial(own_kernel,sizes,unit,len(more)),grid=(D//LB,),
      in_specs=[smem()]+[take(0,R)]*2+[flat(R)]*len(more),out_specs=[blk]*2,
      out_shape=[sds((unit//2,rows,D),F32),sds((unit//2,rows,D),BF)],scratch_shapes=[pltpu.VMEM((R,LB),F32)],name="sum_own")(inner.reshape(1).astype(jnp.int32),mine,got,*more)
    return keep,flip(send,1,total)
def last1_kernel(keep_ref,got_ref,*outs):
    x=keep_ref[...]+got_ref[...].astype(F32)
    *mats,st=outs[:5]; n=mats[0].shape[0]
    for w,o in enumerate(mats): o[...]=x[w*n:(w+1)*n]
    st[...]=x[4*n:4*n+st.shape[0]]
    for r,o in enumerate(outs[5:]):
        o[...]=x[4*n+4+r:4*n+5+r,:o.shape[0]].reshape(o.shape)
def last1(keep,got,n,stamp_rows,sizes):
    D=keep.shape[1]
    vm=pl.BlockSpec(memory_space=pltpu.VMEM)
    outs=[sds((n,D),F32)]*4+[sds((stamp_rows,D),F32)]+[sds((k,),F32) for k in sizes]
    if n%8:
        x=keep+got.astype(F32)
        return [x[w*n:(w+1)*n] for w in range(4)]+[x[4*n:4*n+stamp_rows]]+[x[4*n+4+r,:k] for r,k in enumerate(sizes)]
    return pl.pallas_call(last1_kernel,in_specs=[vm]*2,out_specs=[vm]*len(outs),out_shape=outs,name="last_attn")(keep,got)
def last2_kernel(keep_ref,got_ref,wo,wd,wu):
    x=keep_ref[...]+got_ref[...].astype(F32); n,D=wo.shape; m=wd.shape[0]
    wo[...]=x[:n]; wd[...]=x[n:n+m]
    for c in range(wu.shape[1]//D): wu[:,c*D:(c+1)*D]=x[n+m+c*n:n+m+(c+1)*n]
def last2(keep,got,n,m,FF):
    D=keep.shape[1]
    vm=pl.BlockSpec(memory_space=pltpu.VMEM)
    outs=[sds((n,D),F32),sds((m,D),F32),sds((n,FF),F32)]
    if n%8:
        x=keep+got.astype(F32)
        return x[:n],x[n:n+m],jnp.concatenate([x[n+m+c*n:n+m+(c+1)*n] for c in range(FF//D)],1)
    return pl.pallas_call(last2_kernel,in_specs=[vm]*2,out_specs=[vm]*3,out_shape=outs,name="last_ffn")(keep,got)

INV_SQRT2=0.7071067811865476; INV_SQRT2PI=0.3989422804014327
HEAD=64
RB=256; FC=768
def norm_stats(x):
    mu=jnp.mean(x,axis=1,keepdims=True); c=x-mu
    r=lax.rsqrt(jnp.mean(c*c,axis=1,keepdims=True)+1e-5)
    return c*r,r
def norm_back(e,n,r):
    return r*(e-jnp.mean(e,axis=1,keepdims=True)-n*jnp.mean(e*n,axis=1,keepdims=True))
def colsum(x): return jnp.sum(x,axis=0,keepdims=True)
def mid_kernel(nblk,me_ref,info_ref,mix_ref,cot_ref,att_refs,vec_ref,upb_ref,pieces,
        out_ref,gas_ref,gatt_ref,auxd_ref,mine_ref,theirs_ref,dvec_ref,dupb_ref,
        wo,wd,wu,awo,awd,awu,gel,dgel,sems):
    i=pl.program_id(0); nb=pl.num_programs(0)
    D=wo.shape[0]; FF=wd.shape[0]; ro=D//nblk; rd=FF//nblk
    me=me_ref[0]
    lower=[p[0] if isinstance(p,tuple) else p for p in pieces]
    upper=[(p[1],0) if isinstance(p,tuple) else (p,ro+rd) for p in pieces]
    cps=[load_weights(me,lower,0,ro,wo,sems.at[0]),
        [pltpu.make_async_copy(p.at[pl.ds(at+b*ro,ro),:],wu.at[rows_at(me,t,ro),pl.ds(b*D,D)],sems.at[1])
            for b in range(FF//D) for t,(p,at) in enumerate(upper)],
        load_weights(me,lower,ro,rd,wd,sems.at[2])]
    def wait(which):
        @pl.when(i==0)
        def _():
            for c in cps[which]: c.wait()
    @pl.when(i==0)
    def _():
        for w in cps:
            for c in w: c.start()
        awo[...]=jnp.zeros_like(awo); awd[...]=jnp.zeros_like(awd); awu[...]=jnp.zeros_like(awu)
        dvec_ref[...]=jnp.zeros_like(dvec_ref); dupb_ref[...]=jnp.zeros_like(dupb_ref)
    vec=lambda r: vec_ref[pl.ds(r,1),:].astype(F32)
    nlive=info_ref[i,1]
    x0=mix_ref[...]
    live=(lax.broadcasted_iota(jnp.int32,(RB,1),0)<nlive).astype(F32)
    wait(0)
    att=jnp.concatenate([a[...] for a in att_refs],axis=1)
    asum=x0+(mm(att,wo[...],NN)+vec(OUT_B))
    n1,r1=norm_stats(asum)
    normed=n1*vec(ATT_G)+vec(ATT_S)
    hid=normed.astype(BF)
    wait(1); wait(2)
    down=None
    for f in range(FF//FC):
        c=slice(f*FC,(f+1)*FC)
        u=mm(hid,wu[:,c],NN)+upb_ref[:,c].astype(F32)
        ph=0.5+0.5*lax.erf(u*INV_SQRT2)
        pd=jnp.exp(u*u*-0.5)*INV_SQRT2PI
        g=(u*ph).astype(BF)
        gel[:,c]=g
        dgel[:,c]=ph+u*pd
        t=mm(g,wd[c,:],NN)
        down=t if down is None else down+t
    fsum=normed+(down+vec(DOWN_B))
    n2,r2=norm_stats(fsum)
    g2=vec(FFN_G)
    out_ref[0]=((n2*g2+vec(FFN_S))*live).astype(BF)
    og=cot_ref[0].astype(F32)*live
    dvec_ref[pl.ds(FFN_G,1),:]+=colsum(og*n2)
    dvec_ref[pl.ds(FFN_S,1),:]+=colsum(og)
    gf=norm_back(og*g2,n2,r2)
    gd=gf.astype(BF)
    dvec_ref[pl.ds(DOWN_B,1),:]+=colsum(gd.astype(F32))
    gn=gf
    for f in range(FF//FC):
        c=slice(f*FC,(f+1)*FC)
        gu=(mm(gd,wd[c,:],NT)*dgel[:,c]).astype(BF)
        dupb_ref[:,c]+=colsum(gu.astype(F32))
        awd[c,:]+=mm(gel[:,c],gd,TN)
        awu[:,c]+=mm(hid,gu,TN)
        gn=gn+mm(gu,wu[:,c],NT)
    dvec_ref[pl.ds(ATT_G,1),:]+=colsum(gn*n1)
    dvec_ref[pl.ds(ATT_S,1),:]+=colsum(gn)
    ga=norm_back(gn*vec(ATT_G),n1,r1)
    gas_ref[...]=ga
    gb=ga.astype(BF)
    dvec_ref[pl.ds(OUT_B,1),:]+=colsum(gb.astype(F32))
    awo[...]+=mm(att,gb,TN)
    gatt=mm(gb,wo[...],NT).astype(BF)
    gatt_ref[...]=gatt
    pr=-(gatt.astype(F32)*att.astype(F32))
    hi,mid,lo=split3(pr)
    hrow=lax.broadcasted_iota(jnp.int32,(D,128),0)//64
    hcol=lax.broadcasted_iota(jnp.int32,(D,128),1)
    ind=((hcol>=3*hrow)&(hcol<3*hrow+3)).astype(BF)
    dl=mm(hi.astype(BF),ind,NN)+mm(mid.astype(BF),ind,NN)
    h2,m2,l2=split3(dl)
    ln=lanes(dl.shape)%3
    auxd_ref[...]=jnp.where(ln==0,h2,jnp.where(ln==1,m2,l2)).astype(BF)
    @pl.when(i==nb-1)
    def _():
        def send(src,at,n):
            cps=[pltpu.make_async_copy(src.at[rows_at(me,t,n),:],(mine_ref if t<4 else theirs_ref).at[t%4,pl.ds(at,n),:],sems.at[3]) for t in range(8)]
            for c in cps: c.start()
            return cps
        wo[...]=awo[...].astype(BF)
        out=send(wo,0,ro)
        wd[...]=awd[...].astype(BF)
        out+=send(wd,ro,rd)
        wu[...]=awu[...].astype(BF)
        for b in range(FF//D): out+=send(wu.at[:,pl.ds(b*D,D)],ro+rd+b*ro,ro)
        for c in out: c.wait()
def middle(me,info,mixed,cot,atts,vec,upb,pieces):
    nblk=8; L,D=mixed.shape; FF=upb.shape[1]; ro=D//8; rd=FF//8
    nb=L//RB; na=len(atts)
    flat_pieces=jax.tree.leaves(pieces)
    def kern(me_ref,info_ref,mix_ref,cot_ref,*rest):
        att=rest[:na]; rest=rest[na:]
        given=iter(rest[2:2+len(flat_pieces)])
        blocks=[(next(given),next(given)) if isinstance(p,tuple) else next(given) for p in pieces]
        mid_kernel(nblk,me_ref,info_ref,mix_ref,cot_ref,att,rest[0],rest[1],blocks,*rest[2+len(flat_pieces):])
    full=lambda a: pl.BlockSpec(a.shape,lambda i:(0,)*a.ndim)
    blk=pl.BlockSpec((1,RB,D),lambda i:(i,0,0)); row=pl.BlockSpec((RB,D),lambda i:(i,0))
    outs=[sds((nb,RB,D),BF),sds((L,D),F32),sds((L,D),BF),sds((L,128),BF)]+[sds((4,)+pieces[0].shape,BF)]*2+[sds((16,D),F32),sds((1,FF),F32)]
    return pl.pallas_call(kern,grid=(nb,),
      in_specs=[smem(),smem(),row,blk]+[pl.BlockSpec((RB,a.shape[1]),lambda i:(i,0)) for a in atts]+[full(vec),full(upb)]+[anyw()]*len(flat_pieces),
      out_specs=[blk,row,row,pl.BlockSpec((RB,128),lambda i:(i,0)),anyw(),anyw()]+[once(s) for s in outs[6:]],
      out_shape=outs,
      scratch_shapes=[pltpu.VMEM((D,D),BF),pltpu.VMEM((FF,D),BF),pltpu.VMEM((D,FF),BF),
        pltpu.VMEM((D,D),F32),pltpu.VMEM((FF,D),F32),pltpu.VMEM((D,FF),F32),
        pltpu.VMEM((RB,FF),BF),pltpu.VMEM((RB,FF),F32),pltpu.SemaphoreType.DMA((4,))],
      compiler_params=pltpu.CompilerParams(vmem_limit_bytes=61*2**20),
      cost_estimate=pl.CostEstimate(flops=2*L*D*(3*D+6*FF),bytes_accessed=60_000_000,transcendentals=2*L*FF),
      name="middle")(me,info,mixed,cot,*atts,vec,upb,*flat_pieces)

GROUPS=8
AXES=("seq","stream")
def flip(x,mask,total):
    return lax.ppermute(x,AXES,[(i,i^mask) for i in range(total)])
def far_first(count):
    bits=[]; bit=count//2
    while bit: bits.append(bit); bit//=2
    return bits
def widen(x,bit,total): return jnp.concatenate([x,flip(x,bit,total)])
def settle(x,inner,count):
    ids=[0]
    for bit in far_first(count): ids=ids+[i^bit for i in ids]
    return in_order(jnp.stack([x[ids.index(k)] for k in range(count)]),inner)
def in_order(x,index):
    n=x.shape[0]; bit=1
    while bit<n:
        turned=jnp.concatenate([x[k^bit][None] for k in range(n)])
        x=jnp.where((index&bit)!=0,turned,x); bit*=2
    return x
def after(x,*deps):
    return lax.optimization_barrier((x,)+deps)[0]
def sync(*xs): return lax.optimization_barrier(xs)
def spread_start(own,unit,total):
    across=lambda x,g: flip(x,g*unit,total)
    return [own,across(own,2),across(own,4)]
def split_send(x,bit,total):
    send=jnp.stack([x[j] for j in range(1,x.shape[0],2)]).astype(BF)
    return jnp.stack([x[j] for j in range(0,x.shape[0],2)]),flip(send,bit,total)
def finish2(keep,got,total):
    bit=2
    while keep.shape[0]>1:
        keep,got=split_send(keep+got.astype(F32),bit,total); bit*=2
    return keep[0],got[0]
def on_device(tokens,source_len,target_len,timesteps,cotangent,query_weight,query_bias,key_weight,value_weight,value_bias,
        out_weight,out_bias,attn_gain,attn_shift,up_weight,up_bias,down_weight,down_bias,ffn_gain,ffn_shift,
        stamp_weight,stamp_bias,embed_weight,embed_bias):
    seqs,R,D=tokens.shape
    streams=lax.axis_size("stream"); seq_size=lax.axis_size("seq"); total=seq_size*streams
    s0=lax.axis_index("stream"); flat=lax.axis_index("seq")*streams+s0
    unit=total//GROUPS
    inner=flat%unit; group=flat//unit
    me=group.astype(jnp.int32).reshape(1)
    n=D//GROUPS; shard=D//total; stamp_rows=stamp_weight.shape[0]; FF=up_weight.shape[1]; ff_shard=FF//total
    vecs=(query_bias,value_bias,out_bias,attn_gain,attn_shift,down_bias,ffn_gain,ffn_shift,stamp_bias,embed_bias,up_bias)
    first,second=pack((query_weight,key_weight,value_weight,embed_weight,stamp_weight,out_weight,down_weight,up_weight),vecs)
    def rowwise(x,sizes):
        at=0; out=[]
        for count,size in sizes:
            part=x[:,at:at+count*size].reshape(unit,count,size,x.shape[2])
            out.append(part.transpose(1,0,2,3).reshape(count*unit*size,x.shape[2])); at+=count*size
        return jnp.concatenate(out) if len(out)>1 else out[0]
    def exchange(chunks):
        return [x if c==0 else flip(x,c,total) for c,x in enumerate(chunks)]
    def chunks_of(x): return [lax.dynamic_index_in_dim(x,s0^c,0,keepdims=False) for c in range(streams)]
    order=jnp.asarray(ORDER,jnp.int32)
    source=source_len[s0]; target=target_len[s0]; stamp=timesteps[s0]
    half=R*streams//2
    place=(s0^jnp.arange(streams))*R
    flag=(place>=half).astype(jnp.int32)
    nlive=jnp.clip(jnp.where(flag==1,target-(place-half),source-place),0,R).astype(jnp.int32)
    info=jnp.stack([flag,nlive],1)
    tdim=stamp_rows*total; halfway=tdim//2
    t_ids=(((order^group)[:,None,None]*unit+jnp.arange(unit)[None,:,None])*stamp_rows+jnp.arange(SMALL)[None,None,:])
    valid=(jnp.arange(SMALL)<stamp_rows)[None,None,:]
    t_ids=jnp.where(valid,t_ids,0).reshape(-1)
    rates=jnp.exp(-math.log(10000.0)*(t_ids%halfway).astype(F32)/halfway)
    angle=stamp.astype(F32)*rates
    feats=jnp.where(t_ids<halfway,jnp.sin(angle),jnp.cos(angle))
    feats=jnp.where(jnp.broadcast_to(valid,(GROUPS,unit,SMALL)).reshape(-1),feats,0.0)
    feat=jnp.broadcast_to(feats.astype(BF)[None],(8,feats.shape[0]))
    bits=far_first(unit)
    first=widen(first[None],bits[0],total)
    first,second=sync(first,second)
    second=widen(second[None],bits[0],total)
    for bit in bits[1:]: first=widen(first,bit,total)
    first=rowwise(settle(first,inner,unit),((4,shard),(1,SMALL)))
    cells=chunks_of(tokens)
    first,second,feat,info,*cells=sync(first,second,feat,info,*cells)
    for bit in bits[1:]: second=widen(second,bit,total)
    n1=[first]+[flip(first,g*unit,total) for g in (2,4,6)]
    toks=[cells[0]]+[None]*(streams-1)
    early,late=list(range(2,streams)),[1]
    for c in early: toks[c]=flip(cells[c],c,total)
    n1[1],n1[2],toks[2],second=sync(n1[1],n1[2],toks[2],second)
    second=rowwise(settle(second,inner,unit),((1,shard),(1,ff_shard),(FF//D,shard)))
    for c in late: toks[c]=flip(after(cells[c],second),c,total)
    n2=spread_start(second,unit,total)
    p1=n1+[flip(x,unit,total) for x in n1]
    *cells,_=sync(*chunks_of(cotangent),toks)
    far=[flip(n2[0],unit,total)]
    cots=[cells[0]]+[flip(cells[c],c,total) for c in range(1,streams-1)]
    mixed,inputs,q,k,v,auxk,pre,hid,vec,upb=project(me,info,feat,toks,p1,unit,FF)
    pairs=D//(2*HEAD); parts=(2,pairs-2)
    atts=[];auxq=[]
    def forward(c,q):
        a,x=attn_fwd(q,k,v,auxk,sum(parts[:c]),parts[c]); atts.append(a); auxq.append(x)
    forward(0,q)
    q,n2,far,cots,cells,atts=sync(q,n2,far,cots,cells,atts)
    cut=n+FF//GROUPS
    low=flip(n2[2][:cut],2*unit,total); high=flip(n2[1][cut:],4*unit,total)
    cots.append(flip(cells[streams-1],streams-1,total))
    far+=[flip(n2[1],unit,total),flip(n2[2],unit,total)]
    forward(1,q)
    low,high,far,atts,cots=sync(low,high,far,atts,cots)
    diag=(low,high)
    p2=n2+[diag]+far+[tuple(flip(x,unit,total) for x in diag)]
    cot=jnp.stack(cots)
    output,ga,gatt,auxd,mine2,theirs2,dvec,dupb=sync(*middle(me,info,mixed,cot,atts,vec,upb,p2))
    grads=[]
    per=pairs//3
    def backward(c,q):
        grads.append(attn_bwd(q,k,v,gatt,auxk,auxq[min(c,1)],auxd,c*per,per,c*per-sum(parts[:min(c,1)])))
    got=flip(theirs2,unit,total)
    backs=[output[0],flip(output[1],1,total)]
    backward(0,q)
    got,q,output,backs,grads=sync(got,q,output,backs,grads)
    low,high=sum_diag(mine2,got,cut)
    low=flip(low,2*unit,total); high=flip(high,4*unit,total)
    backs.append(flip(output[2],2,total))
    backward(1,q)
    held=backs.pop()
    low,high,q,output,backs,grads=sync(low,high,q,output,backs,grads)
    fx,fy,held=sync(*sum_near(mine2,got,low,high),held)
    backs.append(held)
    fx=flip(fx,2*unit,total); fy=flip(fy,4*unit,total)
    backs.append(flip(output[3],3,total))
    backward(2,q)
    backs,grads=sync(backs,grads)
    def place(chunks,dtype):
        out=jnp.zeros((seqs,R,D),dtype)
        for c,part in enumerate(chunks):
            out=lax.dynamic_update_index_in_dim(out,part.astype(dtype),s0^c,0)
        return out
    tg,rows4=token_grads(me,info,ga,pre,grads,p1,R)
    tg,rows4,fx,fy=sync(tg,rows4,fx,fy)
    keep2,got2=sum_own(inner,mine2,got,(fx,fy),((1,shard),(1,ff_shard),(FF//D,shard)),unit,total)
    tgs=[tg[0],None,flip(tg[2],2,total)]
    rows4,keep2,tg=sync(rows4,keep2,tg)
    mine1,theirs1=weight_grads(me,inputs,rows4,hid,feat,dvec,dupb,grads,unit,R)
    mine1,theirs1,got2,tg,tgs=sync(mine1,theirs1,got2,tg,tgs)
    got1=flip(theirs1,unit,total)
    tgs[1]=flip(tg[1],1,total)
    blocks=sum_three(mine1,got1)
    blocks,tgs,tg,keep2,got2=sync(blocks,tgs,tg,keep2,got2)
    fx,fy,fd=(flip(x,g*unit,total) for x,g in zip(blocks,(2,4,6)))
    tgs.append(flip(tg[3],3,total))
    keep2,got2=finish2(keep2,got2,total)
    fx,fy,fd,keep2,got2,tgs,backs=sync(fx,fy,fd,keep2,got2,tgs,backs)
    output=place(backs,BF)
    dwo,dwd,dwu=last2(keep2,got2,shard,ff_shard,FF)
    keep1,got1=finish2(*sum_own(inner,mine1,got1,(fx,fy,fd),((4,shard),(1,SMALL)),unit,total),total)
    dwq,dwk,dwv,dwe,dws,bq,bv,bo,ag,as_,bd,fg,fs,bs,be,bu=last1(keep1,got1,shard,stamp_rows,[shard]*10+[ff_shard])
    token_grad=place(tgs,F32)
    return (output,token_grad,dwq,bq,dwk,dwv,bv,dwo,bo,ag,as_,dwu,bu,dwd,bd,fg,fs,dws,bs,dwe,be)

def solution(mesh):
    cells=P("seq","stream",None); per=P("seq"); mat=P(("seq","stream"),None); row=P(("seq","stream"))
    return jax.shard_map(on_device,mesh=mesh,
        in_specs=(cells,per,per,per,cells,mat,row,mat,mat,row,mat,row,row,row,mat,row,mat,row,row,row,mat,row,mat,row),
        out_specs=(cells,cells,mat,row,mat,mat,row,mat,row,row,row,mat,row,mat,row,row,row,mat,row,mat,row),
        check_vma=False)
```

```python
import functools
import math

import jax
import jax.numpy as jnp
from jax import lax
from jax.experimental import pallas as pl
from jax.experimental.pallas import tpu as pltpu
from jax.sharding import PartitionSpec as P

F32=jnp.float32; BF=jnp.bfloat16
NT=(((1,),(1,)),((),())); NN=(((1,),(0,)),((),())); TN=(((0,),(0,)),((),()))
def mm(a,b,dims): return lax.dot_general(a,b,dims,preferred_element_type=F32)
def lanes(shape): return lax.broadcasted_iota(jnp.int32,shape,len(shape)-1)
def split3(x):
    hi=x.astype(BF).astype(F32); r=x-hi
    mid=r.astype(BF).astype(F32); lo=r-mid
    return hi,mid,lo
QB=256
def fwd_kernel(q_ref,k_ref,v_ref,auxk_ref,o_ref,auxq_ref,kaug,vm):
    L=q_ref.shape[0]
    k=k_ref[...]; v=v_ref[...]; ln=lanes(k.shape)
    for e in range(2):
        sel=(ln<64) if e==0 else (ln>=64)
        kaug[e,:,:128]=jnp.where(sel,k,jnp.zeros_like(k))
        kaug[e,:,128:]=auxk_ref[...]
        vm[e]=jnp.where(sel,v,(ln==64*(1-e)).astype(BF))
    ln=lanes((QB,128)); one=jnp.where(ln==64,1.0,0.0).astype(BF)
    steps=[(b,e) for b in range(L//QB) for e in range(2)]
    def score(b,e):
        return mm(jnp.concatenate([q_ref[pl.ds(b*QB,QB),:],one],axis=1),kaug[e],NT)
    s=score(*steps[0]); out=None; aux=None
    for t,(b,e) in enumerate(steps):
        later=score(*steps[t+1]) if t+1<len(steps) else None
        m=jnp.max(s,axis=1,keepdims=True)
        p=jnp.exp(s-m).astype(BF)
        o=mm(p,vm[e],NN)
        l=o[:,64*(1-e):64*(1-e)+1]
        o=jnp.where((ln<64) if e==0 else (ln>=64),o*(1.0/l),0.0)
        hi,mid,lo=split3(-(m+jnp.log(l)))
        if e==0: out=o; aux=jnp.where(ln==64,1.0,0.0)
        else: out=out+o
        aux=jnp.where(ln==3*e,hi,aux); aux=jnp.where(ln==3*e+1,mid,aux); aux=jnp.where(ln==3*e+2,lo,aux)
        if e==1:
            r=pl.ds(b*QB,QB)
            o_ref[r,:]=out.astype(BF); auxq_ref[0,r,:]=aux.astype(BF)
        s=later
def attn_fwd(q,k,v,auxk,p0,np_):
    L=q.shape[0]
    col=lambda: pl.BlockSpec((L,128),lambda p:(0,p0+p))
    return pl.pallas_call(fwd_kernel,grid=(np_,),
      in_specs=[col(),col(),col(),pl.BlockSpec((L,128),lambda p:(0,0))],
      out_specs=[pl.BlockSpec((L,128),lambda p:(0,p)),pl.BlockSpec((1,L,128),lambda p:(p,0,0))],
      out_shape=[jax.ShapeDtypeStruct((L,128*np_),BF),jax.ShapeDtypeStruct((np_,L,128),BF)],
      scratch_shapes=[pltpu.VMEM((2,L,256),BF),pltpu.VMEM((2,L,128),BF)],
      compiler_params=pltpu.CompilerParams(vmem_limit_bytes=60*2**20),
      cost_estimate=pl.CostEstimate(flops=np_*2*L*L*64*4,bytes_accessed=np_*L*128*2*5,transcendentals=np_*2*L*L),
      name="attn_fwd")(q,k,v,auxk)
def bwd_kernel(p0,q_ref,k_ref,v_ref,do_ref,auxk_ref,auxq_ref,auxd_ref,out_ref,kaug,vaug,qa,doa,qm,dom,dk_acc,dv_acc):
    pair=p0+pl.program_id(0)
    L=q_ref.shape[0]
    k=k_ref[...]; v=v_ref[...]; q=q_ref[...]; do=do_ref[...]
    ln=lanes(k.shape); z=jnp.zeros_like(k); auxk=auxk_ref[...]
    qa[:,:128]=q; qa[:,128:]=auxq_ref[0]
    doa[:,:128]=do; doa[:,128:]=auxd_ref[...]
    for e in range(2):
        sel=(ln<64) if e==0 else (ln>=64)
        on=(ln>=3*e)&(ln<3*e+3)
        kaug[e,:,:128]=jnp.where(sel,k,z)
        kaug[e,:,128:]=jnp.where(on,jnp.ones_like(k),auxk)
        vaug[e,:,:128]=jnp.where(sel,v,z)
        b=6*pair+3*e
        vaug[e,:,128:]=jnp.where((ln>=b)&(ln<b+3),jnp.ones_like(k),z)
        qm[e]=jnp.where(sel,q,z)
        dom[e]=jnp.where(sel,do,z)
    for i in range(L//QB):
        r=pl.ds(i*QB,QB)
        dq=None
        for e in range(2):
            p=jnp.exp(mm(kaug[e],qa[r,:],NT))
            dp=mm(vaug[e],doa[r,:],NT)
            ds=(p*dp).astype(BF)
            dv=mm(p.astype(BF),dom[e,r,:],NN)
            dk=mm(ds,qm[e,r,:],NN)
            if i==0 and e==0: dv_acc[...]=dv; dk_acc[...]=dk
            else: dv_acc[...]+=dv; dk_acc[...]+=dk
            d=mm(ds,kaug[e,:,:128],TN)
            dq=d if dq is None else dq+d
        out_ref[0,r,:]=(dq*0.125).astype(BF)
    out_ref[1]=dk_acc[...].astype(BF)
    out_ref[2]=dv_acc[...].astype(BF)
def attn_bwd(q,k,v,do,auxk,auxq,auxd,p0,np_,a0):
    L=q.shape[0]
    col=lambda: pl.BlockSpec((L,128),lambda p:(0,p0+p))
    con=lambda: pl.BlockSpec((L,128),lambda p:(0,0))
    return pl.pallas_call(functools.partial(bwd_kernel,p0),grid=(np_,),
      in_specs=[col(),col(),col(),col(),con(),pl.BlockSpec((1,L,128),lambda p:(a0+p,0,0)),con()],
      out_specs=pl.BlockSpec((3,L,128),lambda p:(0,0,p)),
      out_shape=jax.ShapeDtypeStruct((3,L,128*np_),BF),
      scratch_shapes=[pltpu.VMEM((2,L,256),BF),pltpu.VMEM((2,L,256),BF),pltpu.VMEM((L,256),BF),pltpu.VMEM((L,256),BF),
        pltpu.VMEM((2,L,128),BF),pltpu.VMEM((2,L,128),BF),pltpu.VMEM((L,128),F32),pltpu.VMEM((L,128),F32)],
      compiler_params=pltpu.CompilerParams(vmem_limit_bytes=60*2**20),
      cost_estimate=pl.CostEstimate(flops=np_*2*L*L*64*10,bytes_accessed=np_*L*128*2*9,transcendentals=np_*2*L*L),
      name="attn_bwd")(q,k,v,do,auxk,auxq,auxd)

SMALL=16; Q_B,V_B,OUT_B,ATT_G,ATT_S,DOWN_B,FFN_G,FFN_S,STAMP_B,EMBED_B=range(4,14); UP_B=14
def owner_of(rows,me,unit,width):
    r=lax.shift_right_logical(lax.broadcasted_iota(jnp.int32,(rows,width),0),SMALL.bit_length()-1)
    shift=unit.bit_length()-1
    t=lax.shift_right_logical(r,shift)
    g=jnp.bitwise_xor(jnp.bitwise_or(jnp.bitwise_and(t*2,7),lax.shift_right_logical(t,2)),me)
    return g*unit+jnp.bitwise_and(r,unit-1)
def repeats(width,shard):
    l=lax.broadcasted_iota(jnp.int32,(128,width),0).astype(F32); d=lax.broadcasted_iota(jnp.int32,(128,width),1).astype(F32)
    return (d-shard*jnp.floor((d+0.5)*(1.0/shard))==l).astype(BF)
def owned(owner,shard):
    d=lax.broadcasted_iota(jnp.int32,owner.shape,1)
    return (d>=owner*shard)&(d<owner*shard+shard)
def pack_kernel(*refs):
    *ins,first_ref,second_ref,scr=refs
    wq,wk,wv,we,st,wo,wd,wu=ins[:8]; vecs=ins[8:]
    scr[...]=jnp.zeros_like(scr)
    scr[:st.shape[0],:]=st[...]
    for r,v in enumerate(vecs):
        scr[4+r:5+r,:v.shape[0]]=v[...].reshape(1,-1)
    D=wq.shape[1]
    first_ref[...]=jnp.concatenate([wq[...],wk[...],wv[...],we[...],scr[...]],axis=0).astype(BF)
    up=[wu[:,c*D:(c+1)*D] for c in range(wu.shape[1]//D)]
    second_ref[...]=jnp.concatenate([wo[...],wd[...]]+up,axis=0).astype(BF)
def pack(mats,vecs):
    wq,wk,wv,we,st,wo,wd,wu=mats; n,D=wq.shape
    vm=pl.BlockSpec(memory_space=pltpu.VMEM)
    second=n+wd.shape[0]+n*(wu.shape[1]//D)
    if n%8:
        small=jnp.concatenate([st]+[jnp.zeros((4-st.shape[0],D),F32)]+[jnp.pad(v,(0,D-v.shape[0]))[None] for v in vecs]+[jnp.zeros((SMALL-4-len(vecs),D),F32)])
        up=[wu[:,c*D:(c+1)*D] for c in range(wu.shape[1]//D)]
        return jnp.concatenate([wq,wk,wv,we,small]).astype(BF),jnp.concatenate([wo,wd]+up).astype(BF)
    return pl.pallas_call(pack_kernel,in_specs=[vm]*(8+len(vecs)),out_specs=[vm]*2,
      out_shape=[sds((4*n+SMALL,D),BF),sds((second,D),BF)],scratch_shapes=[pltpu.VMEM((SMALL,D),F32)],compiler_params=pltpu.CompilerParams(vmem_limit_bytes=60*2**20),name="pack")(*mats,*vecs)
ORDER=(0,2,4,6,1,3,5,7)
def rows_at(me,t,n):
    return pl.ds(pl.multiple_of(jnp.bitwise_xor(me,ORDER[t])*n,n),n)
def sds(*a): return jax.ShapeDtypeStruct(*a)
def once(s): return pl.BlockSpec(s.shape,lambda i:(0,)*len(s.shape),pipeline_mode=pl.Buffered(1))
def smem(): return pl.BlockSpec(memory_space=pltpu.SMEM)
def anyw(): return pl.BlockSpec(memory_space=pl.ANY)
def load_weights(me,pieces,base,n,dst,sem):
    return [pltpu.make_async_copy(p.at[pl.ds(base,n),:],dst.at[rows_at(me,t,n),:],sem) for t,p in enumerate(pieces)]
def in_kernel(nt,unit,me_ref,info_ref,feat_ref,*rest):
    toks=rest[:nt]; pieces=rest[nt:nt+8]
    mixed_ref,inp_ref,q_ref,k_ref,v_ref,auxk_ref,pre_ref,hid_ref,vec_ref,upb_ref,tok,wq,wk,wv,we,ws,emb,sems=rest[nt+8:]
    i=pl.program_id(0); me=me_ref[0]
    D=wq.shape[0]; n=D//8; ns=ws.shape[0]//8
    tcp=[pltpu.make_async_copy(t,tok.at[c],sems.at[5+c]) for c,t in enumerate(toks)]
    scp=[pltpu.make_async_copy(p.at[pl.ds(4*n,ns),:],ws.at[pl.ds(t*ns,ns),:],sems.at[0]) for t,p in enumerate(pieces)]
    wcp=[load_weights(me,pieces,w*n,n,dst,sems.at[1+w]) for w,dst in enumerate((wq,wk,wv,we))]
    vec=lambda r: vec_ref[pl.ds(r,1),:]
    @pl.when(i==0)
    def _():
        for c in scp+wcp[3]+tcp[:1]+wcp[0]+wcp[1]+wcp[2]+tcp[1:]: c.start()
        for c in scp: c.wait()
        rows=8*ns; total=8*unit; FF=upb_ref.shape[1]
        lead=ws[:,:128]
        spread=mm(lead,repeats(D,D//total),NN)
        spread=jnp.where(owned(owner_of(rows,me,unit,D),D//total),spread,0.0)
        vec_ref[...]=jnp.sum(spread.reshape(total,SMALL,D),axis=0)
        ups=lead.astype(F32).reshape(total,SMALL,128)[:,UP_B,:].astype(BF)
        ups=mm(ups,repeats(FF,FF//total),NN)
        own=owner_of(rows,me,unit,128).reshape(total,SMALL,128)[:,0,:1]
        upb_ref[...]=jnp.sum(jnp.where(owned(jnp.broadcast_to(own,(total,FF)),FF//total),ups,0.0),axis=0,keepdims=True)
        pre=mm(feat_ref[...],ws[...],NN)+vec(STAMP_B)
        pre_ref[...]=pre
        hid=(pre/(1.0+jnp.exp(-pre))).astype(BF)
        hid_ref[...]=hid
        for c in wcp[3]: c.wait()
        emb[...]=mm(hid,we[...],NN)+vec(EMBED_B)
    for c in range(nt):
        @pl.when(i==c)
        def _(): tcp[c].wait()
    flag=info_ref[i,0].astype(F32); nlive=info_ref[i,1]
    x=tok[i].astype(F32)+flag*emb[pl.ds(0,1),:]
    mixed_ref[...]=x
    xb=x.astype(BF); inp_ref[...]=xb
    R=x.shape[0]
    ln=lanes((R,128)); row=lax.broadcasted_iota(jnp.int32,(R,128),0)
    auxk_ref[...]=jnp.where((ln==64)&(row>=nlive),-1e30,0.0).astype(BF)
    @pl.when(i==0)
    def _():
        for w in range(3):
            for c in wcp[w]: c.wait()
    q=(mm(xb,wq[...],NN)+vec(Q_B)).astype(BF)
    q_ref[...]=(q.astype(F32)*0.125).astype(BF)
    k_ref[...]=mm(xb,wk[...],NN).astype(BF)
    v_ref[...]=(mm(xb,wv[...],NN)+vec(V_B)).astype(BF)
def project(me,info,feat,toks,pieces,unit,FF):
    nt=len(toks); R,D=toks[0].shape; n=D//8; ns=pieces[0].shape[0]-4*n; L=nt*R
    row=lambda w: pl.BlockSpec((R,w),lambda i:(i,0))
    full=lambda a: pl.BlockSpec(a.shape,lambda i:(0,)*a.ndim)
    outs=[sds((L,D),F32)]+[sds((L,D),BF)]*4+[sds((L,128),BF),sds((8,D),F32),sds((8,D),BF),sds((SMALL,D),F32),sds((1,FF),F32)]
    return pl.pallas_call(functools.partial(in_kernel,nt,unit),grid=(nt,),
      in_specs=[smem(),smem(),full(feat)]+[anyw()]*(nt+8),
      out_specs=[row(D)]*5+[row(128)]+[once(o) for o in outs[6:]],
      out_shape=outs,
      scratch_shapes=[pltpu.VMEM((nt,R,D),BF)]+[pltpu.VMEM((D,D),BF)]*4+[pltpu.VMEM((8*ns,D),BF),pltpu.VMEM((8,D),F32),pltpu.SemaphoreType.DMA((5+nt,))],
      compiler_params=pltpu.CompilerParams(vmem_limit_bytes=60*2**20),
      cost_estimate=pl.CostEstimate(flops=2*L*D*D*3,bytes_accessed=20_000_000,transcendentals=0),
      name="project")(me,info,feat,*toks,*pieces)

def spread3(row):
    hi,mid,lo=split3(row)
    r=lax.broadcasted_iota(jnp.int32,(8,row.shape[1]),0)
    return jnp.where(r==0,hi,jnp.where(r==1,mid,jnp.where(r==2,lo,0.0))).astype(BF)
def three(rows):
    r=lax.broadcasted_iota(jnp.int32,rows.shape,0)
    return jnp.where(r<3,jnp.broadcast_to(rows[0:1,:].astype(F32),rows.shape),0.0).astype(BF)
def token_kernel(nc,me_ref,info_ref,ga_ref,pre_ref,*rest):
    grads=rest[:nc]; pieces=rest[nc:nc+8]
    *tg_refs,rows_ref,wq,wk,wv,we,sems=rest[nc+8:]
    i=pl.program_id(0); me=me_ref[0]
    D=wq.shape[0]; n=D//8
    wcp=[load_weights(me,pieces,w*n,n,dst,sems.at[w]) for w,dst in enumerate((wq,wk,wv,we))]
    @pl.when(i==0)
    def _():
        for w in wcp:
            for c in w: c.start()
        rows_ref[...]=jnp.zeros_like(rows_ref)
    g=ga_ref[...]
    for w,dst in enumerate((wq,wk,wv)):
        y=jnp.concatenate([s[w] for s in grads],axis=1)
        if w!=1: rows_ref[pl.ds(w//2,1),:]+=jnp.sum(y.astype(F32),axis=0,keepdims=True)
        @pl.when(i==0)
        def _():
            for c in wcp[w]: c.wait()
        g=g+mm(y,dst[...],NT)
    R=tg_refs[0].shape[0]; per=g.shape[0]//R
    for c in range(per):
        rows_ref[pl.ds(3,1),:]+=info_ref[i*per+c,0].astype(F32)*jnp.sum(g[c*R:(c+1)*R],axis=0,keepdims=True)
    for c,ref in enumerate(tg_refs):
        @pl.when(i==c//per)
        def _(): ref[...]=g[c%per*R:(c%per+1)*R].astype(BF)
    @pl.when(i==pl.num_programs(0)-1)
    def _():
        for c in wcp[3]: c.wait()
        gh=jnp.sum(mm(spread3(rows_ref[pl.ds(3,1),:]),we[...],NT),axis=0,keepdims=True)
        pre=pre_ref[0:1,:]
        sg=1.0/(1.0+jnp.exp(-pre))
        rows_ref[pl.ds(2,1),:]=gh*(sg*(1.0+pre*(1.0-sg)))
STEP=512
def token_grads(me,info,ga,pre,grads,pieces,C):
    L,D=ga.shape; R=max(STEP,C); nt=L//R; nc=len(grads)
    outs=[sds((C,D),BF)]*(L//C)+[sds((8,D),F32)]
    return pl.pallas_call(functools.partial(token_kernel,nc),grid=(nt,),
      in_specs=[smem(),smem(),pl.BlockSpec((R,D),lambda i:(i,0)),pl.BlockSpec((8,D),lambda i:(0,0))]+[pl.BlockSpec((3,R,a.shape[2]),lambda i:(0,i,0)) for a in grads]+[anyw()]*8,
      out_specs=[once(o) for o in outs],
      out_shape=outs,
      scratch_shapes=[pltpu.VMEM((D,D),BF)]*4+[pltpu.SemaphoreType.DMA((4,))],
      compiler_params=pltpu.CompilerParams(vmem_limit_bytes=60*2**20),
      cost_estimate=pl.CostEstimate(flops=2*L*D*D*3,bytes_accessed=15_000_000,transcendentals=0),
      name="token_grads")(me,info,ga,pre,*grads,*pieces)
def weight_kernel(nc,unit,me_ref,inp_ref,rows_ref,hid_ref,feat_ref,dvec_ref,dupb_ref,*rest):
    grads=rest[:nc]
    mine_ref,theirs_ref,acc=rest[nc:]
    i=pl.program_id(0); me=me_ref[0]
    D=inp_ref.shape[1]; n=D//8; rows=feat_ref.shape[1]; ns=rows//8
    def to(t): return mine_ref if t<4 else theirs_ref
    @pl.when(i==0)
    def _():
        acc[:,3*D:]=mm(three(hid_ref[...]),spread3(rows_ref[3:4,:]),TN)
        total=8*unit; FF=dupb_ref.shape[1]
        r=lax.broadcasted_iota(jnp.int32,(SMALL,D),0)
        vec=dvec_ref[...]
        for at,row in ((Q_B,0),(V_B,1),(STAMP_B,2),(EMBED_B,3)):
            vec=jnp.where(r==at,rows_ref[row:row+1,:],vec)
        vec=jnp.broadcast_to(vec[None],(total,SMALL,D)).reshape(rows,D)
        vec=jnp.where(owned(owner_of(rows,me,unit,D),D//total),vec,0.0).astype(BF)
        vec=mm(vec,repeats(D,D//total),NT)
        own=owner_of(rows,me,unit,128).reshape(total,SMALL,128)[:,0,:1]
        ups=jnp.where(owned(jnp.broadcast_to(own,(total,FF)),FF//total),dupb_ref[...],0.0).astype(BF)
        ups=mm(ups,repeats(FF,FF//total),NT)
        line=jnp.bitwise_and(lax.broadcasted_iota(jnp.int32,(rows,128),0),SMALL-1)
        ups=jnp.broadcast_to(ups[:,None,:],(total,SMALL,128)).reshape(rows,128)
        vec=jnp.where(line==UP_B,ups,jnp.where((line>=4)&(line<UP_B),vec,0.0))
        small=mm(three(feat_ref[...]),spread3(rows_ref[2:3,:]),TN)
        small=small+jnp.concatenate([vec,jnp.zeros((rows,D-128),F32)],axis=1)
        small=small.astype(BF)
        for t in range(8): to(t)[t%4,4*n:,:]=small[t*ns:(t+1)*ns]
    part=mm(inp_ref[...],jnp.concatenate([s[w] for w in range(3) for s in grads],axis=1),TN)
    @pl.when(i==0)
    def _(): acc[:,:3*D]=part
    @pl.when(i>0)
    def _(): acc[:,:3*D]+=part
    @pl.when(i==pl.num_programs(0)-1)
    def _():
        for t in range(8):
            for w in range(4): to(t)[t%4,w*n:(w+1)*n,:]=acc[rows_at(me,t,n),w*D:(w+1)*D].astype(BF)
def weight_grads(me,inp,rows,hid,feat,dvec,dupb,grads,unit):
    L,D=inp.shape; R=STEP; n=D//8; nc=len(grads)
    outs=[sds((4,4*n+feat.shape[1]//8,D),BF)]*2
    full=lambda a: pl.BlockSpec(a.shape,lambda i:(0,)*a.ndim)
    return pl.pallas_call(functools.partial(weight_kernel,nc,unit),grid=(L//R,),
      in_specs=[smem(),pl.BlockSpec((R,D),lambda i:(i,0))]+[full(a) for a in (rows,hid,feat,dvec,dupb)]+[pl.BlockSpec((3,R,a.shape[2]),lambda i:(0,i,0)) for a in grads],
      out_specs=[once(o) for o in outs],out_shape=outs,
      scratch_shapes=[pltpu.VMEM((D,4*D),F32)],
      compiler_params=pltpu.CompilerParams(vmem_limit_bytes=60*2**20),
      cost_estimate=pl.CostEstimate(flops=2*L*D*D*3,bytes_accessed=12_000_000,transcendentals=0),
      name="weight_grads")(me,inp,rows,hid,feat,dvec,dupb,*grads)
LB=384
def take(k,R): return pl.BlockSpec((1,R,LB),lambda i:(k,0,i))
def flat(R): return pl.BlockSpec((R,LB),lambda i:(0,i))
def total_of(refs):
    out=refs[0].astype(F32)
    for r in refs[1:]: out=out+r.astype(F32)
    return out
def three_kernel(a1,b1,a2,b2,a3,b3,o1,o2,o3):
    for a,b,o in ((a1,b1,o1),(a2,b2,o2),(a3,b3,o3)): o[...]=total_of((a[0],b[0])).astype(BF)
def sum_three(mine,got):
    _,R,D=mine.shape
    return pl.pallas_call(three_kernel,grid=(D//LB,),in_specs=[take(1,R)]*2+[take(2,R)]*2+[take(3,R)]*2,
      out_specs=[flat(R)]*3,out_shape=[sds((R,D),BF)]*3,compiler_params=pltpu.CompilerParams(vmem_limit_bytes=60*2**20),name="sum_three")(mine,got,mine,got,mine,got)
def own_kernel(sizes,unit,nx,inner_ref,a,b,*rest):
    more=rest[:nx]; keep,send,scr=rest[nx:]
    inner=inner_ref[0]
    scr[...]=total_of((a[0],b[0])+tuple(x[...] for x in more))
    for j in range(unit):
        k=jnp.bitwise_xor(inner,j); at=0; out=0
        for count,size in sizes:
            for c in range(count):
                x=scr[pl.ds(pl.multiple_of(at+k*size,8),size),:]
                if j%2: send[j//2,out:out+size,:]=x.astype(BF)
                else: keep[j//2,out:out+size,:]=x
                at+=unit*size; out+=size
def sum_own(inner,mine,got,more,sizes,unit):
    _,R,D=mine.shape; rows=R//unit
    if any(size%8 for _,size in sizes):
        x=mine[0].astype(F32)+got[0].astype(F32)+sum(m.astype(F32) for m in more); at=0; parts=[]
        for count,size in sizes:
            for c in range(count):
                parts.append(x[at:at+unit*size].reshape(unit,size,D)); at+=unit*size
        x=in_order(jnp.concatenate(parts,1),inner)
        return jnp.stack([x[j] for j in range(0,unit,2)]),jnp.stack([x[j] for j in range(1,unit,2)]).astype(BF)
    blk=pl.BlockSpec((unit//2,rows,LB),lambda i:(0,0,i))
    keep,send=pl.pallas_call(functools.partial(own_kernel,sizes,unit,len(more)),grid=(D//LB,),
      in_specs=[smem()]+[take(0,R)]*2+[flat(R)]*len(more),out_specs=[blk]*2,
      out_shape=[sds((unit//2,rows,D),F32),sds((unit//2,rows,D),BF)],scratch_shapes=[pltpu.VMEM((R,LB),F32)],compiler_params=pltpu.CompilerParams(vmem_limit_bytes=60*2**20),name="sum_own")(inner.reshape(1).astype(jnp.int32),mine,got,*more)
    return keep,send
def last1_kernel(keep_ref,got_ref,*outs):
    x=keep_ref[...]+got_ref[...].astype(F32)
    *mats,st=outs[:5]; n=mats[0].shape[0]
    for w,o in enumerate(mats): o[...]=x[w*n:(w+1)*n]
    st[...]=x[4*n:4*n+st.shape[0]]
    for r,o in enumerate(outs[5:]):
        o[...]=x[4*n+4+r:4*n+5+r,:o.shape[0]].reshape(o.shape)
def last1(keep,got,n,stamp_rows,sizes):
    D=keep.shape[1]
    vm=pl.BlockSpec(memory_space=pltpu.VMEM)
    outs=[sds((n,D),F32)]*4+[sds((stamp_rows,D),F32)]+[sds((k,),F32) for k in sizes]
    if n%8:
        x=keep+got.astype(F32)
        return [x[w*n:(w+1)*n] for w in range(4)]+[x[4*n:4*n+stamp_rows]]+[x[4*n+4+r,:k] for r,k in enumerate(sizes)]
    return pl.pallas_call(last1_kernel,in_specs=[vm]*2,out_specs=[vm]*len(outs),out_shape=outs,compiler_params=pltpu.CompilerParams(vmem_limit_bytes=60*2**20),name="last_attn")(keep,got)
def last2_kernel(keep_ref,got_ref,wo,wd,wu):
    x=keep_ref[...]+got_ref[...].astype(F32); n,D=wo.shape; m=wd.shape[0]
    wo[...]=x[:n]; wd[...]=x[n:n+m]
    for c in range(wu.shape[1]//D): wu[:,c*D:(c+1)*D]=x[n+m+c*n:n+m+(c+1)*n]
def last2(keep,got,n,m,FF):
    D=keep.shape[1]
    vm=pl.BlockSpec(memory_space=pltpu.VMEM)
    outs=[sds((n,D),F32),sds((m,D),F32),sds((n,FF),F32)]
    if n%8:
        x=keep+got.astype(F32)
        return x[:n],x[n:n+m],jnp.concatenate([x[n+m+c*n:n+m+(c+1)*n] for c in range(FF//D)],1)
    return pl.pallas_call(last2_kernel,in_specs=[vm]*2,out_specs=[vm]*3,out_shape=outs,compiler_params=pltpu.CompilerParams(vmem_limit_bytes=60*2**20),name="last_ffn")(keep,got)

INV_SQRT2=0.7071067811865476; INV_SQRT2PI=0.3989422804014327
HEAD=64
RB=256; FC=768
def norm_stats(x):
    mu=jnp.mean(x,axis=1,keepdims=True); c=x-mu
    r=lax.rsqrt(jnp.mean(c*c,axis=1,keepdims=True)+1e-5)
    return c*r,r
def norm_back(e,n,r):
    return r*(e-jnp.mean(e,axis=1,keepdims=True)-n*jnp.mean(e*n,axis=1,keepdims=True))
def colsum(x): return jnp.sum(x,axis=0,keepdims=True)
def mid_kernel(nblk,me_ref,info_ref,mix_ref,cot_ref,att_refs,vec_ref,upb_ref,pieces,
        out_ref,gas_ref,gatt_ref,auxd_ref,mine_ref,theirs_ref,dvec_ref,dupb_ref,
        wo,wd,wu,awo,awd,awu,gel,dgel,sems):
    i=pl.program_id(0); nb=pl.num_programs(0)
    D=wo.shape[0]; FF=wd.shape[0]; ro=D//nblk; rd=FF//nblk
    me=me_ref[0]
    lower=[p[0] if isinstance(p,tuple) else p for p in pieces]
    upper=[(p[1],0) if isinstance(p,tuple) else (p,ro+rd) for p in pieces]
    cps=[load_weights(me,lower,0,ro,wo,sems.at[0]),
        [pltpu.make_async_copy(p.at[pl.ds(at+b*ro,ro),:],wu.at[rows_at(me,t,ro),pl.ds(b*D,D)],sems.at[1])
            for b in range(FF//D) for t,(p,at) in enumerate(upper)],
        load_weights(me,lower,ro,rd,wd,sems.at[2])]
    def wait(which):
        @pl.when(i==0)
        def _():
            for c in cps[which]: c.wait()
    @pl.when(i==0)
    def _():
        for w in cps:
            for c in w: c.start()
        awo[...]=jnp.zeros_like(awo); awd[...]=jnp.zeros_like(awd); awu[...]=jnp.zeros_like(awu)
        dvec_ref[...]=jnp.zeros_like(dvec_ref); dupb_ref[...]=jnp.zeros_like(dupb_ref)
    vec=lambda r: vec_ref[pl.ds(r,1),:].astype(F32)
    nlive=info_ref[i,1]
    x0=mix_ref[...]
    live=(lax.broadcasted_iota(jnp.int32,(RB,1),0)<nlive).astype(F32)
    wait(0)
    att=jnp.concatenate([a[...] for a in att_refs],axis=1)
    asum=x0+(mm(att,wo[...],NN)+vec(OUT_B))
    n1,r1=norm_stats(asum)
    normed=n1*vec(ATT_G)+vec(ATT_S)
    hid=normed.astype(BF)
    wait(1); wait(2)
    down=None
    for f in range(FF//FC):
        c=slice(f*FC,(f+1)*FC)
        u=mm(hid,wu[:,c],NN)+upb_ref[:,c].astype(F32)
        ph=0.5+0.5*lax.erf(u*INV_SQRT2)
        pd=jnp.exp(u*u*-0.5)*INV_SQRT2PI
        g=(u*ph).astype(BF)
        gel[:,c]=g
        dgel[:,c]=ph+u*pd
        t=mm(g,wd[c,:],NN)
        down=t if down is None else down+t
    fsum=normed+(down+vec(DOWN_B))
    n2,r2=norm_stats(fsum)
    g2=vec(FFN_G)
    out_ref[0]=((n2*g2+vec(FFN_S))*live).astype(BF)
    og=cot_ref[0].astype(F32)*live
    dvec_ref[pl.ds(FFN_G,1),:]+=colsum(og*n2)
    dvec_ref[pl.ds(FFN_S,1),:]+=colsum(og)
    gf=norm_back(og*g2,n2,r2)
    gd=gf.astype(BF)
    dvec_ref[pl.ds(DOWN_B,1),:]+=colsum(gd.astype(F32))
    gn=gf
    for f in range(FF//FC):
        c=slice(f*FC,(f+1)*FC)
        gu=(mm(gd,wd[c,:],NT)*dgel[:,c]).astype(BF)
        dupb_ref[:,c]+=colsum(gu.astype(F32))
        awd[c,:]+=mm(gel[:,c],gd,TN)
        awu[:,c]+=mm(hid,gu,TN)
        gn=gn+mm(gu,wu[:,c],NT)
    dvec_ref[pl.ds(ATT_G,1),:]+=colsum(gn*n1)
    dvec_ref[pl.ds(ATT_S,1),:]+=colsum(gn)
    ga=norm_back(gn*vec(ATT_G),n1,r1)
    gas_ref[...]=ga
    gb=ga.astype(BF)
    dvec_ref[pl.ds(OUT_B,1),:]+=colsum(gb.astype(F32))
    awo[...]+=mm(att,gb,TN)
    gatt=mm(gb,wo[...],NT).astype(BF)
    gatt_ref[...]=gatt
    pr=-(gatt.astype(F32)*att.astype(F32))
    hi,mid,lo=split3(pr)
    hrow=lax.broadcasted_iota(jnp.int32,(D,128),0)//64
    hcol=lax.broadcasted_iota(jnp.int32,(D,128),1)
    ind=((hcol>=3*hrow)&(hcol<3*hrow+3)).astype(BF)
    dl=mm(hi.astype(BF),ind,NN)+mm(mid.astype(BF),ind,NN)
    h2,m2,l2=split3(dl)
    ln=lanes(dl.shape)%3
    auxd_ref[...]=jnp.where(ln==0,h2,jnp.where(ln==1,m2,l2)).astype(BF)
    @pl.when(i==nb-1)
    def _():
        def send(src,at,n):
            cps=[pltpu.make_async_copy(src.at[rows_at(me,t,n),:],(mine_ref if t<4 else theirs_ref).at[t%4,pl.ds(at,n),:],sems.at[3]) for t in range(8)]
            for c in cps: c.start()
            return cps
        wo[...]=awo[...].astype(BF)
        out=send(wo,0,ro)
        wd[...]=awd[...].astype(BF)
        out+=send(wd,ro,rd)
        wu[...]=awu[...].astype(BF)
        for b in range(FF//D): out+=send(wu.at[:,pl.ds(b*D,D)],ro+rd+b*ro,ro)
        for c in out: c.wait()
def middle(me,info,mixed,cot,atts,vec,upb,pieces):
    nblk=8; L,D=mixed.shape; FF=upb.shape[1]; ro=D//8; rd=FF//8
    nb=L//RB; na=len(atts)
    flat_pieces=jax.tree.leaves(pieces)
    def kern(me_ref,info_ref,mix_ref,cot_ref,*rest):
        att=rest[:na]; rest=rest[na:]
        given=iter(rest[2:2+len(flat_pieces)])
        blocks=[(next(given),next(given)) if isinstance(p,tuple) else next(given) for p in pieces]
        mid_kernel(nblk,me_ref,info_ref,mix_ref,cot_ref,att,rest[0],rest[1],blocks,*rest[2+len(flat_pieces):])
    full=lambda a: pl.BlockSpec(a.shape,lambda i:(0,)*a.ndim)
    blk=pl.BlockSpec((1,RB,D),lambda i:(i,0,0)); row=pl.BlockSpec((RB,D),lambda i:(i,0))
    outs=[sds((nb,RB,D),BF),sds((L,D),F32),sds((L,D),BF),sds((L,128),BF)]+[sds((4,)+pieces[0].shape,BF)]*2+[sds((16,D),F32),sds((1,FF),F32)]
    return pl.pallas_call(kern,grid=(nb,),
      in_specs=[smem(),smem(),row,blk]+[pl.BlockSpec((RB,a.shape[1]),lambda i:(i,0)) for a in atts]+[full(vec),full(upb)]+[anyw()]*len(flat_pieces),
      out_specs=[blk,row,row,pl.BlockSpec((RB,128),lambda i:(i,0)),anyw(),anyw()]+[once(s) for s in outs[6:]],
      out_shape=outs,
      scratch_shapes=[pltpu.VMEM((D,D),BF),pltpu.VMEM((FF,D),BF),pltpu.VMEM((D,FF),BF),
        pltpu.VMEM((D,D),F32),pltpu.VMEM((FF,D),F32),pltpu.VMEM((D,FF),F32),
        pltpu.VMEM((RB,FF),BF),pltpu.VMEM((RB,FF),F32),pltpu.SemaphoreType.DMA((4,))],
      compiler_params=pltpu.CompilerParams(vmem_limit_bytes=61*2**20),
      cost_estimate=pl.CostEstimate(flops=2*L*D*(3*D+6*FF),bytes_accessed=60_000_000,transcendentals=2*L*FF),
      name="middle")(me,info,mixed,cot,*atts,vec,upb,*flat_pieces)

GROUPS=8
AXES=("seq","stream")
def flip(x,mask,total):
    return lax.ppermute(x,AXES,[(i,i^mask) for i in range(total)])
def far_first(count):
    bits=[]; bit=count//2
    while bit: bits.append(bit); bit//=2
    return bits
def widen(x,bit,total): return jnp.concatenate([x,flip(x,bit,total)])
def settle(x,inner,count):
    ids=[0]
    for bit in far_first(count): ids=ids+[i^bit for i in ids]
    return in_order(jnp.stack([x[ids.index(k)] for k in range(count)]),inner)
def in_order(x,index):
    n=x.shape[0]; bit=1
    while bit<n:
        turned=jnp.concatenate([x[k^bit][None] for k in range(n)])
        x=jnp.where((index&bit)!=0,turned,x); bit*=2
    return x
def after(x,*deps):
    return lax.optimization_barrier((x,)+deps)[0]
def sync(*xs): return lax.optimization_barrier(xs)
def spread_start(own,unit,total):
    across=lambda x,g: flip(x,g*unit,total)
    return [own,across(own,2),across(own,4)]
def split_send(x,bit,total):
    send=jnp.stack([x[j] for j in range(1,x.shape[0],2)]).astype(BF)
    return jnp.stack([x[j] for j in range(0,x.shape[0],2)]),flip(send,bit,total)
def finish2(keep,got,total):
    bit=2
    while keep.shape[0]>1:
        keep,got=split_send(keep+got.astype(F32),bit,total); bit*=2
    return keep[0],got[0]
def on_device(tokens,source_len,target_len,timesteps,cotangent,query_weight,query_bias,key_weight,value_weight,value_bias,
        out_weight,out_bias,attn_gain,attn_shift,up_weight,up_bias,down_weight,down_bias,ffn_gain,ffn_shift,
        stamp_weight,stamp_bias,embed_weight,embed_bias):
    seqs,R,D=tokens.shape
    streams=lax.axis_size("stream"); seq_size=lax.axis_size("seq"); total=seq_size*streams
    s0=lax.axis_index("stream"); flat=lax.axis_index("seq")*streams+s0
    unit=total//GROUPS
    inner=flat%unit; group=flat//unit
    me=group.astype(jnp.int32).reshape(1)
    n=D//GROUPS; shard=D//total; stamp_rows=stamp_weight.shape[0]; FF=up_weight.shape[1]; ff_shard=FF//total
    vecs=(query_bias,value_bias,out_bias,attn_gain,attn_shift,down_bias,ffn_gain,ffn_shift,stamp_bias,embed_bias,up_bias)
    first,second=pack((query_weight,key_weight,value_weight,embed_weight,stamp_weight,out_weight,down_weight,up_weight),vecs)
    def rowwise(x,sizes):
        at=0; out=[]
        for count,size in sizes:
            part=x[:,at:at+count*size].reshape(unit,count,size,x.shape[2])
            out.append(part.transpose(1,0,2,3).reshape(count*unit*size,x.shape[2])); at+=count*size
        return jnp.concatenate(out) if len(out)>1 else out[0]
    def exchange(chunks):
        return [x if c==0 else flip(x,c,total) for c,x in enumerate(chunks)]
    def chunks_of(x): return [lax.dynamic_index_in_dim(x,s0^c,0,keepdims=False) for c in range(streams)]
    order=jnp.asarray(ORDER,jnp.int32)
    source=source_len[s0]; target=target_len[s0]; stamp=timesteps[s0]
    half=R*streams//2
    place=(s0^jnp.arange(streams))*R
    flag=(place>=half).astype(jnp.int32)
    nlive=jnp.clip(jnp.where(flag==1,target-(place-half),source-place),0,R).astype(jnp.int32)
    info=jnp.stack([flag,nlive],1)
    tdim=stamp_rows*total; halfway=tdim//2
    t_ids=(((order^group)[:,None,None]*unit+jnp.arange(unit)[None,:,None])*stamp_rows+jnp.arange(SMALL)[None,None,:])
    valid=(jnp.arange(SMALL)<stamp_rows)[None,None,:]
    t_ids=jnp.where(valid,t_ids,0).reshape(-1)
    rates=jnp.exp(-math.log(10000.0)*(t_ids%halfway).astype(F32)/halfway)
    angle=stamp.astype(F32)*rates
    feats=jnp.where(t_ids<halfway,jnp.sin(angle),jnp.cos(angle))
    feats=jnp.where(jnp.broadcast_to(valid,(GROUPS,unit,SMALL)).reshape(-1),feats,0.0)
    feat=jnp.broadcast_to(feats.astype(BF)[None],(8,feats.shape[0]))
    bits=far_first(unit)
    first=widen(first[None],bits[0],total)
    first,second=sync(first,second)
    second=widen(second[None],bits[0],total)
    for bit in bits[1:]: first=widen(first,bit,total)
    first=rowwise(settle(first,inner,unit),((4,shard),(1,SMALL)))
    cells=chunks_of(tokens)
    first,second,feat,info,*cells=sync(first,second,feat,info,*cells)
    for bit in bits[1:]: second=widen(second,bit,total)
    n1=[first]+[flip(first,g*unit,total) for g in (2,4,6)]
    toks=[cells[0]]+[None]*(streams-1)
    early,late=list(range(2,streams)),[1]
    for c in early: toks[c]=flip(cells[c],c,total)
    n1[1],n1[2],toks[2],second=sync(n1[1],n1[2],toks[2],second)
    second=rowwise(settle(second,inner,unit),((1,shard),(1,ff_shard),(FF//D,shard)))
    for c in late: toks[c]=flip(after(cells[c],second),c,total)
    n2=spread_start(second,unit,total)
    p1=n1+[flip(x,unit,total) for x in n1]
    *cells,_=sync(*chunks_of(cotangent),toks)
    far=[flip(n2[0],unit,total)]
    cots=[cells[0]]+[flip(cells[c],c,total) for c in range(1,streams-1)]
    mixed,inputs,q,k,v,auxk,pre,hid,vec,upb=project(me,info,feat,toks,p1,unit,FF)
    pairs=D//(2*HEAD); parts=(2,pairs-2)
    atts=[];auxq=[]
    def forward(c,q):
        a,x=attn_fwd(q,k,v,auxk,sum(parts[:c]),parts[c]); atts.append(a); auxq.append(x)
    forward(0,q)
    q,n2,far,cots,cells,atts=sync(q,n2,far,cots,cells,atts)
    cut=n+FF//GROUPS
    low=flip(n2[2][:cut],2*unit,total); high=flip(n2[1][cut:],4*unit,total)
    cots.append(flip(cells[streams-1],streams-1,total))
    far+=[flip(n2[1],unit,total),flip(n2[2],unit,total)]
    forward(1,q)
    low,high,far,atts,cots=sync(low,high,far,atts,cots)
    diag=(low,high)
    p2=n2+[diag]+far+[tuple(flip(x,unit,total) for x in diag)]
    cot=jnp.stack(cots)
    output,ga,gatt,auxd,mine2,theirs2,dvec,dupb=sync(*middle(me,info,mixed,cot,atts,vec,upb,p2))
    grads=[]
    def backward(c,q):
        grads.append(attn_bwd(q,k,v,gatt,auxk,auxq[c],auxd,sum(parts[:c]),parts[c],0))
    got=flip(theirs2,unit,total)
    backs=[output[0],flip(output[1],1,total)]
    backward(0,q)
    got,q,output,backs,grads=sync(got,q,output,backs,grads)
    fx,fy,fd=(flip(x,g*unit,total) for x,g in zip(sum_three(mine2,got),(2,4,6)))
    backs+=[flip(output[c],c,total) for c in range(2,streams)]
    backward(1,q)
    def place(chunks,dtype):
        out=jnp.zeros((seqs,R,D),dtype)
        for c,part in enumerate(chunks):
            out=lax.dynamic_update_index_in_dim(out,part.astype(dtype),s0^c,0)
        return out
    *tg,rows4=token_grads(me,info,ga,pre,grads,p1,R)
    tg,rows4,backs=sync(tg,rows4,backs)
    held=[flip(tg[c],c,total) for c in range(1,streams-1)]
    mine1,theirs1=weight_grads(me,inputs,rows4,hid,feat,dvec,dupb,grads,unit)
    mine1,theirs1,fx,fy,fd=sync(mine1,theirs1,fx,fy,fd)
    keep2,send2=sum_own(inner,mine2,got,(fx,fy,fd),((1,shard),(1,ff_shard),(FF//D,shard)),unit)
    keep2,send2,theirs1,held,tg=sync(keep2,send2,theirs1,held,tg)
    got2=flip(send2,1,total)
    got1=flip(theirs1,unit,total)
    tgs=[tg[0]]+held+[flip(tg[streams-1],streams-1,total)]
    blocks=sum_three(mine1,got1)
    fx,fy,fd=(flip(x,g*unit,total) for x,g in zip(blocks,(2,4,6)))
    keep2,got2=finish2(keep2,got2,total)
    fx,fy,fd,keep2,got2,tgs=sync(fx,fy,fd,keep2,got2,tgs)
    output=place(backs,BF)
    dwo,dwd,dwu=last2(keep2,got2,shard,ff_shard,FF)
    keep1,send1=sum_own(inner,mine1,got1,(fx,fy,fd),((4,shard),(1,SMALL)),unit)
    keep1,got1=finish2(keep1,flip(send1,1,total),total)
    dwq,dwk,dwv,dwe,dws,bq,bv,bo,ag,as_,bd,fg,fs,bs,be,bu=last1(keep1,got1,shard,stamp_rows,[shard]*10+[ff_shard])
    token_grad=place(tgs,F32)
    return (output,token_grad,dwq,bq,dwk,dwv,bv,dwo,bo,ag,as_,dwu,bu,dwd,bd,fg,fs,dws,bs,dwe,be)

def solution(mesh):
    cells=P("seq","stream",None); per=P("seq"); mat=P(("seq","stream"),None); row=P(("seq","stream"))
    return jax.shard_map(on_device,mesh=mesh,
        in_specs=(cells,per,per,per,cells,mat,row,mat,mat,row,mat,row,row,row,mat,row,mat,row,row,row,mat,row,mat,row),
        out_specs=(cells,cells,mat,row,mat,mat,row,mat,row,row,row,mat,row,mat,row,row,row,mat,row,mat,row),
        check_vma=False)
```

```python
import functools
import math

import jax
import jax.numpy as jnp
from jax import lax
from jax.experimental import pallas as pl
from jax.experimental.pallas import tpu as pltpu
from jax.sharding import PartitionSpec as P

F32=jnp.float32; BF=jnp.bfloat16
NT=(((1,),(1,)),((),())); NN=(((1,),(0,)),((),())); TN=(((0,),(0,)),((),()))
def mm(a,b,dims): return lax.dot_general(a,b,dims,preferred_element_type=F32)
def lanes(shape): return lax.broadcasted_iota(jnp.int32,shape,len(shape)-1)
def split3(x):
    hi=x.astype(BF).astype(F32); r=x-hi
    mid=r.astype(BF).astype(F32); lo=r-mid
    return hi,mid,lo
QB=256
def fwd_kernel(q_ref,k_ref,v_ref,auxk_ref,o_ref,auxq_ref,kaug,vm):
    L=q_ref.shape[0]
    k=k_ref[...]; v=v_ref[...]; ln=lanes(k.shape)
    for e in range(2):
        sel=(ln<64) if e==0 else (ln>=64)
        kaug[e,:,:128]=jnp.where(sel,k,jnp.zeros_like(k))
        kaug[e,:,128:]=auxk_ref[...]
        vm[e]=jnp.where(sel,v,(ln==64*(1-e)).astype(BF))
    ln=lanes((QB,128)); one=jnp.where(ln==64,1.0,0.0).astype(BF)
    steps=[(b,e) for b in range(L//QB) for e in range(2)]
    def score(b,e):
        return mm(jnp.concatenate([q_ref[pl.ds(b*QB,QB),:],one],axis=1),kaug[e],NT)
    s=score(*steps[0]); out=None; aux=None
    for t,(b,e) in enumerate(steps):
        later=score(*steps[t+1]) if t+1<len(steps) else None
        m=jnp.max(s,axis=1,keepdims=True)
        p=jnp.exp(s-m).astype(BF)
        o=mm(p,vm[e],NN)
        l=o[:,64*(1-e):64*(1-e)+1]
        o=jnp.where((ln<64) if e==0 else (ln>=64),o*(1.0/l),0.0)
        hi,mid,lo=split3(-(m+jnp.log(l)))
        if e==0: out=o; aux=jnp.where(ln==64,1.0,0.0)
        else: out=out+o
        aux=jnp.where(ln==3*e,hi,aux); aux=jnp.where(ln==3*e+1,mid,aux); aux=jnp.where(ln==3*e+2,lo,aux)
        if e==1:
            r=pl.ds(b*QB,QB)
            o_ref[r,:]=out.astype(BF); auxq_ref[0,r,:]=aux.astype(BF)
        s=later
def attn_fwd(q,k,v,auxk,p0,np_):
    L=q.shape[0]
    col=lambda: pl.BlockSpec((L,128),lambda p:(0,p0+p))
    return pl.pallas_call(fwd_kernel,grid=(np_,),
      in_specs=[col(),col(),col(),pl.BlockSpec((L,128),lambda p:(0,0))],
      out_specs=[pl.BlockSpec((L,128),lambda p:(0,p)),pl.BlockSpec((1,L,128),lambda p:(p,0,0))],
      out_shape=[jax.ShapeDtypeStruct((L,128*np_),BF),jax.ShapeDtypeStruct((np_,L,128),BF)],
      scratch_shapes=[pltpu.VMEM((2,L,256),BF),pltpu.VMEM((2,L,128),BF)],
      compiler_params=pltpu.CompilerParams(vmem_limit_bytes=60*2**20),
      cost_estimate=pl.CostEstimate(flops=np_*2*L*L*64*4,bytes_accessed=np_*L*128*2*5,transcendentals=np_*2*L*L),
      name="attn_fwd")(q,k,v,auxk)
def bwd_pair(p0,q_ref,k_ref,v_ref,do_ref,auxk_ref,auxq_ref,auxd_ref,out_ref,kaug,vaug,qa,doa,qm,dom,dk_acc,dv_acc):
    pair=p0+pl.program_id(0)
    L=q_ref.shape[0]
    k=k_ref[...]; v=v_ref[...]; q=q_ref[...]; do=do_ref[...]
    ln=lanes(k.shape); z=jnp.zeros_like(k); auxk=auxk_ref[...]
    qa[:,:128]=q; qa[:,128:]=auxq_ref[0]
    doa[:,:128]=do; doa[:,128:]=auxd_ref[...]
    for e in range(2):
        sel=(ln<64) if e==0 else (ln>=64)
        on=(ln>=3*e)&(ln<3*e+3)
        kaug[e,:,:128]=jnp.where(sel,k,z)
        kaug[e,:,128:]=jnp.where(on,jnp.ones_like(k),auxk)
        vaug[e,:,:128]=jnp.where(sel,v,z)
        b=6*pair+3*e
        vaug[e,:,128:]=jnp.where((ln>=b)&(ln<b+3),jnp.ones_like(k),z)
        qm[e]=jnp.where(sel,q,z)
        dom[e]=jnp.where(sel,do,z)
    for i in range(L//QB):
        r=pl.ds(i*QB,QB)
        dq=None
        for e in range(2):
            p=jnp.exp(mm(kaug[e],qa[r,:],NT))
            dp=mm(vaug[e],doa[r,:],NT)
            ds=(p*dp).astype(BF)
            dv=mm(p.astype(BF),dom[e,r,:],NN)
            dk=mm(ds,qm[e,r,:],NN)
            if i==0 and e==0: dv_acc[...]=dv; dk_acc[...]=dk
            else: dv_acc[...]+=dv; dk_acc[...]+=dk
            d=mm(ds,kaug[e,:,:128],TN)
            dq=d if dq is None else dq+d
        out_ref[0,r,:]=(dq*0.125).astype(BF)
    out_ref[1]=dk_acc[...].astype(BF)
    out_ref[2]=dv_acc[...].astype(BF)
def bwd_specs(q,k,v,do,auxk,auxq,auxd,p0,a0):
    L=q.shape[0]
    col=lambda: pl.BlockSpec((L,128),lambda p:(0,p0+p))
    con=lambda: pl.BlockSpec((L,128),lambda p:(0,0))
    return ([col(),col(),col(),col(),con(),pl.BlockSpec((1,L,128),lambda p:(a0+p,0,0)),con()],
      [pltpu.VMEM((2,L,256),BF),pltpu.VMEM((2,L,256),BF),pltpu.VMEM((L,256),BF),pltpu.VMEM((L,256),BF),
        pltpu.VMEM((2,L,128),BF),pltpu.VMEM((2,L,128),BF),pltpu.VMEM((L,128),F32),pltpu.VMEM((L,128),F32)])
def bwd_cost(L,np_): return pl.CostEstimate(flops=np_*2*L*L*64*10,bytes_accessed=np_*L*128*2*9,transcendentals=np_*2*L*L)
def attn_bwd(q,k,v,do,auxk,auxq,auxd,p0,np_,a0):
    L=q.shape[0]
    ins,scratch=bwd_specs(q,k,v,do,auxk,auxq,auxd,p0,a0)
    return pl.pallas_call(functools.partial(bwd_pair,p0),grid=(np_,),in_specs=ins,
      out_specs=pl.BlockSpec((3,L,128),lambda p:(0,0,p)),
      out_shape=jax.ShapeDtypeStruct((3,L,128*np_),BF),scratch_shapes=scratch,
      compiler_params=pltpu.CompilerParams(vmem_limit_bytes=60*2**20),
      cost_estimate=bwd_cost(L,np_),
      name="attn_bwd")(q,k,v,do,auxk,auxq,auxd)

SMALL=16; Q_B,V_B,OUT_B,ATT_G,ATT_S,DOWN_B,FFN_G,FFN_S,STAMP_B,EMBED_B=range(4,14); UP_B=14
def owner_of(rows,me,unit,width):
    r=lax.shift_right_logical(lax.broadcasted_iota(jnp.int32,(rows,width),0),SMALL.bit_length()-1)
    shift=unit.bit_length()-1
    t=lax.shift_right_logical(r,shift)
    g=jnp.bitwise_xor(jnp.bitwise_or(jnp.bitwise_and(t*2,7),lax.shift_right_logical(t,2)),me)
    return g*unit+jnp.bitwise_and(r,unit-1)
def repeats(width,shard):
    l=lax.broadcasted_iota(jnp.int32,(128,width),0).astype(F32); d=lax.broadcasted_iota(jnp.int32,(128,width),1).astype(F32)
    return (d-shard*jnp.floor((d+0.5)*(1.0/shard))==l).astype(BF)
def owned(owner,shard):
    d=lax.broadcasted_iota(jnp.int32,owner.shape,1)
    return (d>=owner*shard)&(d<owner*shard+shard)
def pack_kernel(*refs):
    *ins,first_ref,second_ref,scr=refs
    wq,wk,wv,we,st,wo,wd,wu=ins[:8]; vecs=ins[8:]
    scr[...]=jnp.zeros_like(scr)
    scr[:st.shape[0],:]=st[...]
    for r,v in enumerate(vecs):
        scr[4+r:5+r,:v.shape[0]]=v[...].reshape(1,-1)
    D=wq.shape[1]
    first_ref[...]=jnp.concatenate([wq[...],wk[...],wv[...],we[...],scr[...]],axis=0).astype(BF)
    up=[wu[:,c*D:(c+1)*D] for c in range(wu.shape[1]//D)]
    second_ref[...]=jnp.concatenate([wo[...],wd[...]]+up,axis=0).astype(BF)
def pack(mats,vecs):
    wq,wk,wv,we,st,wo,wd,wu=mats; n,D=wq.shape
    vm=pl.BlockSpec(memory_space=pltpu.VMEM)
    second=n+wd.shape[0]+n*(wu.shape[1]//D)
    if n%8:
        small=jnp.concatenate([st]+[jnp.zeros((4-st.shape[0],D),F32)]+[jnp.pad(v,(0,D-v.shape[0]))[None] for v in vecs]+[jnp.zeros((SMALL-4-len(vecs),D),F32)])
        up=[wu[:,c*D:(c+1)*D] for c in range(wu.shape[1]//D)]
        return jnp.concatenate([wq,wk,wv,we,small]).astype(BF),jnp.concatenate([wo,wd]+up).astype(BF)
    return pl.pallas_call(pack_kernel,in_specs=[vm]*(8+len(vecs)),out_specs=[vm]*2,
      out_shape=[sds((4*n+SMALL,D),BF),sds((second,D),BF)],scratch_shapes=[pltpu.VMEM((SMALL,D),F32)],compiler_params=pltpu.CompilerParams(vmem_limit_bytes=60*2**20),name="pack")(*mats,*vecs)
ORDER=(0,2,4,6,1,3,5,7)
def rows_at(me,t,n):
    return pl.ds(pl.multiple_of(jnp.bitwise_xor(me,ORDER[t])*n,n),n)
def sds(*a): return jax.ShapeDtypeStruct(*a)
def once(s): return pl.BlockSpec(s.shape,lambda i:(0,)*len(s.shape),pipeline_mode=pl.Buffered(1))
def smem(): return pl.BlockSpec(memory_space=pltpu.SMEM)
def anyw(): return pl.BlockSpec(memory_space=pl.ANY)
def load_weights(me,pieces,base,n,dst,sem):
    return [pltpu.make_async_copy(p.at[pl.ds(base,n),:],dst.at[rows_at(me,t,n),:],sem) for t,p in enumerate(pieces)]
def in_kernel(nt,unit,me_ref,info_ref,feat_ref,*rest):
    toks=rest[:nt]; pieces=rest[nt:nt+8]
    mixed_ref,inp_ref,q_ref,k_ref,v_ref,auxk_ref,pre_ref,hid_ref,vec_ref,upb_ref,tok,wq,wk,wv,we,ws,emb,sems=rest[nt+8:]
    i=pl.program_id(0); me=me_ref[0]
    D=wq.shape[0]; n=D//8; ns=ws.shape[0]//8
    tcp=[pltpu.make_async_copy(t,tok.at[c],sems.at[5+c]) for c,t in enumerate(toks)]
    scp=[pltpu.make_async_copy(p.at[pl.ds(4*n,ns),:],ws.at[pl.ds(t*ns,ns),:],sems.at[0]) for t,p in enumerate(pieces)]
    wcp=[load_weights(me,pieces,w*n,n,dst,sems.at[1+w]) for w,dst in enumerate((wq,wk,wv,we))]
    vec=lambda r: vec_ref[pl.ds(r,1),:]
    @pl.when(i==0)
    def _():
        for c in scp+wcp[3]+tcp[:1]+wcp[0]+wcp[1]+wcp[2]+tcp[1:]: c.start()
        for c in scp: c.wait()
        rows=8*ns; total=8*unit; FF=upb_ref.shape[1]
        lead=ws[:,:128]
        spread=mm(lead,repeats(D,D//total),NN)
        spread=jnp.where(owned(owner_of(rows,me,unit,D),D//total),spread,0.0)
        vec_ref[...]=jnp.sum(spread.reshape(total,SMALL,D),axis=0)
        ups=lead.astype(F32).reshape(total,SMALL,128)[:,UP_B,:].astype(BF)
        ups=mm(ups,repeats(FF,FF//total),NN)
        own=owner_of(rows,me,unit,128).reshape(total,SMALL,128)[:,0,:1]
        upb_ref[...]=jnp.sum(jnp.where(owned(jnp.broadcast_to(own,(total,FF)),FF//total),ups,0.0),axis=0,keepdims=True)
        pre=mm(feat_ref[...],ws[...],NN)+vec(STAMP_B)
        pre_ref[...]=pre
        hid=(pre/(1.0+jnp.exp(-pre))).astype(BF)
        hid_ref[...]=hid
        for c in wcp[3]: c.wait()
        emb[...]=mm(hid,we[...],NN)+vec(EMBED_B)
    for c in range(nt):
        @pl.when(i==c)
        def _(): tcp[c].wait()
    flag=info_ref[i,0].astype(F32); nlive=info_ref[i,1]
    x=tok[i].astype(F32)+flag*emb[pl.ds(0,1),:]
    mixed_ref[...]=x
    xb=x.astype(BF); inp_ref[...]=xb
    R=x.shape[0]
    ln=lanes((R,128)); row=lax.broadcasted_iota(jnp.int32,(R,128),0)
    auxk_ref[...]=jnp.where((ln==64)&(row>=nlive),-1e30,0.0).astype(BF)
    @pl.when(i==0)
    def _():
        for w in range(3):
            for c in wcp[w]: c.wait()
    q=(mm(xb,wq[...],NN)+vec(Q_B)).astype(BF)
    q_ref[...]=(q.astype(F32)*0.125).astype(BF)
    k_ref[...]=mm(xb,wk[...],NN).astype(BF)
    v_ref[...]=(mm(xb,wv[...],NN)+vec(V_B)).astype(BF)
def project(me,info,feat,toks,pieces,unit,FF):
    nt=len(toks); R,D=toks[0].shape; n=D//8; ns=pieces[0].shape[0]-4*n; L=nt*R
    row=lambda w: pl.BlockSpec((R,w),lambda i:(i,0))
    full=lambda a: pl.BlockSpec(a.shape,lambda i:(0,)*a.ndim)
    outs=[sds((L,D),F32)]+[sds((L,D),BF)]*4+[sds((L,128),BF),sds((8,D),F32),sds((8,D),BF),sds((SMALL,D),F32),sds((1,FF),F32)]
    return pl.pallas_call(functools.partial(in_kernel,nt,unit),grid=(nt,),
      in_specs=[smem(),smem(),full(feat)]+[anyw()]*(nt+8),
      out_specs=[row(D)]*5+[row(128)]+[once(o) for o in outs[6:]],
      out_shape=outs,
      scratch_shapes=[pltpu.VMEM((nt,R,D),BF)]+[pltpu.VMEM((D,D),BF)]*4+[pltpu.VMEM((8*ns,D),BF),pltpu.VMEM((8,D),F32),pltpu.SemaphoreType.DMA((5+nt,))],
      compiler_params=pltpu.CompilerParams(vmem_limit_bytes=60*2**20),
      cost_estimate=pl.CostEstimate(flops=2*L*D*D*3,bytes_accessed=20_000_000,transcendentals=0),
      name="project")(me,info,feat,*toks,*pieces)

def spread3(row):
    hi,mid,lo=split3(row)
    r=lax.broadcasted_iota(jnp.int32,(8,row.shape[1]),0)
    return jnp.where(r==0,hi,jnp.where(r==1,mid,jnp.where(r==2,lo,0.0))).astype(BF)
def three(rows):
    r=lax.broadcasted_iota(jnp.int32,rows.shape,0)
    return jnp.where(r<3,jnp.broadcast_to(rows[0:1,:].astype(F32),rows.shape),0.0).astype(BF)
def finish_kernel(p0,nt,me_ref,info_ref,*rest):
    att=rest[:7]; ga_hbm,pre_ref,first=rest[7:10]; pieces=rest[10:18]
    out_ref=rest[18]; tg_refs=rest[19:19+nt]; rows_ref=rest[19+nt]
    *work,ga,all_grads,wq,wk,wv,we,sems=rest[20+nt:]
    i=pl.program_id(0); me=me_ref[0]
    L,D=ga.shape; n=D//8; F=first.shape[2]
    cps=[pltpu.make_async_copy(first,all_grads.at[:,:,pl.ds(0,F)],sems.at[0]),pltpu.make_async_copy(ga_hbm,ga,sems.at[0])]
    for w,dst in enumerate((wq,wk,wv,we)): cps+=load_weights(me,pieces,w*n,n,dst,sems.at[0])
    @pl.when(i==0)
    def _():
        for c in cps: c.start()
    bwd_pair(p0,*att,out_ref,*work)
    all_grads[:,:,pl.ds(pl.multiple_of(F+i*128,128),128)]=out_ref[...]
    @pl.when(i==pl.num_programs(0)-1)
    def _():
        for c in cps: c.wait()
        rows_ref[...]=jnp.zeros_like(rows_ref)
        R=L//nt
        for c in range(nt):
            r=pl.ds(c*R,R)
            y=[all_grads[w,r,:] for w in range(3)]
            for w in (0,2): rows_ref[pl.ds(w//2,1),:]+=jnp.sum(y[w].astype(F32),axis=0,keepdims=True)
            g=ga[r,:]+(mm(y[0],wq[...],NT)+mm(y[1],wk[...],NT)+mm(y[2],wv[...],NT))
            rows_ref[pl.ds(3,1),:]+=info_ref[c,0].astype(F32)*jnp.sum(g,axis=0,keepdims=True)
            tg_refs[c][...]=g.astype(BF)
        gh=jnp.sum(mm(spread3(rows_ref[pl.ds(3,1),:]),we[...],NT),axis=0,keepdims=True)
        pre=pre_ref[0:1,:]
        sg=1.0/(1.0+jnp.exp(-pre))
        rows_ref[pl.ds(2,1),:]=gh*(sg*(1.0+pre*(1.0-sg)))
def attn_finish(me,info,att,ga,pre,first,pieces,p0,np_,C):
    L,D=ga.shape; nt=L//C
    ins,scratch=bwd_specs(*att,p0,0)
    outs=[sds((3,L,128*np_),BF)]+[sds((C,D),BF)]*nt+[sds((8,D),F32)]
    return pl.pallas_call(functools.partial(finish_kernel,p0,nt),grid=(np_,),
      in_specs=[smem(),smem()]+ins+[anyw(),pl.BlockSpec((8,D),lambda i:(0,0)),anyw()]+[anyw()]*8,
      out_specs=[pl.BlockSpec((3,L,128),lambda p:(0,0,p))]+[once(o) for o in outs[1:]],out_shape=outs,
      scratch_shapes=scratch+[pltpu.VMEM((L,D),F32),pltpu.VMEM((3,L,D),BF)]+[pltpu.VMEM((D,D),BF)]*4+[pltpu.SemaphoreType.DMA((1,))],
      compiler_params=pltpu.CompilerParams(vmem_limit_bytes=60*2**20),
      cost_estimate=bwd_cost(L,np_),
      name="attn_finish")(me,info,*att,ga,pre,first,*pieces)
STEP=1024
def weight_kernel(nc,unit,me_ref,inp_ref,rows_ref,hid_ref,feat_ref,dvec_ref,dupb_ref,*rest):
    grads=rest[:nc]
    mine_ref,theirs_ref,acc=rest[nc:]
    i=pl.program_id(0); me=me_ref[0]
    D=inp_ref.shape[1]; n=D//8; rows=feat_ref.shape[1]; ns=rows//8
    def to(t): return mine_ref if t<4 else theirs_ref
    @pl.when(i==0)
    def _():
        acc[:,3*D:]=mm(three(hid_ref[...]),spread3(rows_ref[3:4,:]),TN)
        total=8*unit; FF=dupb_ref.shape[1]
        r=lax.broadcasted_iota(jnp.int32,(SMALL,D),0)
        vec=dvec_ref[...]
        for at,row in ((Q_B,0),(V_B,1),(STAMP_B,2),(EMBED_B,3)):
            vec=jnp.where(r==at,rows_ref[row:row+1,:],vec)
        vec=jnp.broadcast_to(vec[None],(total,SMALL,D)).reshape(rows,D)
        vec=jnp.where(owned(owner_of(rows,me,unit,D),D//total),vec,0.0).astype(BF)
        vec=mm(vec,repeats(D,D//total),NT)
        own=owner_of(rows,me,unit,128).reshape(total,SMALL,128)[:,0,:1]
        ups=jnp.where(owned(jnp.broadcast_to(own,(total,FF)),FF//total),dupb_ref[...],0.0).astype(BF)
        ups=mm(ups,repeats(FF,FF//total),NT)
        line=jnp.bitwise_and(lax.broadcasted_iota(jnp.int32,(rows,128),0),SMALL-1)
        ups=jnp.broadcast_to(ups[:,None,:],(total,SMALL,128)).reshape(rows,128)
        vec=jnp.where(line==UP_B,ups,jnp.where((line>=4)&(line<UP_B),vec,0.0))
        small=mm(three(feat_ref[...]),spread3(rows_ref[2:3,:]),TN)
        small=small+jnp.concatenate([vec,jnp.zeros((rows,D-128),F32)],axis=1)
        small=small.astype(BF)
        for t in range(8): to(t)[t%4,4*n:,:]=small[t*ns:(t+1)*ns]
    part=mm(inp_ref[...],jnp.concatenate([s[w] for w in range(3) for s in grads],axis=1),TN)
    @pl.when(i==0)
    def _(): acc[:,:3*D]=part
    @pl.when(i>0)
    def _(): acc[:,:3*D]+=part
    @pl.when(i==pl.num_programs(0)-1)
    def _():
        for t in range(8):
            for w in range(4): to(t)[t%4,w*n:(w+1)*n,:]=acc[rows_at(me,t,n),w*D:(w+1)*D].astype(BF)
def weight_grads(me,inp,rows,hid,feat,dvec,dupb,grads,unit):
    L,D=inp.shape; R=min(STEP,L); n=D//8; nc=len(grads)
    outs=[sds((4,4*n+feat.shape[1]//8,D),BF)]*2
    full=lambda a: pl.BlockSpec(a.shape,lambda i:(0,)*a.ndim)
    return pl.pallas_call(functools.partial(weight_kernel,nc,unit),grid=(L//R,),
      in_specs=[smem(),pl.BlockSpec((R,D),lambda i:(i,0))]+[full(a) for a in (rows,hid,feat,dvec,dupb)]+[pl.BlockSpec((3,R,a.shape[2]),lambda i:(0,i,0)) for a in grads],
      out_specs=[once(o) for o in outs],out_shape=outs,
      scratch_shapes=[pltpu.VMEM((D,4*D),F32)],
      compiler_params=pltpu.CompilerParams(vmem_limit_bytes=60*2**20),
      cost_estimate=pl.CostEstimate(flops=2*L*D*D*3,bytes_accessed=12_000_000,transcendentals=0),
      name="weight_grads")(me,inp,rows,hid,feat,dvec,dupb,*grads)
LB=384
def room(rows): return (60 if rows>512 else 20)*2**20
def take(k,R): return pl.BlockSpec((1,R,LB),lambda i:(k,0,i))
def flat(R): return pl.BlockSpec((R,LB),lambda i:(0,i))
def total_of(refs):
    out=refs[0].astype(F32)
    for r in refs[1:]: out=out+r.astype(F32)
    return out
def three_kernel(a1,b1,a2,b2,a3,b3,o1,o2,o3):
    for a,b,o in ((a1,b1,o1),(a2,b2,o2),(a3,b3,o3)): o[...]=total_of((a[0],b[0])).astype(BF)
def sum_three(mine,got):
    _,R,D=mine.shape
    return pl.pallas_call(three_kernel,grid=(D//LB,),in_specs=[take(1,R)]*2+[take(2,R)]*2+[take(3,R)]*2,
      out_specs=[flat(R)]*3,out_shape=[sds((R,D),BF)]*3,compiler_params=pltpu.CompilerParams(vmem_limit_bytes=room(R)),name="sum_three")(mine,got,mine,got,mine,got)
def own_kernel(sizes,unit,nx,inner_ref,a,b,*rest):
    more=rest[:nx]; keep,send,scr=rest[nx:]
    inner=inner_ref[0]
    scr[...]=total_of((a[0],b[0])+tuple(x[...] for x in more))
    for j in range(unit):
        k=jnp.bitwise_xor(inner,j); at=0; out=0
        for count,size in sizes:
            for c in range(count):
                x=scr[pl.ds(pl.multiple_of(at+k*size,8),size),:]
                if j%2: send[j//2,out:out+size,:]=x.astype(BF)
                else: keep[j//2,out:out+size,:]=x
                at+=unit*size; out+=size
def sum_own(inner,mine,got,more,sizes,unit):
    _,R,D=mine.shape; rows=R//unit
    if any(size%8 for _,size in sizes):
        x=mine[0].astype(F32)+got[0].astype(F32)+sum(m.astype(F32) for m in more); at=0; parts=[]
        for count,size in sizes:
            for c in range(count):
                parts.append(x[at:at+unit*size].reshape(unit,size,D)); at+=unit*size
        x=in_order(jnp.concatenate(parts,1),inner)
        return jnp.stack([x[j] for j in range(0,unit,2)]),jnp.stack([x[j] for j in range(1,unit,2)]).astype(BF)
    blk=pl.BlockSpec((unit//2,rows,LB),lambda i:(0,0,i))
    keep,send=pl.pallas_call(functools.partial(own_kernel,sizes,unit,len(more)),grid=(D//LB,),
      in_specs=[smem()]+[take(0,R)]*2+[flat(R)]*len(more),out_specs=[blk]*2,
      out_shape=[sds((unit//2,rows,D),F32),sds((unit//2,rows,D),BF)],scratch_shapes=[pltpu.VMEM((R,LB),F32)],compiler_params=pltpu.CompilerParams(vmem_limit_bytes=room(R)),name="sum_own")(inner.reshape(1).astype(jnp.int32),mine,got,*more)
    return keep,send
def direct_kernel(sizes,unit,nx,inner_ref,a,b,*rest):
    more=rest[:nx]; outs=rest[nx:nx+unit]; scr=rest[nx+unit]
    inner=inner_ref[0]
    scr[...]=total_of((a[0],b[0])+tuple(x[...] for x in more))
    for j,dst in enumerate(outs):
        k=jnp.bitwise_xor(inner,j); at=0; out=0
        for count,size in sizes:
            for c in range(count):
                dst[out:out+size,:]=scr[pl.ds(pl.multiple_of(at+k*size,8),size),:].astype(dst.dtype)
                at+=unit*size; out+=size
def sum_direct(inner,mine,got,more,sizes,unit):
    _,R,D=mine.shape; rows=R//unit
    if any(size%8 for _,size in sizes):
        x=mine[0].astype(F32)+got[0].astype(F32)+sum(m.astype(F32) for m in more); at=0; parts=[]
        for count,size in sizes:
            for c in range(count):
                parts.append(x[at:at+unit*size].reshape(unit,size,D)); at+=unit*size
        x=in_order(jnp.concatenate(parts,1),inner)
        return [x[0]]+[x[j].astype(BF) for j in range(1,unit)]
    return pl.pallas_call(functools.partial(direct_kernel,sizes,unit,len(more)),grid=(D//LB,),
      in_specs=[smem()]+[take(0,R)]*2+[flat(R)]*len(more),out_specs=[flat(rows)]*unit,
      out_shape=[sds((rows,D),F32)]+[sds((rows,D),BF)]*(unit-1),scratch_shapes=[pltpu.VMEM((R,LB),F32)],
      compiler_params=pltpu.CompilerParams(vmem_limit_bytes=room(R)),name="sum_direct")(inner.reshape(1).astype(jnp.int32),mine,got,*more)
def last1_kernel(ng,*refs):
    x=total_of([r[...] for r in refs[:ng]]); outs=refs[ng:]
    *mats,st=outs[:5]; n=mats[0].shape[0]
    for w,o in enumerate(mats): o[...]=x[w*n:(w+1)*n]
    st[...]=x[4*n:4*n+st.shape[0]]
    for r,o in enumerate(outs[5:]):
        o[...]=x[4*n+4+r:4*n+5+r,:o.shape[0]].reshape(o.shape)
def last1(given,n,stamp_rows,sizes):
    D=given[0].shape[1]
    vm=pl.BlockSpec(memory_space=pltpu.VMEM)
    outs=[sds((n,D),F32)]*4+[sds((stamp_rows,D),F32)]+[sds((k,),F32) for k in sizes]
    if n%8:
        x=sum(g.astype(F32) for g in given)
        return [x[w*n:(w+1)*n] for w in range(4)]+[x[4*n:4*n+stamp_rows]]+[x[4*n+4+r,:k] for r,k in enumerate(sizes)]
    return pl.pallas_call(functools.partial(last1_kernel,len(given)),in_specs=[vm]*len(given),out_specs=[vm]*len(outs),out_shape=outs,
      compiler_params=pltpu.CompilerParams(vmem_limit_bytes=12*2**20),name="last_attn")(*given)
def last2_kernel(keep_ref,got_ref,wo,wd,wu):
    x=keep_ref[...]+got_ref[...].astype(F32); n,D=wo.shape; m=wd.shape[0]
    wo[...]=x[:n]; wd[...]=x[n:n+m]
    for c in range(wu.shape[1]//D): wu[:,c*D:(c+1)*D]=x[n+m+c*n:n+m+(c+1)*n]
def last2(keep,got,n,m,FF):
    D=keep.shape[1]
    vm=pl.BlockSpec(memory_space=pltpu.VMEM)
    outs=[sds((n,D),F32),sds((m,D),F32),sds((n,FF),F32)]
    if n%8:
        x=keep+got.astype(F32)
        return x[:n],x[n:n+m],jnp.concatenate([x[n+m+c*n:n+m+(c+1)*n] for c in range(FF//D)],1)
    return pl.pallas_call(last2_kernel,in_specs=[vm]*2,out_specs=[vm]*3,out_shape=outs,compiler_params=pltpu.CompilerParams(vmem_limit_bytes=12*2**20),name="last_ffn")(keep,got)

INV_SQRT2=0.7071067811865476; INV_SQRT2PI=0.3989422804014327
HEAD=64
RB=256; FC=768
def norm_stats(x):
    mu=jnp.mean(x,axis=1,keepdims=True); c=x-mu
    r=lax.rsqrt(jnp.mean(c*c,axis=1,keepdims=True)+1e-5)
    return c*r,r
def norm_back(e,n,r):
    return r*(e-jnp.mean(e,axis=1,keepdims=True)-n*jnp.mean(e*n,axis=1,keepdims=True))
def colsum(x): return jnp.sum(x,axis=0,keepdims=True)
def mid_kernel(nblk,me_ref,info_ref,mix_ref,cot_refs,att_refs,vec_ref,upb_ref,pieces,
        out_refs,gas_ref,gatt_ref,auxd_ref,mine_ref,theirs_ref,dvec_ref,dupb_ref,
        wo,wd,wu,cot,res,atta,hida,gda,gba,gel,gup,dgel,sems):
    i=pl.program_id(0); nb=pl.num_programs(0)
    D=wo.shape[0]; FF=wd.shape[0]; ro=D//nblk; rd=FF//nblk
    me=me_ref[0]
    lower=[p[0] if isinstance(p,tuple) else p for p in pieces]
    upper=[(p[1],0) if isinstance(p,tuple) else (p,ro+rd) for p in pieces]
    cps=[load_weights(me,lower,0,ro,wo,sems.at[0]),
        [pltpu.make_async_copy(p.at[pl.ds(at+b*ro,ro),:],wu.at[rows_at(me,t,ro),pl.ds(b*D,D)],sems.at[1])
            for b in range(FF//D) for t,(p,at) in enumerate(upper)],
        load_weights(me,lower,ro,rd,wd,sems.at[2])]
    cps[0]+=[pltpu.make_async_copy(src,cot.at[c],sems.at[0]) for c,src in enumerate(cot_refs)]
    def wait(which):
        @pl.when(i==0)
        def _():
            for c in cps[which]: c.wait()
    @pl.when(i==0)
    def _():
        for w in cps:
            for c in w: c.start()
        dvec_ref[...]=jnp.zeros_like(dvec_ref); dupb_ref[...]=jnp.zeros_like(dupb_ref)
    vec=lambda r: vec_ref[pl.ds(r,1),:].astype(F32)
    nlive=info_ref[i,1]
    x0=mix_ref[...]
    live=(lax.broadcasted_iota(jnp.int32,(RB,1),0)<nlive).astype(F32)
    wait(0)
    att=jnp.concatenate([a[...] for a in att_refs],axis=1)
    rows=pl.ds(pl.multiple_of(i*RB,RB),RB)
    atta[rows,:]=att
    asum=x0+(mm(att,wo[...],NN)+vec(OUT_B))
    n1,r1=norm_stats(asum)
    normed=n1*vec(ATT_G)+vec(ATT_S)
    hid=normed.astype(BF)
    hida[rows,:]=hid
    wait(1); wait(2)
    down=None
    for f in range(FF//FC):
        c=slice(f*FC,(f+1)*FC)
        u=mm(hid,wu[:,c],NN)+upb_ref[:,c].astype(F32)
        ph=0.5+0.5*lax.erf(u*INV_SQRT2)
        pd=jnp.exp(u*u*-0.5)*INV_SQRT2PI
        g=(u*ph).astype(BF)
        gel[rows,c]=g
        dgel[:,c]=ph+u*pd
        t=mm(g,wd[c,:],NN)
        down=t if down is None else down+t
    fsum=normed+(down+vec(DOWN_B))
    n2,r2=norm_stats(fsum)
    g2=vec(FFN_G)
    res[i]=((n2*g2+vec(FFN_S))*live).astype(BF)
    og=cot[i].astype(F32)*live
    dvec_ref[pl.ds(FFN_G,1),:]+=colsum(og*n2)
    dvec_ref[pl.ds(FFN_S,1),:]+=colsum(og)
    gf=norm_back(og*g2,n2,r2)
    gd=gf.astype(BF)
    gda[rows,:]=gd
    dvec_ref[pl.ds(DOWN_B,1),:]+=colsum(gd.astype(F32))
    gn=gf
    for f in range(FF//FC):
        c=slice(f*FC,(f+1)*FC)
        gu=(mm(gd,wd[c,:],NT)*dgel[:,c]).astype(BF)
        dupb_ref[:,c]+=colsum(gu.astype(F32))
        gup[rows,c]=gu
        gn=gn+mm(gu,wu[:,c],NT)
    dvec_ref[pl.ds(ATT_G,1),:]+=colsum(gn*n1)
    dvec_ref[pl.ds(ATT_S,1),:]+=colsum(gn)
    ga=norm_back(gn*vec(ATT_G),n1,r1)
    gas_ref[...]=ga
    gb=ga.astype(BF)
    dvec_ref[pl.ds(OUT_B,1),:]+=colsum(gb.astype(F32))
    gba[rows,:]=gb
    gatt=mm(gb,wo[...],NT).astype(BF)
    gatt_ref[...]=gatt
    pr=-(gatt.astype(F32)*att.astype(F32))
    hi,mid,lo=split3(pr)
    hrow=lax.broadcasted_iota(jnp.int32,(D,128),0)//64
    hcol=lax.broadcasted_iota(jnp.int32,(D,128),1)
    ind=((hcol>=3*hrow)&(hcol<3*hrow+3)).astype(BF)
    dl=mm(hi.astype(BF),ind,NN)+mm(mid.astype(BF),ind,NN)
    h2,m2,l2=split3(dl)
    ln=lanes(dl.shape)%3
    auxd_ref[...]=jnp.where(ln==0,h2,jnp.where(ln==1,m2,l2)).astype(BF)
    @pl.when(i==nb-1)
    def _():
        def send(src,at,n):
            cps=[pltpu.make_async_copy(src.at[rows_at(me,t,n),:],(mine_ref if t<4 else theirs_ref).at[t%4,pl.ds(at,n),:],sems.at[3]) for t in range(8)]
            for c in cps: c.start()
            return cps
        out=[pltpu.make_async_copy(res.at[c],dst,sems.at[3]) for c,dst in enumerate(out_refs)]
        for c in out: c.start()
        for b in range(FF//D):
            c=slice(b*D,(b+1)*D)
            wd[c,:]=mm(gel[:,c],gda[...],TN).astype(BF)
        out+=send(wd,ro,rd)
        wo[...]=mm(atta[...],gba[...],TN).astype(BF)
        out+=send(wo,0,ro)
        for b in range(FF//D):
            c=slice(b*D,(b+1)*D)
            wu[:,c]=mm(hida[...],gup[:,c],TN).astype(BF)
            out+=send(wu.at[:,pl.ds(b*D,D)],ro+rd+b*ro,ro)
        for c in out: c.wait()
def middle(me,info,mixed,cots,atts,vec,upb,pieces):
    nblk=8; L,D=mixed.shape; FF=upb.shape[1]; ro=D//8; rd=FF//8
    nb=L//RB; na=len(atts); nt=len(cots)
    flat_pieces=jax.tree.leaves(pieces)
    def kern(me_ref,info_ref,mix_ref,*rest):
        cot=rest[:nt]; att=rest[nt:nt+na]; rest=rest[nt+na:]
        given=iter(rest[2:2+len(flat_pieces)])
        blocks=[(next(given),next(given)) if isinstance(p,tuple) else next(given) for p in pieces]
        rest_out=rest[2+len(flat_pieces):]
        mid_kernel(nblk,me_ref,info_ref,mix_ref,cot,att,rest[0],rest[1],blocks,rest_out[:nt],*rest_out[nt:])
    full=lambda a: pl.BlockSpec(a.shape,lambda i:(0,)*a.ndim)
    row=pl.BlockSpec((RB,D),lambda i:(i,0))
    outs=[sds((RB,D),BF)]*nt+[sds((L,D),F32),sds((L,D),BF),sds((L,128),BF)]+[sds((4,)+pieces[0].shape,BF)]*2+[sds((16,D),F32),sds((1,FF),F32)]
    return pl.pallas_call(kern,grid=(nb,),
      in_specs=[smem(),smem(),row]+[anyw()]*nt+[pl.BlockSpec((RB,a.shape[1]),lambda i:(i,0)) for a in atts]+[full(vec),full(upb)]+[anyw()]*len(flat_pieces),
      out_specs=[anyw()]*nt+[row,row,pl.BlockSpec((RB,128),lambda i:(i,0)),anyw(),anyw()]+[once(s) for s in outs[nt+5:]],
      out_shape=outs,
      scratch_shapes=[pltpu.VMEM((D,D),BF),pltpu.VMEM((FF,D),BF),pltpu.VMEM((D,FF),BF),
        pltpu.VMEM((nt,RB,D),BF),pltpu.VMEM((nt,RB,D),BF)]+[pltpu.VMEM((L,D),BF)]*4+[pltpu.VMEM((L,FF),BF)]*2+[
        pltpu.VMEM((RB,FF),F32),pltpu.SemaphoreType.DMA((4,))],
      compiler_params=pltpu.CompilerParams(vmem_limit_bytes=61*2**20),
      cost_estimate=pl.CostEstimate(flops=2*L*D*(3*D+6*FF),bytes_accessed=60_000_000,transcendentals=2*L*FF),
      name="middle")(me,info,mixed,*cots,*atts,vec,upb,*flat_pieces)

GROUPS=8
AXES=("seq","stream")
def flip(x,mask,total):
    return lax.ppermute(x,AXES,[(i,i^mask) for i in range(total)])
def far_first(count):
    bits=[]; bit=count//2
    while bit: bits.append(bit); bit//=2
    return bits
def widen(x,bit,total): return jnp.concatenate([x,flip(x,bit,total)])
def settle(x,inner,count):
    ids=[0]
    for bit in far_first(count): ids=ids+[i^bit for i in ids]
    return in_order(jnp.stack([x[ids.index(k)] for k in range(count)]),inner)
def in_order(x,index):
    n=x.shape[0]; bit=1
    while bit<n:
        turned=jnp.concatenate([x[k^bit][None] for k in range(n)])
        x=jnp.where((index&bit)!=0,turned,x); bit*=2
    return x
def after(x,*deps):
    return lax.optimization_barrier((x,)+deps)[0]
def sync(*xs): return lax.optimization_barrier(xs)
def spread_start(own,unit,total):
    across=lambda x,g: flip(x,g*unit,total)
    return [own,across(own,2),across(own,4)]
def split_send(x,bit,total):
    send=jnp.stack([x[j] for j in range(1,x.shape[0],2)]).astype(BF)
    return jnp.stack([x[j] for j in range(0,x.shape[0],2)]),flip(send,bit,total)
def finish2(keep,got,total):
    bit=2
    while keep.shape[0]>1:
        keep,got=split_send(keep+got.astype(F32),bit,total); bit*=2
    return keep[0],got[0]
def on_device(tokens,source_len,target_len,timesteps,cotangent,query_weight,query_bias,key_weight,value_weight,value_bias,
        out_weight,out_bias,attn_gain,attn_shift,up_weight,up_bias,down_weight,down_bias,ffn_gain,ffn_shift,
        stamp_weight,stamp_bias,embed_weight,embed_bias):
    seqs,R,D=tokens.shape
    streams=lax.axis_size("stream"); seq_size=lax.axis_size("seq"); total=seq_size*streams
    s0=lax.axis_index("stream"); flat=lax.axis_index("seq")*streams+s0
    unit=total//GROUPS
    inner=flat%unit; group=flat//unit
    me=group.astype(jnp.int32).reshape(1)
    n=D//GROUPS; shard=D//total; stamp_rows=stamp_weight.shape[0]; FF=up_weight.shape[1]; ff_shard=FF//total
    vecs=(query_bias,value_bias,out_bias,attn_gain,attn_shift,down_bias,ffn_gain,ffn_shift,stamp_bias,embed_bias,up_bias)
    first,second=pack((query_weight,key_weight,value_weight,embed_weight,stamp_weight,out_weight,down_weight,up_weight),vecs)
    def rowwise(x,sizes):
        at=0; out=[]
        for count,size in sizes:
            part=x[:,at:at+count*size].reshape(unit,count,size,x.shape[2])
            out.append(part.transpose(1,0,2,3).reshape(count*unit*size,x.shape[2])); at+=count*size
        return jnp.concatenate(out) if len(out)>1 else out[0]
    def exchange(chunks):
        return [x if c==0 else flip(x,c,total) for c,x in enumerate(chunks)]
    def chunks_of(x): return [lax.dynamic_index_in_dim(x,s0^c,0,keepdims=False) for c in range(streams)]
    order=jnp.asarray(ORDER,jnp.int32)
    source=source_len[s0]; target=target_len[s0]; stamp=timesteps[s0]
    half=R*streams//2
    place=(s0^jnp.arange(streams))*R
    flag=(place>=half).astype(jnp.int32)
    nlive=jnp.clip(jnp.where(flag==1,target-(place-half),source-place),0,R).astype(jnp.int32)
    info=jnp.stack([flag,nlive],1)
    tdim=stamp_rows*total; halfway=tdim//2
    t_ids=(((order^group)[:,None,None]*unit+jnp.arange(unit)[None,:,None])*stamp_rows+jnp.arange(SMALL)[None,None,:])
    valid=(jnp.arange(SMALL)<stamp_rows)[None,None,:]
    t_ids=jnp.where(valid,t_ids,0).reshape(-1)
    rates=jnp.exp(-math.log(10000.0)*(t_ids%halfway).astype(F32)/halfway)
    angle=stamp.astype(F32)*rates
    feats=jnp.where(t_ids<halfway,jnp.sin(angle),jnp.cos(angle))
    feats=jnp.where(jnp.broadcast_to(valid,(GROUPS,unit,SMALL)).reshape(-1),feats,0.0)
    feat=jnp.broadcast_to(feats.astype(BF)[None],(8,feats.shape[0]))
    bits=far_first(unit)
    first=widen(first[None],bits[0],total)
    first,second=sync(first,second)
    second=widen(second[None],bits[0],total)
    for bit in bits[1:]: first=widen(first,bit,total)
    first=rowwise(settle(first,inner,unit),((4,shard),(1,SMALL)))
    cells=chunks_of(tokens)
    first,second,feat,info,*cells=sync(first,second,feat,info,*cells)
    for bit in bits[1:]: second=widen(second,bit,total)
    n1=[first]+[flip(first,g*unit,total) for g in (2,4,6)]
    toks=[cells[0]]+[None]*(streams-1)
    early,late=list(range(2,streams)),[1]
    for c in early: toks[c]=flip(cells[c],c,total)
    n1[1],n1[2],toks[2],second=sync(n1[1],n1[2],toks[2],second)
    second=rowwise(settle(second,inner,unit),((1,shard),(1,ff_shard),(FF//D,shard)))
    for c in late: toks[c]=flip(after(cells[c],second),c,total)
    n2=spread_start(second,unit,total)
    p1=n1+[flip(x,unit,total) for x in n1]
    *cells,_=sync(*chunks_of(cotangent),toks)
    far=[flip(n2[0],unit,total)]
    cots=[cells[0]]+[flip(cells[c],c,total) for c in range(1,streams-1)]
    mixed,inputs,q,k,v,auxk,pre,hid,vec,upb=project(me,info,feat,toks,p1,unit,FF)
    pairs=D//(2*HEAD); parts=(2,pairs-2)
    atts=[];auxq=[]
    def forward(c,q):
        a,x=attn_fwd(q,k,v,auxk,sum(parts[:c]),parts[c]); atts.append(a); auxq.append(x)
    forward(0,q)
    q,n2,far,cots,cells,atts=sync(q,n2,far,cots,cells,atts)
    cut=n+FF//GROUPS
    low=flip(n2[2][:cut],2*unit,total); high=flip(n2[1][cut:],4*unit,total)
    cots.append(flip(cells[streams-1],streams-1,total))
    far+=[flip(n2[1],unit,total),flip(n2[2],unit,total)]
    forward(1,q)
    low,high,far,atts,cots=sync(low,high,far,atts,cots)
    diag=(low,high)
    p2=n2+[diag]+far+[tuple(flip(x,unit,total) for x in diag)]
    *output,ga,gatt,auxd,mine2,theirs2,dvec,dupb=sync(*middle(me,info,mixed,cots,atts,vec,upb,p2))
    grads=[]
    def backward(c,q):
        grads.append(attn_bwd(q,k,v,gatt,auxk,auxq[c],auxd,sum(parts[:c]),parts[c],0))
    got=flip(theirs2,unit,total)
    backs=[output[0],flip(output[1],1,total)]
    backward(0,q)
    got,q,output,backs,grads=sync(got,q,output,backs,grads)
    fx,fy,fd=(flip(x,g*unit,total) for x,g in zip(sum_three(mine2,got),(2,4,6)))
    backs+=[flip(output[c],c,total) for c in range(2,streams)]
    out,*tg,rows4=attn_finish(me,info,(q,k,v,gatt,auxk,auxq[1],auxd),ga,pre,grads[0],p1,parts[0],parts[1],R)
    grads.append(out)
    def place(chunks,dtype):
        out=jnp.zeros((seqs,R,D),dtype)
        for c,part in enumerate(chunks):
            out=lax.dynamic_update_index_in_dim(out,part.astype(dtype),s0^c,0)
        return out
    tg,rows4,backs=sync(tg,rows4,backs)
    held=[flip(tg[c],c,total) for c in range(1,streams-1)]
    mine1,theirs1=weight_grads(me,inputs,rows4,hid,feat,dvec,dupb,grads,unit)
    mine1,theirs1,fx,fy,fd,held=sync(mine1,theirs1,fx,fy,fd,held)
    keep2,send2=sum_own(inner,mine2,got,(fx,fy,fd),((1,shard),(1,ff_shard),(FF//D,shard)),unit)
    got1=flip(theirs1,unit,total)
    keep2,send2,tg=sync(keep2,send2,tg)
    got2=flip(send2,1,total)
    tgs=[tg[0]]+held+[flip(tg[streams-1],streams-1,total)]
    blocks=sum_three(mine1,got1)
    fx,fy,fd=(flip(x,g*unit,total) for x,g in zip(blocks,(2,4,6)))
    keep2,got2=finish2(keep2,got2,total)
    fx,fy,fd,keep2,got2,tgs=sync(fx,fy,fd,keep2,got2,tgs)
    output=place(backs,BF)
    dwo,dwd,dwu=last2(keep2,got2,shard,ff_shard,FF)
    keep1,*sends=sum_direct(inner,mine1,got1,(fx,fy,fd),((4,shard),(1,SMALL)),unit)
    given=[keep1]+[flip(x,c+1,total) for c,x in enumerate(sends)]
    dwq,dwk,dwv,dwe,dws,bq,bv,bo,ag,as_,bd,fg,fs,bs,be,bu=last1(given,shard,stamp_rows,[shard]*10+[ff_shard])
    token_grad=place(tgs,F32)
    return (output,token_grad,dwq,bq,dwk,dwv,bv,dwo,bo,ag,as_,dwu,bu,dwd,bd,fg,fs,dws,bs,dwe,be)

def solution(mesh):
    cells=P("seq","stream",None); per=P("seq"); mat=P(("seq","stream"),None); row=P(("seq","stream"))
    return jax.shard_map(on_device,mesh=mesh,
        in_specs=(cells,per,per,per,cells,mat,row,mat,mat,row,mat,row,row,row,mat,row,mat,row,row,row,mat,row,mat,row),
        out_specs=(cells,cells,mat,row,mat,mat,row,mat,row,row,row,mat,row,mat,row,row,row,mat,row,mat,row),
        check_vma=False)
```

```python
import functools
import math

import jax
import jax.numpy as jnp
from jax import lax
from jax.experimental import pallas as pl
from jax.experimental.pallas import tpu as pltpu
from jax.sharding import PartitionSpec as P

F32=jnp.float32; BF=jnp.bfloat16
NT=(((1,),(1,)),((),())); NN=(((1,),(0,)),((),())); TN=(((0,),(0,)),((),()))
def mm(a,b,dims): return lax.dot_general(a,b,dims,preferred_element_type=F32)
def lanes(shape): return lax.broadcasted_iota(jnp.int32,shape,len(shape)-1)
def split3(x):
    hi=x.astype(BF).astype(F32); r=x-hi
    mid=r.astype(BF).astype(F32); lo=r-mid
    return hi,mid,lo
QB=256
def fwd_kernel(q_ref,k_ref,v_ref,auxk_ref,o_ref,auxq_ref,kaug,vm):
    L=q_ref.shape[0]
    k=k_ref[...]; v=v_ref[...]; ln=lanes(k.shape)
    for e in range(2):
        sel=(ln<64) if e==0 else (ln>=64)
        kaug[e,:,:128]=jnp.where(sel,k,jnp.zeros_like(k))
        kaug[e,:,128:]=auxk_ref[...]
        vm[e]=jnp.where(sel,v,(ln==64*(1-e)).astype(BF))
    ln=lanes((QB,128)); one=jnp.where(ln==64,1.0,0.0).astype(BF)
    steps=[(b,e) for b in range(L//QB) for e in range(2)]
    def score(b,e):
        return mm(jnp.concatenate([q_ref[pl.ds(b*QB,QB),:],one],axis=1),kaug[e],NT)
    s=score(*steps[0]); out=None; aux=None
    for t,(b,e) in enumerate(steps):
        later=score(*steps[t+1]) if t+1<len(steps) else None
        m=jnp.max(s,axis=1,keepdims=True)
        p=jnp.exp(s-m).astype(BF)
        o=mm(p,vm[e],NN)
        l=o[:,64*(1-e):64*(1-e)+1]
        o=jnp.where((ln<64) if e==0 else (ln>=64),o*(1.0/l),0.0)
        hi,mid,lo=split3(-(m+jnp.log(l)))
        if e==0: out=o; aux=jnp.where(ln==64,1.0,0.0)
        else: out=out+o
        aux=jnp.where(ln==3*e,hi,aux); aux=jnp.where(ln==3*e+1,mid,aux); aux=jnp.where(ln==3*e+2,lo,aux)
        if e==1:
            r=pl.ds(b*QB,QB)
            o_ref[r,:]=out.astype(BF); auxq_ref[0,r,:]=aux.astype(BF)
        s=later
def attn_fwd(q,k,v,auxk,p0,np_):
    L=q.shape[0]
    col=lambda: pl.BlockSpec((L,128),lambda p:(0,p0+p))
    return pl.pallas_call(fwd_kernel,grid=(np_,),
      in_specs=[col(),col(),col(),pl.BlockSpec((L,128),lambda p:(0,0))],
      out_specs=[pl.BlockSpec((L,128),lambda p:(0,p)),pl.BlockSpec((1,L,128),lambda p:(p,0,0))],
      out_shape=[jax.ShapeDtypeStruct((L,128*np_),BF),jax.ShapeDtypeStruct((np_,L,128),BF)],
      scratch_shapes=[pltpu.VMEM((2,L,256),BF),pltpu.VMEM((2,L,128),BF)],
      compiler_params=pltpu.CompilerParams(vmem_limit_bytes=60*2**20),
      cost_estimate=pl.CostEstimate(flops=np_*2*L*L*64*4,bytes_accessed=np_*L*128*2*5,transcendentals=np_*2*L*L),
      name="attn_fwd")(q,k,v,auxk)
def bwd_pair(p0,q_ref,k_ref,v_ref,do_ref,auxk_ref,auxq_ref,auxd_ref,out_ref,kaug,vaug,qa,doa,qm,dom,dk_acc,dv_acc):
    pair=p0+pl.program_id(0)
    L=q_ref.shape[0]
    k=k_ref[...]; v=v_ref[...]; q=q_ref[...]; do=do_ref[...]
    ln=lanes(k.shape); z=jnp.zeros_like(k); auxk=auxk_ref[...]
    qa[:,:128]=q; qa[:,128:]=auxq_ref[0]
    doa[:,:128]=do; doa[:,128:]=auxd_ref[...]
    for e in range(2):
        sel=(ln<64) if e==0 else (ln>=64)
        on=(ln>=3*e)&(ln<3*e+3)
        kaug[e,:,:128]=jnp.where(sel,k,z)
        kaug[e,:,128:]=jnp.where(on,jnp.ones_like(k),auxk)
        vaug[e,:,:128]=jnp.where(sel,v,z)
        b=6*pair+3*e
        vaug[e,:,128:]=jnp.where((ln>=b)&(ln<b+3),jnp.ones_like(k),z)
        qm[e]=jnp.where(sel,q,z)
        dom[e]=jnp.where(sel,do,z)
    for i in range(L//QB):
        r=pl.ds(i*QB,QB)
        dq=None
        for e in range(2):
            p=jnp.exp(mm(kaug[e],qa[r,:],NT))
            dp=mm(vaug[e],doa[r,:],NT)
            ds=(p*dp).astype(BF)
            dv=mm(p.astype(BF),dom[e,r,:],NN)
            dk=mm(ds,qm[e,r,:],NN)
            if i==0 and e==0: dv_acc[...]=dv; dk_acc[...]=dk
            else: dv_acc[...]+=dv; dk_acc[...]+=dk
            d=mm(ds,kaug[e,:,:128],TN)
            dq=d if dq is None else dq+d
        out_ref[0,r,:]=(dq*0.125).astype(BF)
    out_ref[1]=dk_acc[...].astype(BF)
    out_ref[2]=dv_acc[...].astype(BF)
def bwd_specs(q,k,v,do,auxk,auxq,auxd,p0,a0):
    L=q.shape[0]
    col=lambda: pl.BlockSpec((L,128),lambda p:(0,p0+p))
    con=lambda: pl.BlockSpec((L,128),lambda p:(0,0))
    return ([col(),col(),col(),col(),con(),pl.BlockSpec((1,L,128),lambda p:(a0+p,0,0)),con()],
      [pltpu.VMEM((2,L,256),BF),pltpu.VMEM((2,L,256),BF),pltpu.VMEM((L,256),BF),pltpu.VMEM((L,256),BF),
        pltpu.VMEM((2,L,128),BF),pltpu.VMEM((2,L,128),BF),pltpu.VMEM((L,128),F32),pltpu.VMEM((L,128),F32)])
def bwd_cost(L,np_): return pl.CostEstimate(flops=np_*2*L*L*64*10,bytes_accessed=np_*L*128*2*9,transcendentals=np_*2*L*L)
def attn_bwd(q,k,v,do,auxk,auxq,auxd,p0,np_,a0):
    L=q.shape[0]
    ins,scratch=bwd_specs(q,k,v,do,auxk,auxq,auxd,p0,a0)
    return pl.pallas_call(functools.partial(bwd_pair,p0),grid=(np_,),in_specs=ins,
      out_specs=pl.BlockSpec((3,L,128),lambda p:(0,0,p)),
      out_shape=jax.ShapeDtypeStruct((3,L,128*np_),BF),scratch_shapes=scratch,
      compiler_params=pltpu.CompilerParams(vmem_limit_bytes=60*2**20),
      cost_estimate=bwd_cost(L,np_),
      name="attn_bwd")(q,k,v,do,auxk,auxq,auxd)

SMALL=16; Q_B,V_B,OUT_B,ATT_G,ATT_S,DOWN_B,FFN_G,FFN_S,STAMP_B,EMBED_B=range(4,14); UP_B=14
def owner_of(rows,me,unit,width):
    r=lax.shift_right_logical(lax.broadcasted_iota(jnp.int32,(rows,width),0),SMALL.bit_length()-1)
    shift=unit.bit_length()-1
    t=lax.shift_right_logical(r,shift)
    g=jnp.bitwise_xor(jnp.bitwise_or(jnp.bitwise_and(t*2,7),lax.shift_right_logical(t,2)),me)
    return g*unit+jnp.bitwise_and(r,unit-1)
def repeats(width,shard):
    l=lax.broadcasted_iota(jnp.int32,(128,width),0).astype(F32); d=lax.broadcasted_iota(jnp.int32,(128,width),1).astype(F32)
    return (d-shard*jnp.floor((d+0.5)*(1.0/shard))==l).astype(BF)
def owned(owner,shard):
    d=lax.broadcasted_iota(jnp.int32,owner.shape,1)
    return (d>=owner*shard)&(d<owner*shard+shard)
def pack_kernel(*refs):
    *ins,first_ref,second_ref,scr=refs
    wq,wk,wv,we,st,wo,wd,wu=ins[:8]; vecs=ins[8:]
    scr[...]=jnp.zeros_like(scr)
    scr[:st.shape[0],:]=st[...]
    for r,v in enumerate(vecs):
        scr[4+r:5+r,:v.shape[0]]=v[...].reshape(1,-1)
    D=wq.shape[1]
    first_ref[...]=jnp.concatenate([wq[...],wk[...],wv[...],we[...],scr[...]],axis=0).astype(BF)
    up=[wu[:,c*D:(c+1)*D] for c in range(wu.shape[1]//D)]
    second_ref[...]=jnp.concatenate([wo[...],wd[...]]+up,axis=0).astype(BF)
def pack(mats,vecs):
    wq,wk,wv,we,st,wo,wd,wu=mats; n,D=wq.shape
    vm=pl.BlockSpec(memory_space=pltpu.VMEM)
    second=n+wd.shape[0]+n*(wu.shape[1]//D)
    if n%8:
        small=jnp.concatenate([st]+[jnp.zeros((4-st.shape[0],D),F32)]+[jnp.pad(v,(0,D-v.shape[0]))[None] for v in vecs]+[jnp.zeros((SMALL-4-len(vecs),D),F32)])
        up=[wu[:,c*D:(c+1)*D] for c in range(wu.shape[1]//D)]
        return jnp.concatenate([wq,wk,wv,we,small]).astype(BF),jnp.concatenate([wo,wd]+up).astype(BF)
    return pl.pallas_call(pack_kernel,in_specs=[vm]*(8+len(vecs)),out_specs=[vm]*2,
      out_shape=[sds((4*n+SMALL,D),BF),sds((second,D),BF)],scratch_shapes=[pltpu.VMEM((SMALL,D),F32)],compiler_params=pltpu.CompilerParams(vmem_limit_bytes=60*2**20),name="pack")(*mats,*vecs)
ORDER=(0,2,4,6,1,3,5,7)
def rows_at(me,t,n):
    return pl.ds(pl.multiple_of(jnp.bitwise_xor(me,ORDER[t])*n,n),n)
def sds(*a): return jax.ShapeDtypeStruct(*a)
def once(s): return pl.BlockSpec(s.shape,lambda i:(0,)*len(s.shape),pipeline_mode=pl.Buffered(1))
def smem(): return pl.BlockSpec(memory_space=pltpu.SMEM)
def anyw(): return pl.BlockSpec(memory_space=pl.ANY)
def load_weights(me,pieces,base,n,dst,sem):
    return [pltpu.make_async_copy(p.at[pl.ds(base,n),:],dst.at[rows_at(me,t,n),:],sem) for t,p in enumerate(pieces)]
def in_kernel(nt,unit,me_ref,info_ref,feat_ref,*rest):
    toks=rest[:nt]; pieces=rest[nt:nt+8]
    mixed_ref,inp_ref,q_ref,k_ref,v_ref,auxk_ref,pre_ref,hid_ref,vec_ref,upb_ref,tok,wq,wk,wv,we,ws,emb,sems=rest[nt+8:]
    i=pl.program_id(0); me=me_ref[0]
    D=wq.shape[0]; n=D//8; ns=ws.shape[0]//8
    tcp=[pltpu.make_async_copy(t,tok.at[c],sems.at[5+c]) for c,t in enumerate(toks)]
    scp=[pltpu.make_async_copy(p.at[pl.ds(4*n,ns),:],ws.at[pl.ds(t*ns,ns),:],sems.at[0]) for t,p in enumerate(pieces)]
    wcp=[load_weights(me,pieces,w*n,n,dst,sems.at[1+w]) for w,dst in enumerate((wq,wk,wv,we))]
    vec=lambda r: vec_ref[pl.ds(r,1),:]
    @pl.when(i==0)
    def _():
        for c in scp+wcp[3]+tcp[:1]+wcp[0]+wcp[1]+wcp[2]+tcp[1:]: c.start()
        for c in scp: c.wait()
        rows=8*ns; total=8*unit; FF=upb_ref.shape[1]
        lead=ws[:,:128]
        spread=mm(lead,repeats(D,D//total),NN)
        spread=jnp.where(owned(owner_of(rows,me,unit,D),D//total),spread,0.0)
        vec_ref[...]=jnp.sum(spread.reshape(total,SMALL,D),axis=0)
        ups=lead.astype(F32).reshape(total,SMALL,128)[:,UP_B,:].astype(BF)
        ups=mm(ups,repeats(FF,FF//total),NN)
        own=owner_of(rows,me,unit,128).reshape(total,SMALL,128)[:,0,:1]
        upb_ref[...]=jnp.sum(jnp.where(owned(jnp.broadcast_to(own,(total,FF)),FF//total),ups,0.0),axis=0,keepdims=True)
        pre=mm(feat_ref[...],ws[...],NN)+vec(STAMP_B)
        pre_ref[...]=pre
        hid=(pre/(1.0+jnp.exp(-pre))).astype(BF)
        hid_ref[...]=hid
        for c in wcp[3]: c.wait()
        emb[...]=mm(hid,we[...],NN)+vec(EMBED_B)
    for c in range(nt):
        @pl.when(i==c)
        def _(): tcp[c].wait()
    flag=info_ref[i,0].astype(F32); nlive=info_ref[i,1]
    x=tok[i].astype(F32)+flag*emb[pl.ds(0,1),:]
    mixed_ref[...]=x
    xb=x.astype(BF); inp_ref[...]=xb
    R=x.shape[0]
    ln=lanes((R,128)); row=lax.broadcasted_iota(jnp.int32,(R,128),0)
    auxk_ref[...]=jnp.where((ln==64)&(row>=nlive),-1e30,0.0).astype(BF)
    @pl.when(i==0)
    def _():
        for w in range(3):
            for c in wcp[w]: c.wait()
    q=(mm(xb,wq[...],NN)+vec(Q_B)).astype(BF)
    q_ref[...]=(q.astype(F32)*0.125).astype(BF)
    k_ref[...]=mm(xb,wk[...],NN).astype(BF)
    v_ref[...]=(mm(xb,wv[...],NN)+vec(V_B)).astype(BF)
def project(me,info,feat,toks,pieces,unit,FF):
    nt=len(toks); R,D=toks[0].shape; n=D//8; ns=pieces[0].shape[0]-4*n; L=nt*R
    row=lambda w: pl.BlockSpec((R,w),lambda i:(i,0))
    full=lambda a: pl.BlockSpec(a.shape,lambda i:(0,)*a.ndim)
    outs=[sds((L,D),F32)]+[sds((L,D),BF)]*4+[sds((L,128),BF),sds((8,D),F32),sds((8,D),BF),sds((SMALL,D),F32),sds((1,FF),F32)]
    return pl.pallas_call(functools.partial(in_kernel,nt,unit),grid=(nt,),
      in_specs=[smem(),smem(),full(feat)]+[anyw()]*(nt+8),
      out_specs=[row(D)]*5+[row(128)]+[once(o) for o in outs[6:]],
      out_shape=outs,
      scratch_shapes=[pltpu.VMEM((nt,R,D),BF)]+[pltpu.VMEM((D,D),BF)]*4+[pltpu.VMEM((8*ns,D),BF),pltpu.VMEM((8,D),F32),pltpu.SemaphoreType.DMA((5+nt,))],
      compiler_params=pltpu.CompilerParams(vmem_limit_bytes=60*2**20),
      cost_estimate=pl.CostEstimate(flops=2*L*D*D*3,bytes_accessed=20_000_000,transcendentals=0),
      name="project")(me,info,feat,*toks,*pieces)

def spread3(row):
    hi,mid,lo=split3(row)
    r=lax.broadcasted_iota(jnp.int32,(8,row.shape[1]),0)
    return jnp.where(r==0,hi,jnp.where(r==1,mid,jnp.where(r==2,lo,0.0))).astype(BF)
def three(rows):
    r=lax.broadcasted_iota(jnp.int32,rows.shape,0)
    return jnp.where(r<3,jnp.broadcast_to(rows.astype(F32)[0:1,:],rows.shape),0.0).astype(BF)
def finish_kernel(p0,nt,me_ref,info_ref,*rest):
    att=rest[:7]; ga_hbm,pre_ref,first=rest[7:10]; pieces=rest[10:18]
    out_ref=rest[18]; tg_refs=rest[19:19+nt]; rows_ref=rest[19+nt]
    *work,ga,all_grads,wqkv,we,sems=rest[20+nt:]
    i=pl.program_id(0); me=me_ref[0]
    L,D=ga.shape; n=D//8; F=first.shape[2]
    cps=[pltpu.make_async_copy(ga_hbm,ga,sems.at[0])]
    for w in range(3):
        cps.append(pltpu.make_async_copy(first.at[w],all_grads.at[:,pl.ds(w*D,F)],sems.at[0]))
        cps+=load_weights(me,pieces,w*n,n,wqkv.at[:,pl.ds(w*D,D)],sems.at[0])
    cps+=load_weights(me,pieces,3*n,n,we,sems.at[0])
    @pl.when(i==0)
    def _():
        for c in cps: c.start()
    bwd_pair(p0,*att,out_ref,*work)
    for w in range(3): all_grads[:,pl.ds(pl.multiple_of(w*D+F+i*128,128),128)]=out_ref[w]
    @pl.when(i==pl.num_programs(0)-1)
    def _():
        for c in cps: c.wait()
        rows_ref[...]=jnp.zeros_like(rows_ref)
        R=L//nt; per=max(1,MROWS//R)
        for c in range(0,nt,per):
            r=pl.ds(c*R,per*R)
            y=all_grads[r,:]
            for w in (0,2): rows_ref[pl.ds(w//2,1),:]+=jnp.sum(y[:,w*D:(w+1)*D].astype(F32),axis=0,keepdims=True)
            g=ga[r,:]+mm(y,wqkv[...],NT)
            for p in range(per):
                part=g[p*R:(p+1)*R]
                rows_ref[pl.ds(3,1),:]+=info_ref[c+p,0].astype(F32)*jnp.sum(part,axis=0,keepdims=True)
                tg_refs[c+p][...]=part.astype(BF)
        gh=jnp.sum(mm(spread3(rows_ref[pl.ds(3,1),:]),we[...],NT),axis=0,keepdims=True)
        pre=pre_ref[0:1,:]
        sg=1.0/(1.0+jnp.exp(-pre))
        rows_ref[pl.ds(2,1),:]=gh*(sg*(1.0+pre*(1.0-sg)))
def attn_finish(me,info,att,ga,pre,first,pieces,p0,np_,C):
    L,D=ga.shape; nt=L//C
    ins,scratch=bwd_specs(*att,p0,0)
    outs=[sds((3,L,128*np_),BF)]+[sds((C,D),BF)]*nt+[sds((8,D),F32)]
    return pl.pallas_call(functools.partial(finish_kernel,p0,nt),grid=(np_,),
      in_specs=[smem(),smem()]+ins+[anyw(),pl.BlockSpec((8,D),lambda i:(0,0)),anyw()]+[anyw()]*8,
      out_specs=[pl.BlockSpec((3,L,128),lambda p:(0,0,p))]+[once(o) for o in outs[1:]],out_shape=outs,
      scratch_shapes=scratch+[pltpu.VMEM((L,D),F32),pltpu.VMEM((L,3*D),BF),pltpu.VMEM((D,3*D),BF),pltpu.VMEM((D,D),BF)]+[pltpu.SemaphoreType.DMA((1,))],
      compiler_params=pltpu.CompilerParams(vmem_limit_bytes=60*2**20),
      cost_estimate=bwd_cost(L,np_),
      name="attn_finish")(me,info,*att,ga,pre,first,*pieces)
STEP=1024
MROWS=512
def weight_kernel(nc,unit,me_ref,inp_ref,rows_ref,hid_ref,feat_ref,dvec_ref,dupb_ref,*rest):
    grads=rest[:nc]
    mine_ref,theirs_ref,acc=rest[nc:]
    i=pl.program_id(0); me=me_ref[0]
    D=inp_ref.shape[1]; n=D//8; rows=feat_ref.shape[1]; ns=rows//8
    def to(t): return mine_ref if t<4 else theirs_ref
    @pl.when(i==0)
    def _():
        acc[:,3*D:]=mm(three(hid_ref[...]),spread3(rows_ref[3:4,:]),TN)
        total=8*unit; FF=dupb_ref.shape[1]
        r=lax.broadcasted_iota(jnp.int32,(SMALL,D),0)
        vec=dvec_ref[...]
        for at,row in ((Q_B,0),(V_B,1),(STAMP_B,2),(EMBED_B,3)):
            vec=jnp.where(r==at,rows_ref[row:row+1,:],vec)
        vec=jnp.broadcast_to(vec[None],(total,SMALL,D)).reshape(rows,D)
        vec=jnp.where(owned(owner_of(rows,me,unit,D),D//total),vec,0.0).astype(BF)
        vec=mm(vec,repeats(D,D//total),NT)
        own=owner_of(rows,me,unit,128).reshape(total,SMALL,128)[:,0,:1]
        ups=jnp.where(owned(jnp.broadcast_to(own,(total,FF)),FF//total),dupb_ref[...],0.0).astype(BF)
        ups=mm(ups,repeats(FF,FF//total),NT)
        line=jnp.bitwise_and(lax.broadcasted_iota(jnp.int32,(rows,128),0),SMALL-1)
        ups=jnp.broadcast_to(ups[:,None,:],(total,SMALL,128)).reshape(rows,128)
        vec=jnp.where(line==UP_B,ups,jnp.where((line>=4)&(line<UP_B),vec,0.0))
        small=mm(three(feat_ref[...]),spread3(rows_ref[2:3,:]),TN)
        small=small+jnp.concatenate([vec,jnp.zeros((rows,D-128),F32)],axis=1)
        small=small.astype(BF)
        for t in range(8): to(t)[t%4,4*n:,:]=small[t*ns:(t+1)*ns]
    part=mm(inp_ref[...],jnp.concatenate([s[w] for w in range(3) for s in grads],axis=1),TN)
    @pl.when(i==0)
    def _(): acc[:,:3*D]=part
    @pl.when(i>0)
    def _(): acc[:,:3*D]+=part
    @pl.when(i==pl.num_programs(0)-1)
    def _():
        for t in range(8):
            for w in range(4): to(t)[t%4,w*n:(w+1)*n,:]=acc[rows_at(me,t,n),w*D:(w+1)*D].astype(BF)
def weight_grads(me,inp,rows,hid,feat,dvec,dupb,grads,unit):
    L,D=inp.shape; R=min(STEP,L); n=D//8; nc=len(grads)
    outs=[sds((4,4*n+feat.shape[1]//8,D),BF)]*2
    full=lambda a: pl.BlockSpec(a.shape,lambda i:(0,)*a.ndim)
    return pl.pallas_call(functools.partial(weight_kernel,nc,unit),grid=(L//R,),
      in_specs=[smem(),pl.BlockSpec((R,D),lambda i:(i,0))]+[full(a) for a in (rows,hid,feat,dvec,dupb)]+[pl.BlockSpec((3,R,a.shape[2]),lambda i:(0,i,0)) for a in grads],
      out_specs=[once(o) for o in outs],out_shape=outs,
      scratch_shapes=[pltpu.VMEM((D,4*D),F32)],
      compiler_params=pltpu.CompilerParams(vmem_limit_bytes=60*2**20),
      cost_estimate=pl.CostEstimate(flops=2*L*D*D*3,bytes_accessed=12_000_000,transcendentals=0),
      name="weight_grads")(me,inp,rows,hid,feat,dvec,dupb,*grads)
LB=384
def room(rows): return (60 if rows>512 else 20)*2**20
def take(k,R): return pl.BlockSpec((1,R,LB),lambda i:(k,0,i))
def flat(R): return pl.BlockSpec((R,LB),lambda i:(0,i))
def total_of(refs):
    out=refs[0].astype(F32)
    for r in refs[1:]: out=out+r.astype(F32)
    return out
def three_kernel(a1,b1,a2,b2,a3,b3,o1,o2,o3):
    for a,b,o in ((a1,b1,o1),(a2,b2,o2),(a3,b3,o3)): o[...]=total_of((a[0],b[0])).astype(BF)
def sum_three(mine,got):
    _,R,D=mine.shape
    return pl.pallas_call(three_kernel,grid=(D//LB,),in_specs=[take(1,R)]*2+[take(2,R)]*2+[take(3,R)]*2,
      out_specs=[flat(R)]*3,out_shape=[sds((R,D),BF)]*3,compiler_params=pltpu.CompilerParams(vmem_limit_bytes=room(R)),name="sum_three")(mine,got,mine,got,mine,got)
def inner_rows(scr,tmp,sizes,unit,k):
    at=0; out=0
    for count,size in sizes:
        for c in range(count):
            tmp[out:out+size,:]=scr[pl.ds(pl.multiple_of(at+k*size,8),size),:]
            at+=unit*size; out+=size
    return tmp[...]
def own_kernel(sizes,unit,nx,inner_ref,a,b,*rest):
    more=rest[:nx]; keep,send,scr,tmp=rest[nx:]
    scr[...]=total_of((a[0],b[0])+tuple(x[...] for x in more))
    for j in range(unit):
        dst=send if j%2 else keep
        dst[j//2]=inner_rows(scr,tmp,sizes,unit,jnp.bitwise_xor(inner_ref[0],j)).astype(dst.dtype)
def sum_own(inner,mine,got,more,sizes,unit):
    _,R,D=mine.shape; rows=R//unit
    if any(size%8 for _,size in sizes):
        x=mine[0].astype(F32)+got[0].astype(F32)+sum(m.astype(F32) for m in more); at=0; parts=[]
        for count,size in sizes:
            for c in range(count):
                parts.append(x[at:at+unit*size].reshape(unit,size,D)); at+=unit*size
        x=in_order(jnp.concatenate(parts,1),inner)
        return jnp.stack([x[j] for j in range(0,unit,2)]),jnp.stack([x[j] for j in range(1,unit,2)]).astype(BF)
    blk=pl.BlockSpec((unit//2,rows,LB),lambda i:(0,0,i))
    keep,send=pl.pallas_call(functools.partial(own_kernel,sizes,unit,len(more)),grid=(D//LB,),
      in_specs=[smem()]+[take(0,R)]*2+[flat(R)]*len(more),out_specs=[blk]*2,
      out_shape=[sds((unit//2,rows,D),F32),sds((unit//2,rows,D),BF)],scratch_shapes=[pltpu.VMEM((R,LB),F32),pltpu.VMEM((rows,LB),F32)],compiler_params=pltpu.CompilerParams(vmem_limit_bytes=room(R)),name="sum_own")(inner.reshape(1).astype(jnp.int32),mine,got,*more)
    return keep,send
def direct_kernel(sizes,unit,nx,inner_ref,a,b,*rest):
    more=rest[:nx]; outs=rest[nx:nx+unit]; scr,tmp=rest[nx+unit:]
    scr[...]=total_of((a[0],b[0])+tuple(x[...] for x in more))
    for j,dst in enumerate(outs):
        dst[...]=inner_rows(scr,tmp,sizes,unit,jnp.bitwise_xor(inner_ref[0],j)).astype(dst.dtype)
def sum_direct(inner,mine,got,more,sizes,unit):
    _,R,D=mine.shape; rows=R//unit
    if any(size%8 for _,size in sizes):
        x=mine[0].astype(F32)+got[0].astype(F32)+sum(m.astype(F32) for m in more); at=0; parts=[]
        for count,size in sizes:
            for c in range(count):
                parts.append(x[at:at+unit*size].reshape(unit,size,D)); at+=unit*size
        x=in_order(jnp.concatenate(parts,1),inner)
        return [x[0]]+[x[j].astype(BF) for j in range(1,unit)]
    return pl.pallas_call(functools.partial(direct_kernel,sizes,unit,len(more)),grid=(D//LB,),
      in_specs=[smem()]+[take(0,R)]*2+[flat(R)]*len(more),out_specs=[flat(rows)]*unit,
      out_shape=[sds((rows,D),F32)]+[sds((rows,D),BF)]*(unit-1),scratch_shapes=[pltpu.VMEM((R,LB),F32),pltpu.VMEM((rows,LB),F32)],
      compiler_params=pltpu.CompilerParams(vmem_limit_bytes=room(R)),name="sum_direct")(inner.reshape(1).astype(jnp.int32),mine,got,*more)
def last1_kernel(ng,*refs):
    x=total_of([r[...] for r in refs[:ng]]); outs=refs[ng:]
    *mats,st=outs[:5]; n=mats[0].shape[0]
    for w,o in enumerate(mats): o[...]=x[w*n:(w+1)*n]
    st[...]=x[4*n:4*n+st.shape[0]]
    for r,o in enumerate(outs[5:]):
        o[...]=x[4*n+4+r:4*n+5+r,:o.shape[0]].reshape(o.shape)
def last1(given,n,stamp_rows,sizes):
    D=given[0].shape[1]
    vm=pl.BlockSpec(memory_space=pltpu.VMEM)
    outs=[sds((n,D),F32)]*4+[sds((stamp_rows,D),F32)]+[sds((k,),F32) for k in sizes]
    if n%8:
        x=sum(g.astype(F32) for g in given)
        return [x[w*n:(w+1)*n] for w in range(4)]+[x[4*n:4*n+stamp_rows]]+[x[4*n+4+r,:k] for r,k in enumerate(sizes)]
    return pl.pallas_call(functools.partial(last1_kernel,len(given)),in_specs=[vm]*len(given),out_specs=[vm]*len(outs),out_shape=outs,
      compiler_params=pltpu.CompilerParams(vmem_limit_bytes=12*2**20),name="last_attn")(*given)
def last2_kernel(keep_ref,got_ref,wo,wd,wu):
    x=keep_ref[...]+got_ref[...].astype(F32); n,D=wo.shape; m=wd.shape[0]
    wo[...]=x[:n]; wd[...]=x[n:n+m]
    for c in range(wu.shape[1]//D): wu[:,c*D:(c+1)*D]=x[n+m+c*n:n+m+(c+1)*n]
def last2(keep,got,n,m,FF):
    D=keep.shape[1]
    vm=pl.BlockSpec(memory_space=pltpu.VMEM)
    outs=[sds((n,D),F32),sds((m,D),F32),sds((n,FF),F32)]
    if n%8:
        x=keep+got.astype(F32)
        return x[:n],x[n:n+m],jnp.concatenate([x[n+m+c*n:n+m+(c+1)*n] for c in range(FF//D)],1)
    return pl.pallas_call(last2_kernel,in_specs=[vm]*2,out_specs=[vm]*3,out_shape=outs,compiler_params=pltpu.CompilerParams(vmem_limit_bytes=12*2**20),name="last_ffn")(keep,got)

INV_SQRT2=0.7071067811865476; INV_SQRT2PI=0.3989422804014327
HEAD=64
RB=256; FC=768
def norm_stats(x):
    mu=jnp.mean(x,axis=1,keepdims=True); c=x-mu
    r=lax.rsqrt(jnp.mean(c*c,axis=1,keepdims=True)+1e-5)
    return c*r,r
def norm_back(e,n,r):
    return r*(e-jnp.mean(e,axis=1,keepdims=True)-n*jnp.mean(e*n,axis=1,keepdims=True))
def colsum(x): return jnp.sum(x,axis=0,keepdims=True)
def mid_kernel(nblk,me_ref,info_ref,mix_ref,cot_refs,att_refs,vec_ref,upb_ref,pieces,
        out_refs,gas_ref,gatt_ref,auxd_ref,mine_ref,theirs_ref,dvec_ref,dupb_ref,
        wo,wd,wu,cot,res,atta,hida,gda,gba,gel,gup,dgel,sems):
    i=pl.program_id(0); nb=pl.num_programs(0)
    D=wo.shape[0]; FF=wd.shape[0]; ro=D//nblk; rd=FF//nblk
    me=me_ref[0]
    lower=[p[0] if isinstance(p,tuple) else p for p in pieces]
    upper=[(p[1],0) if isinstance(p,tuple) else (p,ro+rd) for p in pieces]
    cps=[load_weights(me,lower,0,ro,wo,sems.at[0]),
        [pltpu.make_async_copy(p.at[pl.ds(at+b*ro,ro),:],wu.at[rows_at(me,t,ro),pl.ds(b*D,D)],sems.at[1])
            for b in range(FF//D) for t,(p,at) in enumerate(upper)],
        load_weights(me,lower,ro,rd,wd,sems.at[2])]
    cps[0]+=[pltpu.make_async_copy(src,cot.at[c],sems.at[0]) for c,src in enumerate(cot_refs)]
    def wait(which):
        @pl.when(i==0)
        def _():
            for c in cps[which]: c.wait()
    @pl.when(i==0)
    def _():
        for w in cps:
            for c in w: c.start()
        dvec_ref[...]=jnp.zeros_like(dvec_ref); dupb_ref[...]=jnp.zeros_like(dupb_ref)
    vec=lambda r: vec_ref[pl.ds(r,1),:].astype(F32)
    nlive=info_ref[i,1]
    x0=mix_ref[...]
    live=(lax.broadcasted_iota(jnp.int32,(RB,1),0)<nlive).astype(F32)
    wait(0)
    att=jnp.concatenate([a[...] for a in att_refs],axis=1)
    rows=pl.ds(pl.multiple_of(i*RB,RB),RB)
    atta[rows,:]=att
    asum=x0+(mm(att,wo[...],NN)+vec(OUT_B))
    n1,r1=norm_stats(asum)
    normed=n1*vec(ATT_G)+vec(ATT_S)
    hid=normed.astype(BF)
    hida[rows,:]=hid
    wait(1); wait(2)
    down=None
    for f in range(FF//FC):
        c=slice(f*FC,(f+1)*FC)
        u=mm(hid,wu[:,c],NN)+upb_ref[:,c].astype(F32)
        ph=0.5+0.5*lax.erf(u*INV_SQRT2)
        pd=jnp.exp(u*u*-0.5)*INV_SQRT2PI
        g=(u*ph).astype(BF)
        gel[rows,c]=g
        dgel[:,c]=ph+u*pd
        t=mm(g,wd[c,:],NN)
        down=t if down is None else down+t
    fsum=normed+(down+vec(DOWN_B))
    n2,r2=norm_stats(fsum)
    g2=vec(FFN_G)
    res[i]=((n2*g2+vec(FFN_S))*live).astype(BF)
    og=cot[i].astype(F32)*live
    dvec_ref[pl.ds(FFN_G,1),:]+=colsum(og*n2)
    dvec_ref[pl.ds(FFN_S,1),:]+=colsum(og)
    gf=norm_back(og*g2,n2,r2)
    gd=gf.astype(BF)
    gda[rows,:]=gd
    dvec_ref[pl.ds(DOWN_B,1),:]+=colsum(gd.astype(F32))
    gn=gf
    for f in range(FF//FC):
        c=slice(f*FC,(f+1)*FC)
        gu=(mm(gd,wd[c,:],NT)*dgel[:,c]).astype(BF)
        dupb_ref[:,c]+=colsum(gu.astype(F32))
        gup[rows,c]=gu
        gn=gn+mm(gu,wu[:,c],NT)
    dvec_ref[pl.ds(ATT_G,1),:]+=colsum(gn*n1)
    dvec_ref[pl.ds(ATT_S,1),:]+=colsum(gn)
    ga=norm_back(gn*vec(ATT_G),n1,r1)
    gas_ref[...]=ga
    gb=ga.astype(BF)
    dvec_ref[pl.ds(OUT_B,1),:]+=colsum(gb.astype(F32))
    gba[rows,:]=gb
    gatt=mm(gb,wo[...],NT).astype(BF)
    gatt_ref[...]=gatt
    pr=-(gatt.astype(F32)*att.astype(F32))
    hi,mid,lo=split3(pr)
    hrow=lax.broadcasted_iota(jnp.int32,(D,128),0)//64
    hcol=lax.broadcasted_iota(jnp.int32,(D,128),1)
    ind=((hcol>=3*hrow)&(hcol<3*hrow+3)).astype(BF)
    dl=mm(hi.astype(BF),ind,NN)+mm(mid.astype(BF),ind,NN)
    h2,m2,l2=split3(dl)
    ln=lanes(dl.shape)%3
    auxd_ref[...]=jnp.where(ln==0,h2,jnp.where(ln==1,m2,l2)).astype(BF)
    @pl.when(i==nb-1)
    def _():
        def send(src,at,n):
            cps=[pltpu.make_async_copy(src.at[rows_at(me,t,n),:],(mine_ref if t<4 else theirs_ref).at[t%4,pl.ds(at,n),:],sems.at[3]) for t in range(8)]
            for c in cps: c.start()
            return cps
        out=[pltpu.make_async_copy(res.at[c],dst,sems.at[3]) for c,dst in enumerate(out_refs)]
        for c in out: c.start()
        for b in range(FF//D):
            c=slice(b*D,(b+1)*D)
            wd[c,:]=mm(gel[:,c],gda[...],TN).astype(BF)
        out+=send(wd,ro,rd)
        wo[...]=mm(atta[...],gba[...],TN).astype(BF)
        out+=send(wo,0,ro)
        for b in range(FF//D):
            c=slice(b*D,(b+1)*D)
            wu[:,c]=mm(hida[...],gup[:,c],TN).astype(BF)
            out+=send(wu.at[:,pl.ds(b*D,D)],ro+rd+b*ro,ro)
        for c in out: c.wait()
def middle(me,info,mixed,cots,atts,vec,upb,pieces):
    nblk=8; L,D=mixed.shape; FF=upb.shape[1]; ro=D//8; rd=FF//8
    nb=L//RB; na=len(atts); nt=len(cots)
    flat_pieces=jax.tree.leaves(pieces)
    def kern(me_ref,info_ref,mix_ref,*rest):
        cot=rest[:nt]; att=rest[nt:nt+na]; rest=rest[nt+na:]
        given=iter(rest[2:2+len(flat_pieces)])
        blocks=[(next(given),next(given)) if isinstance(p,tuple) else next(given) for p in pieces]
        rest_out=rest[2+len(flat_pieces):]
        mid_kernel(nblk,me_ref,info_ref,mix_ref,cot,att,rest[0],rest[1],blocks,rest_out[:nt],*rest_out[nt:])
    full=lambda a: pl.BlockSpec(a.shape,lambda i:(0,)*a.ndim)
    row=pl.BlockSpec((RB,D),lambda i:(i,0))
    outs=[sds((RB,D),BF)]*nt+[sds((L,D),F32),sds((L,D),BF),sds((L,128),BF)]+[sds((4,)+pieces[0].shape,BF)]*2+[sds((16,D),F32),sds((1,FF),F32)]
    return pl.pallas_call(kern,grid=(nb,),
      in_specs=[smem(),smem(),row]+[anyw()]*nt+[pl.BlockSpec((RB,a.shape[1]),lambda i:(i,0)) for a in atts]+[full(vec),full(upb)]+[anyw()]*len(flat_pieces),
      out_specs=[anyw()]*nt+[row,row,pl.BlockSpec((RB,128),lambda i:(i,0)),anyw(),anyw()]+[once(s) for s in outs[nt+5:]],
      out_shape=outs,
      scratch_shapes=[pltpu.VMEM((D,D),BF),pltpu.VMEM((FF,D),BF),pltpu.VMEM((D,FF),BF),
        pltpu.VMEM((nt,RB,D),BF),pltpu.VMEM((nt,RB,D),BF)]+[pltpu.VMEM((L,D),BF)]*4+[pltpu.VMEM((L,FF),BF)]*2+[
        pltpu.VMEM((RB,FF),F32),pltpu.SemaphoreType.DMA((4,))],
      compiler_params=pltpu.CompilerParams(vmem_limit_bytes=61*2**20),
      cost_estimate=pl.CostEstimate(flops=2*L*D*(3*D+6*FF),bytes_accessed=60_000_000,transcendentals=2*L*FF),
      name="middle")(me,info,mixed,*cots,*atts,vec,upb,*flat_pieces)

GROUPS=8
AXES=("seq","stream")
def flip(x,mask,total):
    return lax.ppermute(x,AXES,[(i,i^mask) for i in range(total)])
def far_first(count):
    bits=[]; bit=count//2
    while bit: bits.append(bit); bit//=2
    return bits
def widen(x,bit,total): return jnp.concatenate([x,flip(x,bit,total)])
def settle(x,inner,count):
    ids=[0]
    for bit in far_first(count): ids=ids+[i^bit for i in ids]
    return in_order(jnp.stack([x[ids.index(k)] for k in range(count)]),inner)
def in_order(x,index):
    n=x.shape[0]; bit=1
    while bit<n:
        turned=jnp.concatenate([x[k^bit][None] for k in range(n)])
        x=jnp.where((index&bit)!=0,turned,x); bit*=2
    return x
def after(x,*deps):
    return lax.optimization_barrier((x,)+deps)[0]
def sync(*xs): return lax.optimization_barrier(xs)
def spread_start(own,unit,total):
    across=lambda x,g: flip(x,g*unit,total)
    return [own,across(own,2),across(own,4)]
def split_send(x,bit,total):
    send=jnp.stack([x[j] for j in range(1,x.shape[0],2)]).astype(BF)
    return jnp.stack([x[j] for j in range(0,x.shape[0],2)]),flip(send,bit,total)
def finish2(keep,got,total):
    bit=2
    while keep.shape[0]>1:
        keep,got=split_send(keep+got.astype(F32),bit,total); bit*=2
    return keep[0],got[0]
def on_device(tokens,source_len,target_len,timesteps,cotangent,query_weight,query_bias,key_weight,value_weight,value_bias,
        out_weight,out_bias,attn_gain,attn_shift,up_weight,up_bias,down_weight,down_bias,ffn_gain,ffn_shift,
        stamp_weight,stamp_bias,embed_weight,embed_bias):
    seqs,R,D=tokens.shape
    streams=lax.axis_size("stream"); seq_size=lax.axis_size("seq"); total=seq_size*streams
    s0=lax.axis_index("stream"); flat=lax.axis_index("seq")*streams+s0
    unit=total//GROUPS
    inner=flat%unit; group=flat//unit
    me=group.astype(jnp.int32).reshape(1)
    n=D//GROUPS; shard=D//total; stamp_rows=stamp_weight.shape[0]; FF=up_weight.shape[1]; ff_shard=FF//total
    vecs=(query_bias,value_bias,out_bias,attn_gain,attn_shift,down_bias,ffn_gain,ffn_shift,stamp_bias,embed_bias,up_bias)
    first,second=pack((query_weight,key_weight,value_weight,embed_weight,stamp_weight,out_weight,down_weight,up_weight),vecs)
    def rowwise(x,sizes):
        at=0; out=[]
        for count,size in sizes:
            part=x[:,at:at+count*size].reshape(unit,count,size,x.shape[2])
            out.append(part.transpose(1,0,2,3).reshape(count*unit*size,x.shape[2])); at+=count*size
        return jnp.concatenate(out) if len(out)>1 else out[0]
    def exchange(chunks):
        return [x if c==0 else flip(x,c,total) for c,x in enumerate(chunks)]
    def chunks_of(x): return [lax.dynamic_index_in_dim(x,s0^c,0,keepdims=False) for c in range(streams)]
    order=jnp.asarray(ORDER,jnp.int32)
    source=source_len[s0]; target=target_len[s0]; stamp=timesteps[s0]
    half=R*streams//2
    place=(s0^jnp.arange(streams))*R
    flag=(place>=half).astype(jnp.int32)
    nlive=jnp.clip(jnp.where(flag==1,target-(place-half),source-place),0,R).astype(jnp.int32)
    info=jnp.stack([flag,nlive],1)
    tdim=stamp_rows*total; halfway=tdim//2
    t_ids=(((order^group)[:,None,None]*unit+jnp.arange(unit)[None,:,None])*stamp_rows+jnp.arange(SMALL)[None,None,:])
    valid=(jnp.arange(SMALL)<stamp_rows)[None,None,:]
    t_ids=jnp.where(valid,t_ids,0).reshape(-1)
    rates=jnp.exp(-math.log(10000.0)*(t_ids%halfway).astype(F32)/halfway)
    angle=stamp.astype(F32)*rates
    feats=jnp.where(t_ids<halfway,jnp.sin(angle),jnp.cos(angle))
    feats=jnp.where(jnp.broadcast_to(valid,(GROUPS,unit,SMALL)).reshape(-1),feats,0.0)
    feat=jnp.broadcast_to(feats.astype(BF)[None],(8,feats.shape[0]))
    bits=far_first(unit)
    first=widen(first[None],bits[0],total)
    first,second=sync(first,second)
    second=widen(second[None],bits[0],total)
    for bit in bits[1:]: first=widen(first,bit,total)
    first=rowwise(settle(first,inner,unit),((4,shard),(1,SMALL)))
    cells=chunks_of(tokens)
    first,second,feat,info,*cells=sync(first,second,feat,info,*cells)
    for bit in bits[1:]: second=widen(second,bit,total)
    n1=[first]+[flip(first,g*unit,total) for g in (2,4,6)]
    toks=[cells[0]]+[None]*(streams-1)
    early,late=list(range(2,streams)),[1]
    for c in early: toks[c]=flip(cells[c],c,total)
    n1[1],n1[2],toks[2],second=sync(n1[1],n1[2],toks[2],second)
    second=rowwise(settle(second,inner,unit),((1,shard),(1,ff_shard),(FF//D,shard)))
    for c in late: toks[c]=flip(after(cells[c],second),c,total)
    n2=spread_start(second,unit,total)
    p1=n1+[flip(x,unit,total) for x in n1]
    *cells,_=sync(*chunks_of(cotangent),toks)
    far=[flip(n2[0],unit,total)]
    cots=[cells[0]]+[flip(cells[c],c,total) for c in range(1,streams-1)]
    mixed,inputs,q,k,v,auxk,pre,hid,vec,upb=project(me,info,feat,toks,p1,unit,FF)
    pairs=D//(2*HEAD); parts=(2,pairs-2)
    atts=[];auxq=[]
    def forward(c,q):
        a,x=attn_fwd(q,k,v,auxk,sum(parts[:c]),parts[c]); atts.append(a); auxq.append(x)
    forward(0,q)
    q,n2,far,cots,cells,atts=sync(q,n2,far,cots,cells,atts)
    cut=n+FF//GROUPS
    low=flip(n2[2][:cut],2*unit,total); high=flip(n2[1][cut:],4*unit,total)
    cots.append(flip(cells[streams-1],streams-1,total))
    far+=[flip(n2[1],unit,total),flip(n2[2],unit,total)]
    forward(1,q)
    low,high,far,atts,cots=sync(low,high,far,atts,cots)
    diag=(low,high)
    p2=n2+[diag]+far+[tuple(flip(x,unit,total) for x in diag)]
    *output,ga,gatt,auxd,mine2,theirs2,dvec,dupb=sync(*middle(me,info,mixed,cots,atts,vec,upb,p2))
    grads=[]
    def backward(c,q):
        grads.append(attn_bwd(q,k,v,gatt,auxk,auxq[c],auxd,sum(parts[:c]),parts[c],0))
    got=flip(theirs2,unit,total)
    backs=[output[0],flip(output[1],1,total)]
    backward(0,q)
    got,q,output,backs,grads=sync(got,q,output,backs,grads)
    fx,fy,fd=(flip(x,g*unit,total) for x,g in zip(sum_three(mine2,got),(2,4,6)))
    backs+=[flip(output[c],c,total) for c in range(2,streams)]
    out,*tg,rows4=attn_finish(me,info,(q,k,v,gatt,auxk,auxq[1],auxd),ga,pre,grads[0],p1,parts[0],parts[1],R)
    grads.append(out)
    def place(chunks,dtype):
        out=jnp.zeros((seqs,R,D),dtype)
        for c,part in enumerate(chunks):
            out=lax.dynamic_update_index_in_dim(out,part.astype(dtype),s0^c,0)
        return out
    tg,rows4,backs=sync(tg,rows4,backs)
    held=[flip(tg[c],c,total) for c in range(1,streams-1)]
    mine1,theirs1=weight_grads(me,inputs,rows4,hid,feat,dvec,dupb,grads,unit)
    mine1,theirs1,fx,fy,fd,held=sync(mine1,theirs1,fx,fy,fd,held)
    keep2,send2=sum_own(inner,mine2,got,(fx,fy,fd),((1,shard),(1,ff_shard),(FF//D,shard)),unit)
    got1=flip(theirs1,unit,total)
    keep2,send2,tg=sync(keep2,send2,tg)
    got2=flip(send2,1,total)
    tgs=[tg[0]]+held+[flip(tg[streams-1],streams-1,total)]
    blocks=sum_three(mine1,got1)
    fx,fy,fd=(flip(x,g*unit,total) for x,g in zip(blocks,(2,4,6)))
    keep2,got2=finish2(keep2,got2,total)
    fx,fy,fd,keep2,got2,tgs=sync(fx,fy,fd,keep2,got2,tgs)
    output=place(backs,BF)
    dwo,dwd,dwu=last2(keep2,got2,shard,ff_shard,FF)
    keep1,*sends=sum_direct(inner,mine1,got1,(fx,fy,fd),((4,shard),(1,SMALL)),unit)
    given=[keep1]+[flip(x,c+1,total) for c,x in enumerate(sends)]
    dwq,dwk,dwv,dwe,dws,bq,bv,bo,ag,as_,bd,fg,fs,bs,be,bu=last1(given,shard,stamp_rows,[shard]*10+[ff_shard])
    token_grad=place(tgs,F32)
    return (output,token_grad,dwq,bq,dwk,dwv,bv,dwo,bo,ag,as_,dwu,bu,dwd,bd,fg,fs,dws,bs,dwe,be)

def solution(mesh):
    cells=P("seq","stream",None); per=P("seq"); mat=P(("seq","stream"),None); row=P(("seq","stream"))
    return jax.shard_map(on_device,mesh=mesh,
        in_specs=(cells,per,per,per,cells,mat,row,mat,mat,row,mat,row,row,row,mat,row,mat,row,row,row,mat,row,mat,row),
        out_specs=(cells,cells,mat,row,mat,mat,row,mat,row,row,row,mat,row,mat,row,row,row,mat,row,mat,row),
        check_vma=False)
```

```python
import functools
import math

import jax
import jax.numpy as jnp
from jax import lax
from jax.experimental import pallas as pl
from jax.experimental.pallas import tpu as pltpu
from jax.sharding import PartitionSpec as P

F32=jnp.float32; BF=jnp.bfloat16
NT=(((1,),(1,)),((),())); NN=(((1,),(0,)),((),())); TN=(((0,),(0,)),((),()))
def mm(a,b,dims): return lax.dot_general(a,b,dims,preferred_element_type=F32)
def lanes(shape): return lax.broadcasted_iota(jnp.int32,shape,len(shape)-1)
def split3(x):
    hi=x.astype(BF).astype(F32); r=x-hi
    mid=r.astype(BF).astype(F32); lo=r-mid
    return hi,mid,lo
QB=256
def fwd_kernel(q_ref,k_ref,v_ref,auxk_ref,o_ref,auxq_ref,kaug,vm):
    L=q_ref.shape[0]
    k=k_ref[...]; v=v_ref[...]; ln=lanes(k.shape)
    for e in range(2):
        sel=(ln<64) if e==0 else (ln>=64)
        kaug[e,:,:128]=jnp.where(sel,k,jnp.zeros_like(k))
        kaug[e,:,128:]=auxk_ref[...]
        vm[e]=jnp.where(sel,v,(ln==64*(1-e)).astype(BF))
    ln=lanes((QB,128)); one=jnp.where(ln==64,1.0,0.0).astype(BF)
    steps=[(b,e) for b in range(L//QB) for e in range(2)]
    def score(b,e):
        return mm(jnp.concatenate([q_ref[pl.ds(b*QB,QB),:],one],axis=1),kaug[e],NT)
    s=score(*steps[0]); out=None; aux=None
    for t,(b,e) in enumerate(steps):
        later=score(*steps[t+1]) if t+1<len(steps) else None
        m=jnp.max(s,axis=1,keepdims=True)
        p=jnp.exp(s-m).astype(BF)
        o=mm(p,vm[e],NN)
        l=o[:,64*(1-e):64*(1-e)+1]
        o=jnp.where((ln<64) if e==0 else (ln>=64),o*(1.0/l),0.0)
        hi,mid,lo=split3(-(m+jnp.log(l)))
        if e==0: out=o; aux=jnp.where(ln==64,1.0,0.0)
        else: out=out+o
        aux=jnp.where(ln==3*e,hi,aux); aux=jnp.where(ln==3*e+1,mid,aux); aux=jnp.where(ln==3*e+2,lo,aux)
        if e==1:
            r=pl.ds(b*QB,QB)
            o_ref[r,:]=out.astype(BF); auxq_ref[0,r,:]=aux.astype(BF)
        s=later
def attn_fwd(q,k,v,auxk,p0,np_):
    L=q.shape[0]
    col=lambda: pl.BlockSpec((L,128),lambda p:(0,p0+p))
    return pl.pallas_call(fwd_kernel,grid=(np_,),
      in_specs=[col(),col(),col(),pl.BlockSpec((L,128),lambda p:(0,0))],
      out_specs=[pl.BlockSpec((L,128),lambda p:(0,p)),pl.BlockSpec((1,L,128),lambda p:(p,0,0))],
      out_shape=[jax.ShapeDtypeStruct((L,128*np_),BF),jax.ShapeDtypeStruct((np_,L,128),BF)],
      scratch_shapes=[pltpu.VMEM((2,L,256),BF),pltpu.VMEM((2,L,128),BF)],
      compiler_params=pltpu.CompilerParams(vmem_limit_bytes=60*2**20),
      cost_estimate=pl.CostEstimate(flops=np_*2*L*L*64*4,bytes_accessed=np_*L*128*2*5,transcendentals=np_*2*L*L),
      name="attn_fwd")(q,k,v,auxk)
def bwd_pair(p0,q_ref,k_ref,v_ref,do_ref,auxk_ref,auxq_ref,auxd_ref,out_ref,kaug,vaug,qa,doa,qm,dom,dk_acc,dv_acc):
    pair=p0+pl.program_id(0)
    L=q_ref.shape[0]
    k=k_ref[...]; v=v_ref[...]; q=q_ref[...]; do=do_ref[...]
    ln=lanes(k.shape); z=jnp.zeros_like(k); auxk=auxk_ref[...]
    qa[:,:128]=q; qa[:,128:]=auxq_ref[0]
    doa[:,:128]=do; doa[:,128:]=auxd_ref[...]
    for e in range(2):
        sel=(ln<64) if e==0 else (ln>=64)
        on=(ln>=3*e)&(ln<3*e+3)
        kaug[e,:,:128]=jnp.where(sel,k,z)
        kaug[e,:,128:]=jnp.where(on,jnp.ones_like(k),auxk)
        vaug[e,:,:128]=jnp.where(sel,v,z)
        b=6*pair+3*e
        vaug[e,:,128:]=jnp.where((ln>=b)&(ln<b+3),jnp.ones_like(k),z)
        qm[e]=jnp.where(sel,q,z)
        dom[e]=jnp.where(sel,do,z)
    for i in range(L//QB):
        r=pl.ds(i*QB,QB)
        dq=None
        for e in range(2):
            p=jnp.exp(mm(kaug[e],qa[r,:],NT))
            dp=mm(vaug[e],doa[r,:],NT)
            ds=(p*dp).astype(BF)
            dv=mm(p.astype(BF),dom[e,r,:],NN)
            dk=mm(ds,qm[e,r,:],NN)
            if i==0 and e==0: dv_acc[...]=dv; dk_acc[...]=dk
            else: dv_acc[...]+=dv; dk_acc[...]+=dk
            d=mm(ds,kaug[e,:,:128],TN)
            dq=d if dq is None else dq+d
        out_ref[0,r,:]=(dq*0.125).astype(BF)
    out_ref[1]=dk_acc[...].astype(BF)
    out_ref[2]=dv_acc[...].astype(BF)
def bwd_specs(q,k,v,do,auxk,auxq,auxd,p0,a0):
    L=q.shape[0]
    col=lambda: pl.BlockSpec((L,128),lambda p:(0,p0+p))
    con=lambda: pl.BlockSpec((L,128),lambda p:(0,0))
    return ([col(),col(),col(),col(),con(),pl.BlockSpec((1,L,128),lambda p:(a0+p,0,0)),con()],
      [pltpu.VMEM((2,L,256),BF),pltpu.VMEM((2,L,256),BF),pltpu.VMEM((L,256),BF),pltpu.VMEM((L,256),BF),
        pltpu.VMEM((2,L,128),BF),pltpu.VMEM((2,L,128),BF),pltpu.VMEM((L,128),F32),pltpu.VMEM((L,128),F32)])
def bwd_cost(L,np_): return pl.CostEstimate(flops=np_*2*L*L*64*10,bytes_accessed=np_*L*128*2*9,transcendentals=np_*2*L*L)
def attn_bwd(q,k,v,do,auxk,auxq,auxd,p0,np_,a0):
    L=q.shape[0]
    ins,scratch=bwd_specs(q,k,v,do,auxk,auxq,auxd,p0,a0)
    return pl.pallas_call(functools.partial(bwd_pair,p0),grid=(np_,),in_specs=ins,
      out_specs=pl.BlockSpec((3,L,128),lambda p:(0,0,p)),
      out_shape=jax.ShapeDtypeStruct((3,L,128*np_),BF),scratch_shapes=scratch,
      compiler_params=pltpu.CompilerParams(vmem_limit_bytes=60*2**20),
      cost_estimate=bwd_cost(L,np_),
      name="attn_bwd")(q,k,v,do,auxk,auxq,auxd)

SMALL=16; Q_B,V_B,OUT_B,ATT_G,ATT_S,DOWN_B,FFN_G,FFN_S,STAMP_B,EMBED_B=range(4,14); UP_B=14
def owner_of(rows,me,unit,width):
    r=lax.shift_right_logical(lax.broadcasted_iota(jnp.int32,(rows,width),0),SMALL.bit_length()-1)
    shift=unit.bit_length()-1
    t=lax.shift_right_logical(r,shift)
    g=jnp.bitwise_xor(jnp.bitwise_or(jnp.bitwise_and(t*2,7),lax.shift_right_logical(t,2)),me)
    return g*unit+jnp.bitwise_and(r,unit-1)
def repeats(width,shard):
    l=lax.broadcasted_iota(jnp.int32,(128,width),0).astype(F32); d=lax.broadcasted_iota(jnp.int32,(128,width),1).astype(F32)
    return (d-shard*jnp.floor((d+0.5)*(1.0/shard))==l).astype(BF)
def owned(owner,shard):
    d=lax.broadcasted_iota(jnp.int32,owner.shape,1)
    return (d>=owner*shard)&(d<owner*shard+shard)
def pack_kernel(*refs):
    *ins,first_ref,second_ref,scr=refs
    wq,wk,wv,we,st,wo,wd,wu=ins[:8]; vecs=ins[8:]
    scr[...]=jnp.zeros_like(scr)
    scr[:st.shape[0],:]=st[...]
    for r,v in enumerate(vecs):
        scr[4+r:5+r,:v.shape[0]]=v[...].reshape(1,-1)
    D=wq.shape[1]
    first_ref[...]=jnp.concatenate([wq[...],wk[...],wv[...],we[...],scr[...]],axis=0).astype(BF)
    up=[wu[:,c*D:(c+1)*D] for c in range(wu.shape[1]//D)]
    second_ref[...]=jnp.concatenate([wo[...],wd[...]]+up,axis=0).astype(BF)
def pack(mats,vecs):
    wq,wk,wv,we,st,wo,wd,wu=mats; n,D=wq.shape
    vm=pl.BlockSpec(memory_space=pltpu.VMEM)
    second=n+wd.shape[0]+n*(wu.shape[1]//D)
    if n%8:
        small=jnp.concatenate([st]+[jnp.zeros((4-st.shape[0],D),F32)]+[jnp.pad(v,(0,D-v.shape[0]))[None] for v in vecs]+[jnp.zeros((SMALL-4-len(vecs),D),F32)])
        up=[wu[:,c*D:(c+1)*D] for c in range(wu.shape[1]//D)]
        return jnp.concatenate([wq,wk,wv,we,small]).astype(BF),jnp.concatenate([wo,wd]+up).astype(BF)
    return pl.pallas_call(pack_kernel,in_specs=[vm]*(8+len(vecs)),out_specs=[vm]*2,
      out_shape=[sds((4*n+SMALL,D),BF),sds((second,D),BF)],scratch_shapes=[pltpu.VMEM((SMALL,D),F32)],compiler_params=pltpu.CompilerParams(vmem_limit_bytes=60*2**20),name="pack")(*mats,*vecs)
ORDER=(0,2,4,6,1,3,5,7)
def rows_at(me,t,n):
    return pl.ds(pl.multiple_of(jnp.bitwise_xor(me,ORDER[t])*n,n),n)
def sds(*a): return jax.ShapeDtypeStruct(*a)
def once(s): return pl.BlockSpec(s.shape,lambda i:(0,)*len(s.shape),pipeline_mode=pl.Buffered(1))
def smem(): return pl.BlockSpec(memory_space=pltpu.SMEM)
def anyw(): return pl.BlockSpec(memory_space=pl.ANY)
def load_weights(me,pieces,base,n,dst,sem):
    return [pltpu.make_async_copy(p.at[pl.ds(base,n),:],dst.at[rows_at(me,t,n),:],sem) for t,p in enumerate(pieces)]
def in_kernel(nt,unit,me_ref,info_ref,feat_ref,*rest):
    toks=rest[:nt]; pieces=rest[nt:nt+8]
    mixed_ref,inp_ref,q_ref,k_ref,v_ref,auxk_ref,pre_ref,hid_ref,vec_ref,upb_ref,tok,wq,wk,wv,we,ws,emb,sems=rest[nt+8:]
    i=pl.program_id(0); me=me_ref[0]
    D=wq.shape[0]; n=D//8; ns=ws.shape[0]//8
    tcp=[pltpu.make_async_copy(t,tok.at[c],sems.at[5+c]) for c,t in enumerate(toks)]
    scp=[pltpu.make_async_copy(p.at[pl.ds(4*n,ns),:],ws.at[pl.ds(t*ns,ns),:],sems.at[0]) for t,p in enumerate(pieces)]
    wcp=[load_weights(me,pieces,w*n,n,dst,sems.at[1+w]) for w,dst in enumerate((wq,wk,wv,we))]
    vec=lambda r: vec_ref[pl.ds(r,1),:]
    @pl.when(i==0)
    def _():
        for c in scp+wcp[3]+tcp[:1]+wcp[0]+wcp[1]+wcp[2]+tcp[1:]: c.start()
        for c in scp: c.wait()
        rows=8*ns; total=8*unit; FF=upb_ref.shape[1]
        lead=ws[:,:128]
        spread=mm(lead,repeats(D,D//total),NN)
        spread=jnp.where(owned(owner_of(rows,me,unit,D),D//total),spread,0.0)
        vec_ref[...]=jnp.sum(spread.reshape(total,SMALL,D),axis=0)
        ups=lead.astype(F32).reshape(total,SMALL,128)[:,UP_B,:].astype(BF)
        ups=mm(ups,repeats(FF,FF//total),NN)
        own=owner_of(rows,me,unit,128).reshape(total,SMALL,128)[:,0,:1]
        upb_ref[...]=jnp.sum(jnp.where(owned(jnp.broadcast_to(own,(total,FF)),FF//total),ups,0.0),axis=0,keepdims=True)
        pre=mm(feat_ref[...],ws[...],NN)+vec(STAMP_B)
        pre_ref[...]=pre
        hid=(pre/(1.0+jnp.exp(-pre))).astype(BF)
        hid_ref[...]=hid
        for c in wcp[3]: c.wait()
        emb[...]=mm(hid,we[...],NN)+vec(EMBED_B)
    for c in range(nt):
        @pl.when(i==c)
        def _(): tcp[c].wait()
    flag=info_ref[i,0].astype(F32); nlive=info_ref[i,1]
    x=tok[i].astype(F32)+flag*emb[pl.ds(0,1),:]
    mixed_ref[...]=x
    xb=x.astype(BF); inp_ref[...]=xb
    R=x.shape[0]
    ln=lanes((R,128)); row=lax.broadcasted_iota(jnp.int32,(R,128),0)
    auxk_ref[...]=jnp.where((ln==64)&(row>=nlive),-1e30,0.0).astype(BF)
    @pl.when(i==0)
    def _():
        for w in range(3):
            for c in wcp[w]: c.wait()
    q=(mm(xb,wq[...],NN)+vec(Q_B)).astype(BF)
    q_ref[...]=(q.astype(F32)*0.125).astype(BF)
    k_ref[...]=mm(xb,wk[...],NN).astype(BF)
    v_ref[...]=(mm(xb,wv[...],NN)+vec(V_B)).astype(BF)
def project(me,info,feat,toks,pieces,unit,FF):
    nt=len(toks); R,D=toks[0].shape; n=D//8; ns=pieces[0].shape[0]-4*n; L=nt*R
    row=lambda w: pl.BlockSpec((R,w),lambda i:(i,0))
    full=lambda a: pl.BlockSpec(a.shape,lambda i:(0,)*a.ndim)
    outs=[sds((L,D),F32)]+[sds((L,D),BF)]*4+[sds((L,128),BF),sds((8,D),F32),sds((8,D),BF),sds((SMALL,D),F32),sds((1,FF),F32)]
    return pl.pallas_call(functools.partial(in_kernel,nt,unit),grid=(nt,),
      in_specs=[smem(),smem(),full(feat)]+[anyw()]*(nt+8),
      out_specs=[row(D)]*5+[row(128)]+[once(o) for o in outs[6:]],
      out_shape=outs,
      scratch_shapes=[pltpu.VMEM((nt,R,D),BF)]+[pltpu.VMEM((D,D),BF)]*4+[pltpu.VMEM((8*ns,D),BF),pltpu.VMEM((8,D),F32),pltpu.SemaphoreType.DMA((5+nt,))],
      compiler_params=pltpu.CompilerParams(vmem_limit_bytes=60*2**20),
      cost_estimate=pl.CostEstimate(flops=2*L*D*D*3,bytes_accessed=20_000_000,transcendentals=0),
      name="project")(me,info,feat,*toks,*pieces)

def spread3(row):
    hi,mid,lo=split3(row)
    r=lax.broadcasted_iota(jnp.int32,(8,row.shape[1]),0)
    return jnp.where(r==0,hi,jnp.where(r==1,mid,jnp.where(r==2,lo,0.0))).astype(BF)
def three(rows):
    r=lax.broadcasted_iota(jnp.int32,rows.shape,0)
    return jnp.where(r<3,jnp.broadcast_to(rows.astype(F32)[0:1,:],rows.shape),0.0).astype(BF)
def finish_kernel(p0,nt,me_ref,info_ref,*rest):
    att=rest[:7]; ga_hbm,pre_ref,first=rest[7:10]; pieces=rest[10:18]
    out_ref=rest[18]; tg_refs=rest[19:19+nt]; rows_ref=rest[19+nt]
    *work,ga,all_grads,wqkv,we,sems=rest[20+nt:]
    i=pl.program_id(0); me=me_ref[0]
    L,D=ga.shape; n=D//8; F=first.shape[2]
    cps=[pltpu.make_async_copy(ga_hbm,ga,sems.at[0])]
    for w in range(3):
        cps.append(pltpu.make_async_copy(first.at[w],all_grads.at[:,pl.ds(w*D,F)],sems.at[0]))
        cps+=load_weights(me,pieces,w*n,n,wqkv.at[:,pl.ds(w*D,D)],sems.at[0])
    cps+=load_weights(me,pieces,3*n,n,we,sems.at[0])
    @pl.when(i==0)
    def _():
        for c in cps: c.start()
    bwd_pair(p0,*att,out_ref,*work)
    for w in range(3): all_grads[:,pl.ds(pl.multiple_of(w*D+F+i*128,128),128)]=out_ref[w]
    @pl.when(i==pl.num_programs(0)-1)
    def _():
        for c in cps: c.wait()
        rows_ref[...]=jnp.zeros_like(rows_ref)
        R=L//nt; per=max(1,MROWS//R)
        for c in range(0,nt,per):
            r=pl.ds(c*R,per*R)
            y=all_grads[r,:]
            for w in (0,2): rows_ref[pl.ds(w//2,1),:]+=jnp.sum(y[:,w*D:(w+1)*D].astype(F32),axis=0,keepdims=True)
            g=ga[r,:]+mm(y,wqkv[...],NT)
            for p in range(per):
                part=g[p*R:(p+1)*R]
                rows_ref[pl.ds(3,1),:]+=info_ref[c+p,0].astype(F32)*jnp.sum(part,axis=0,keepdims=True)
                tg_refs[c+p][...]=part.astype(BF)
        gh=jnp.sum(mm(spread3(rows_ref[pl.ds(3,1),:]),we[...],NT),axis=0,keepdims=True)
        pre=pre_ref[0:1,:]
        sg=1.0/(1.0+jnp.exp(-pre))
        rows_ref[pl.ds(2,1),:]=gh*(sg*(1.0+pre*(1.0-sg)))
def attn_finish(me,info,att,ga,pre,first,pieces,p0,np_,C):
    L,D=ga.shape; nt=L//C
    ins,scratch=bwd_specs(*att,p0,0)
    outs=[sds((3,L,128*np_),BF)]+[sds((C,D),BF)]*nt+[sds((8,D),F32)]
    return pl.pallas_call(functools.partial(finish_kernel,p0,nt),grid=(np_,),
      in_specs=[smem(),smem()]+ins+[anyw(),pl.BlockSpec((8,D),lambda i:(0,0)),anyw()]+[anyw()]*8,
      out_specs=[pl.BlockSpec((3,L,128),lambda p:(0,0,p))]+[once(o) for o in outs[1:]],out_shape=outs,
      scratch_shapes=scratch+[pltpu.VMEM((L,D),F32),pltpu.VMEM((L,3*D),BF),pltpu.VMEM((D,3*D),BF),pltpu.VMEM((D,D),BF)]+[pltpu.SemaphoreType.DMA((1,))],
      compiler_params=pltpu.CompilerParams(vmem_limit_bytes=60*2**20),
      cost_estimate=bwd_cost(L,np_),
      name="attn_finish")(me,info,*att,ga,pre,first,*pieces)
STEP=1024
MROWS=1024
def weight_kernel(nc,unit,me_ref,inp_ref,rows_ref,hid_ref,feat_ref,dvec_ref,dupb_ref,*rest):
    grads=rest[:nc]
    mine_ref,theirs_ref,acc=rest[nc:]
    i=pl.program_id(0); me=me_ref[0]
    D=inp_ref.shape[1]; n=D//8; rows=feat_ref.shape[1]; ns=rows//8
    def to(t): return mine_ref if t<4 else theirs_ref
    @pl.when(i==0)
    def _():
        acc[:,3*D:]=mm(three(hid_ref[...]),spread3(rows_ref[3:4,:]),TN)
        total=8*unit; FF=dupb_ref.shape[1]
        r=lax.broadcasted_iota(jnp.int32,(SMALL,D),0)
        vec=dvec_ref[...]
        for at,row in ((Q_B,0),(V_B,1),(STAMP_B,2),(EMBED_B,3)):
            vec=jnp.where(r==at,rows_ref[row:row+1,:],vec)
        vec=jnp.broadcast_to(vec[None],(total,SMALL,D)).reshape(rows,D)
        vec=jnp.where(owned(owner_of(rows,me,unit,D),D//total),vec,0.0).astype(BF)
        vec=mm(vec,repeats(D,D//total),NT)
        own=owner_of(rows,me,unit,128).reshape(total,SMALL,128)[:,0,:1]
        ups=jnp.where(owned(jnp.broadcast_to(own,(total,FF)),FF//total),dupb_ref[...],0.0).astype(BF)
        ups=mm(ups,repeats(FF,FF//total),NT)
        line=jnp.bitwise_and(lax.broadcasted_iota(jnp.int32,(rows,128),0),SMALL-1)
        ups=jnp.broadcast_to(ups[:,None,:],(total,SMALL,128)).reshape(rows,128)
        vec=jnp.where(line==UP_B,ups,jnp.where((line>=4)&(line<UP_B),vec,0.0))
        small=mm(three(feat_ref[...]),spread3(rows_ref[2:3,:]),TN)
        small=small+jnp.concatenate([vec,jnp.zeros((rows,D-128),F32)],axis=1)
        small=small.astype(BF)
        for t in range(8): to(t)[t%4,4*n:,:]=small[t*ns:(t+1)*ns]
    part=mm(inp_ref[...],jnp.concatenate([s[w] for w in range(3) for s in grads],axis=1),TN)
    @pl.when(i==0)
    def _(): acc[:,:3*D]=part
    @pl.when(i>0)
    def _(): acc[:,:3*D]+=part
    @pl.when(i==pl.num_programs(0)-1)
    def _():
        for t in range(8):
            for w in range(4): to(t)[t%4,w*n:(w+1)*n,:]=acc[rows_at(me,t,n),w*D:(w+1)*D].astype(BF)
def weight_grads(me,inp,rows,hid,feat,dvec,dupb,grads,unit):
    L,D=inp.shape; R=min(STEP,L); n=D//8; nc=len(grads)
    outs=[sds((4,4*n+feat.shape[1]//8,D),BF)]*2
    full=lambda a: pl.BlockSpec(a.shape,lambda i:(0,)*a.ndim)
    return pl.pallas_call(functools.partial(weight_kernel,nc,unit),grid=(L//R,),
      in_specs=[smem(),pl.BlockSpec((R,D),lambda i:(i,0))]+[full(a) for a in (rows,hid,feat,dvec,dupb)]+[pl.BlockSpec((3,R,a.shape[2]),lambda i:(0,i,0)) for a in grads],
      out_specs=[once(o) for o in outs],out_shape=outs,
      scratch_shapes=[pltpu.VMEM((D,4*D),F32)],
      compiler_params=pltpu.CompilerParams(vmem_limit_bytes=60*2**20),
      cost_estimate=pl.CostEstimate(flops=2*L*D*D*3,bytes_accessed=12_000_000,transcendentals=0),
      name="weight_grads")(me,inp,rows,hid,feat,dvec,dupb,*grads)
LB=384
def room(rows): return (60 if rows>512 else 20)*2**20
def take(k,R): return pl.BlockSpec((1,R,LB),lambda i:(k,0,i))
def flat(R): return pl.BlockSpec((R,LB),lambda i:(0,i))
def total_of(refs):
    out=refs[0].astype(F32)
    for r in refs[1:]: out=out+r.astype(F32)
    return out
def three_kernel(a1,b1,a2,b2,a3,b3,o1,o2,o3):
    for a,b,o in ((a1,b1,o1),(a2,b2,o2),(a3,b3,o3)): o[...]=total_of((a[0],b[0])).astype(BF)
def sum_three(mine,got):
    _,R,D=mine.shape
    return pl.pallas_call(three_kernel,grid=(D//LB,),in_specs=[take(1,R)]*2+[take(2,R)]*2+[take(3,R)]*2,
      out_specs=[flat(R)]*3,out_shape=[sds((R,D),BF)]*3,compiler_params=pltpu.CompilerParams(vmem_limit_bytes=room(R)),name="sum_three")(mine,got,mine,got,mine,got)
def inner_rows(scr,tmp,sizes,unit,k):
    at=0; out=0
    for count,size in sizes:
        for c in range(count):
            tmp[out:out+size,:]=scr[pl.ds(pl.multiple_of(at+k*size,8),size),:]
            at+=unit*size; out+=size
    return tmp[...]
def own_kernel(sizes,unit,nx,inner_ref,a,b,*rest):
    more=rest[:nx]; keep,send,scr,tmp=rest[nx:]
    scr[...]=total_of((a[0],b[0])+tuple(x[...] for x in more))
    for j in range(unit):
        dst=send if j%2 else keep
        dst[j//2]=inner_rows(scr,tmp,sizes,unit,jnp.bitwise_xor(inner_ref[0],j)).astype(dst.dtype)
def sum_own(inner,mine,got,more,sizes,unit):
    _,R,D=mine.shape; rows=R//unit
    if any(size%8 for _,size in sizes):
        x=mine[0].astype(F32)+got[0].astype(F32)+sum(m.astype(F32) for m in more); at=0; parts=[]
        for count,size in sizes:
            for c in range(count):
                parts.append(x[at:at+unit*size].reshape(unit,size,D)); at+=unit*size
        x=in_order(jnp.concatenate(parts,1),inner)
        return jnp.stack([x[j] for j in range(0,unit,2)]),jnp.stack([x[j] for j in range(1,unit,2)]).astype(BF)
    blk=pl.BlockSpec((unit//2,rows,LB),lambda i:(0,0,i))
    keep,send=pl.pallas_call(functools.partial(own_kernel,sizes,unit,len(more)),grid=(D//LB,),
      in_specs=[smem()]+[take(0,R)]*2+[flat(R)]*len(more),out_specs=[blk]*2,
      out_shape=[sds((unit//2,rows,D),F32),sds((unit//2,rows,D),BF)],scratch_shapes=[pltpu.VMEM((R,LB),F32),pltpu.VMEM((rows,LB),F32)],compiler_params=pltpu.CompilerParams(vmem_limit_bytes=room(R)),name="sum_own")(inner.reshape(1).astype(jnp.int32),mine,got,*more)
    return keep,send
def direct_kernel(sizes,unit,nx,inner_ref,a,b,*rest):
    more=rest[:nx]; outs=rest[nx:nx+unit]; scr,tmp=rest[nx+unit:]
    scr[...]=total_of((a[0],b[0])+tuple(x[...] for x in more))
    for j,dst in enumerate(outs):
        dst[...]=inner_rows(scr,tmp,sizes,unit,jnp.bitwise_xor(inner_ref[0],j)).astype(dst.dtype)
def sum_direct(inner,mine,got,more,sizes,unit):
    _,R,D=mine.shape; rows=R//unit
    if any(size%8 for _,size in sizes):
        x=mine[0].astype(F32)+got[0].astype(F32)+sum(m.astype(F32) for m in more); at=0; parts=[]
        for count,size in sizes:
            for c in range(count):
                parts.append(x[at:at+unit*size].reshape(unit,size,D)); at+=unit*size
        x=in_order(jnp.concatenate(parts,1),inner)
        return [x[0]]+[x[j].astype(BF) for j in range(1,unit)]
    return pl.pallas_call(functools.partial(direct_kernel,sizes,unit,len(more)),grid=(D//LB,),
      in_specs=[smem()]+[take(0,R)]*2+[flat(R)]*len(more),out_specs=[flat(rows)]*unit,
      out_shape=[sds((rows,D),F32)]+[sds((rows,D),BF)]*(unit-1),scratch_shapes=[pltpu.VMEM((R,LB),F32),pltpu.VMEM((rows,LB),F32)],
      compiler_params=pltpu.CompilerParams(vmem_limit_bytes=room(R)),name="sum_direct")(inner.reshape(1).astype(jnp.int32),mine,got,*more)
def last1_kernel(ng,*refs):
    x=total_of([r[...] for r in refs[:ng]]); outs=refs[ng:]
    *mats,st=outs[:5]; n=mats[0].shape[0]
    for w,o in enumerate(mats): o[...]=x[w*n:(w+1)*n]
    st[...]=x[4*n:4*n+st.shape[0]]
    for r,o in enumerate(outs[5:]):
        o[...]=x[4*n+4+r:4*n+5+r,:o.shape[0]].reshape(o.shape)
def last1(given,n,stamp_rows,sizes):
    D=given[0].shape[1]
    vm=pl.BlockSpec(memory_space=pltpu.VMEM)
    outs=[sds((n,D),F32)]*4+[sds((stamp_rows,D),F32)]+[sds((k,),F32) for k in sizes]
    if n%8:
        x=sum(g.astype(F32) for g in given)
        return [x[w*n:(w+1)*n] for w in range(4)]+[x[4*n:4*n+stamp_rows]]+[x[4*n+4+r,:k] for r,k in enumerate(sizes)]
    return pl.pallas_call(functools.partial(last1_kernel,len(given)),in_specs=[vm]*len(given),out_specs=[vm]*len(outs),out_shape=outs,
      compiler_params=pltpu.CompilerParams(vmem_limit_bytes=12*2**20),name="last_attn")(*given)
def last2_kernel(keep_ref,got_ref,wo,wd,wu):
    x=keep_ref[...]+got_ref[...].astype(F32); n,D=wo.shape; m=wd.shape[0]
    wo[...]=x[:n]; wd[...]=x[n:n+m]
    for c in range(wu.shape[1]//D): wu[:,c*D:(c+1)*D]=x[n+m+c*n:n+m+(c+1)*n]
def last2(keep,got,n,m,FF):
    D=keep.shape[1]
    vm=pl.BlockSpec(memory_space=pltpu.VMEM)
    outs=[sds((n,D),F32),sds((m,D),F32),sds((n,FF),F32)]
    if n%8:
        x=keep+got.astype(F32)
        return x[:n],x[n:n+m],jnp.concatenate([x[n+m+c*n:n+m+(c+1)*n] for c in range(FF//D)],1)
    return pl.pallas_call(last2_kernel,in_specs=[vm]*2,out_specs=[vm]*3,out_shape=outs,compiler_params=pltpu.CompilerParams(vmem_limit_bytes=12*2**20),name="last_ffn")(keep,got)

INV_SQRT2=0.7071067811865476; INV_SQRT2PI=0.3989422804014327
HEAD=64
RB=256; FC=768
def norm_stats(x):
    mu=jnp.mean(x,axis=1,keepdims=True); c=x-mu
    r=lax.rsqrt(jnp.mean(c*c,axis=1,keepdims=True)+1e-5)
    return c*r,r
def norm_back(e,n,r):
    return r*(e-jnp.mean(e,axis=1,keepdims=True)-n*jnp.mean(e*n,axis=1,keepdims=True))
def colsum(x): return jnp.sum(x,axis=0,keepdims=True)
def mid_kernel(nblk,me_ref,info_ref,mix_ref,cot_refs,att_refs,vec_ref,upb_ref,pieces,
        out_refs,gas_ref,gatt_ref,auxd_ref,mine_ref,theirs_ref,dvec_ref,dupb_ref,
        wo,wd,wu,cot,res,atta,hida,gda,gba,gel,gup,dgel,sems):
    i=pl.program_id(0); nb=pl.num_programs(0)
    D=wo.shape[0]; FF=wd.shape[0]; ro=D//nblk; rd=FF//nblk
    me=me_ref[0]
    lower=[p[0] if isinstance(p,tuple) else p for p in pieces]
    upper=[(p[1],0) if isinstance(p,tuple) else (p,ro+rd) for p in pieces]
    cps=[load_weights(me,lower,0,ro,wo,sems.at[0]),
        [pltpu.make_async_copy(p.at[pl.ds(at+b*ro,ro),:],wu.at[rows_at(me,t,ro),pl.ds(b*D,D)],sems.at[1])
            for b in range(FF//D) for t,(p,at) in enumerate(upper)],
        load_weights(me,lower,ro,rd,wd,sems.at[2])]
    cps[0]+=[pltpu.make_async_copy(src,cot.at[c],sems.at[0]) for c,src in enumerate(cot_refs)]
    def wait(which):
        @pl.when(i==0)
        def _():
            for c in cps[which]: c.wait()
    @pl.when(i==0)
    def _():
        for w in cps:
            for c in w: c.start()
        dvec_ref[...]=jnp.zeros_like(dvec_ref); dupb_ref[...]=jnp.zeros_like(dupb_ref)
    vec=lambda r: vec_ref[pl.ds(r,1),:].astype(F32)
    nlive=info_ref[i,1]
    x0=mix_ref[...]
    live=(lax.broadcasted_iota(jnp.int32,(RB,1),0)<nlive).astype(F32)
    wait(0)
    att=jnp.concatenate([a[...] for a in att_refs],axis=1)
    rows=pl.ds(pl.multiple_of(i*RB,RB),RB)
    atta[rows,:]=att
    asum=x0+(mm(att,wo[...],NN)+vec(OUT_B))
    n1,r1=norm_stats(asum)
    normed=n1*vec(ATT_G)+vec(ATT_S)
    hid=normed.astype(BF)
    hida[rows,:]=hid
    wait(1); wait(2)
    down=None
    for f in range(FF//FC):
        c=slice(f*FC,(f+1)*FC)
        u=mm(hid,wu[:,c],NN)+upb_ref[:,c].astype(F32)
        ph=0.5+0.5*lax.erf(u*INV_SQRT2)
        pd=jnp.exp(u*u*-0.5)*INV_SQRT2PI
        g=(u*ph).astype(BF)
        gel[rows,c]=g
        dgel[:,c]=ph+u*pd
        t=mm(g,wd[c,:],NN)
        down=t if down is None else down+t
    fsum=normed+(down+vec(DOWN_B))
    n2,r2=norm_stats(fsum)
    g2=vec(FFN_G)
    res[i]=((n2*g2+vec(FFN_S))*live).astype(BF)
    og=cot[i].astype(F32)*live
    dvec_ref[pl.ds(FFN_G,1),:]+=colsum(og*n2)
    dvec_ref[pl.ds(FFN_S,1),:]+=colsum(og)
    gf=norm_back(og*g2,n2,r2)
    gd=gf.astype(BF)
    gda[rows,:]=gd
    dvec_ref[pl.ds(DOWN_B,1),:]+=colsum(gd.astype(F32))
    gn=gf
    for f in range(FF//FC):
        c=slice(f*FC,(f+1)*FC)
        gu=(mm(gd,wd[c,:],NT)*dgel[:,c]).astype(BF)
        dupb_ref[:,c]+=colsum(gu.astype(F32))
        gup[rows,c]=gu
        gn=gn+mm(gu,wu[:,c],NT)
    dvec_ref[pl.ds(ATT_G,1),:]+=colsum(gn*n1)
    dvec_ref[pl.ds(ATT_S,1),:]+=colsum(gn)
    ga=norm_back(gn*vec(ATT_G),n1,r1)
    gas_ref[...]=ga
    gb=ga.astype(BF)
    dvec_ref[pl.ds(OUT_B,1),:]+=colsum(gb.astype(F32))
    gba[rows,:]=gb
    gatt=mm(gb,wo[...],NT).astype(BF)
    gatt_ref[...]=gatt
    pr=-(gatt.astype(F32)*att.astype(F32))
    hi,mid,lo=split3(pr)
    hrow=lax.broadcasted_iota(jnp.int32,(D,128),0)//64
    hcol=lax.broadcasted_iota(jnp.int32,(D,128),1)
    ind=((hcol>=3*hrow)&(hcol<3*hrow+3)).astype(BF)
    dl=mm(hi.astype(BF),ind,NN)+mm(mid.astype(BF),ind,NN)
    h2,m2,l2=split3(dl)
    ln=lanes(dl.shape)%3
    auxd_ref[...]=jnp.where(ln==0,h2,jnp.where(ln==1,m2,l2)).astype(BF)
    @pl.when(i==nb-1)
    def _():
        def send(src,at,n):
            cps=[pltpu.make_async_copy(src.at[rows_at(me,t,n),:],(mine_ref if t<4 else theirs_ref).at[t%4,pl.ds(at,n),:],sems.at[3]) for t in range(8)]
            for c in cps: c.start()
            return cps
        out=[pltpu.make_async_copy(res.at[c],dst,sems.at[3]) for c,dst in enumerate(out_refs)]
        for c in out: c.start()
        for b in range(FF//D):
            c=slice(b*D,(b+1)*D)
            wd[c,:]=mm(gel[:,c],gda[...],TN).astype(BF)
        out+=send(wd,ro,rd)
        wo[...]=mm(atta[...],gba[...],TN).astype(BF)
        out+=send(wo,0,ro)
        for b in range(FF//D):
            c=slice(b*D,(b+1)*D)
            wu[:,c]=mm(hida[...],gup[:,c],TN).astype(BF)
            out+=send(wu.at[:,pl.ds(b*D,D)],ro+rd+b*ro,ro)
        for c in out: c.wait()
def middle(me,info,mixed,cots,atts,vec,upb,pieces):
    nblk=8; L,D=mixed.shape; FF=upb.shape[1]; ro=D//8; rd=FF//8
    nb=L//RB; na=len(atts); nt=len(cots)
    flat_pieces=jax.tree.leaves(pieces)
    def kern(me_ref,info_ref,mix_ref,*rest):
        cot=rest[:nt]; att=rest[nt:nt+na]; rest=rest[nt+na:]
        given=iter(rest[2:2+len(flat_pieces)])
        blocks=[(next(given),next(given)) if isinstance(p,tuple) else next(given) for p in pieces]
        rest_out=rest[2+len(flat_pieces):]
        mid_kernel(nblk,me_ref,info_ref,mix_ref,cot,att,rest[0],rest[1],blocks,rest_out[:nt],*rest_out[nt:])
    full=lambda a: pl.BlockSpec(a.shape,lambda i:(0,)*a.ndim)
    row=pl.BlockSpec((RB,D),lambda i:(i,0))
    outs=[sds((RB,D),BF)]*nt+[sds((L,D),F32),sds((L,D),BF),sds((L,128),BF)]+[sds((4,)+pieces[0].shape,BF)]*2+[sds((16,D),F32),sds((1,FF),F32)]
    return pl.pallas_call(kern,grid=(nb,),
      in_specs=[smem(),smem(),row]+[anyw()]*nt+[pl.BlockSpec((RB,a.shape[1]),lambda i:(i,0)) for a in atts]+[full(vec),full(upb)]+[anyw()]*len(flat_pieces),
      out_specs=[anyw()]*nt+[row,row,pl.BlockSpec((RB,128),lambda i:(i,0)),anyw(),anyw()]+[once(s) for s in outs[nt+5:]],
      out_shape=outs,
      scratch_shapes=[pltpu.VMEM((D,D),BF),pltpu.VMEM((FF,D),BF),pltpu.VMEM((D,FF),BF),
        pltpu.VMEM((nt,RB,D),BF),pltpu.VMEM((nt,RB,D),BF)]+[pltpu.VMEM((L,D),BF)]*4+[pltpu.VMEM((L,FF),BF)]*2+[
        pltpu.VMEM((RB,FF),F32),pltpu.SemaphoreType.DMA((4,))],
      compiler_params=pltpu.CompilerParams(vmem_limit_bytes=61*2**20),
      cost_estimate=pl.CostEstimate(flops=2*L*D*(3*D+6*FF),bytes_accessed=60_000_000,transcendentals=2*L*FF),
      name="middle")(me,info,mixed,*cots,*atts,vec,upb,*flat_pieces)

GROUPS=8
AXES=("seq","stream")
def flip(x,mask,total):
    return lax.ppermute(x,AXES,[(i,i^mask) for i in range(total)])
def far_first(count):
    bits=[]; bit=count//2
    while bit: bits.append(bit); bit//=2
    return bits
def widen(x,bit,total): return jnp.concatenate([x,flip(x,bit,total)])
def settle(x,inner,count):
    ids=[0]
    for bit in far_first(count): ids=ids+[i^bit for i in ids]
    return in_order(jnp.stack([x[ids.index(k)] for k in range(count)]),inner)
def in_order(x,index):
    n=x.shape[0]; bit=1
    while bit<n:
        turned=jnp.concatenate([x[k^bit][None] for k in range(n)])
        x=jnp.where((index&bit)!=0,turned,x); bit*=2
    return x
def after(x,*deps):
    return lax.optimization_barrier((x,)+deps)[0]
def sync(*xs): return lax.optimization_barrier(xs)
def spread_start(own,unit,total):
    across=lambda x,g: flip(x,g*unit,total)
    return [own,across(own,2),across(own,4)]
def split_send(x,bit,total):
    send=jnp.stack([x[j] for j in range(1,x.shape[0],2)]).astype(BF)
    return jnp.stack([x[j] for j in range(0,x.shape[0],2)]),flip(send,bit,total)
def finish2(keep,got,total):
    bit=2
    while keep.shape[0]>1:
        keep,got=split_send(keep+got.astype(F32),bit,total); bit*=2
    return keep[0],got[0]
def on_device(tokens,source_len,target_len,timesteps,cotangent,query_weight,query_bias,key_weight,value_weight,value_bias,
        out_weight,out_bias,attn_gain,attn_shift,up_weight,up_bias,down_weight,down_bias,ffn_gain,ffn_shift,
        stamp_weight,stamp_bias,embed_weight,embed_bias):
    seqs,R,D=tokens.shape
    streams=lax.axis_size("stream"); seq_size=lax.axis_size("seq"); total=seq_size*streams
    s0=lax.axis_index("stream"); flat=lax.axis_index("seq")*streams+s0
    unit=total//GROUPS
    inner=flat%unit; group=flat//unit
    me=group.astype(jnp.int32).reshape(1)
    n=D//GROUPS; shard=D//total; stamp_rows=stamp_weight.shape[0]; FF=up_weight.shape[1]; ff_shard=FF//total
    vecs=(query_bias,value_bias,out_bias,attn_gain,attn_shift,down_bias,ffn_gain,ffn_shift,stamp_bias,embed_bias,up_bias)
    first,second=pack((query_weight,key_weight,value_weight,embed_weight,stamp_weight,out_weight,down_weight,up_weight),vecs)
    def rowwise(x,sizes):
        at=0; out=[]
        for count,size in sizes:
            part=x[:,at:at+count*size].reshape(unit,count,size,x.shape[2])
            out.append(part.transpose(1,0,2,3).reshape(count*unit*size,x.shape[2])); at+=count*size
        return jnp.concatenate(out) if len(out)>1 else out[0]
    def exchange(chunks):
        return [x if c==0 else flip(x,c,total) for c,x in enumerate(chunks)]
    def chunks_of(x): return [lax.dynamic_index_in_dim(x,s0^c,0,keepdims=False) for c in range(streams)]
    order=jnp.asarray(ORDER,jnp.int32)
    source=source_len[s0]; target=target_len[s0]; stamp=timesteps[s0]
    half=R*streams//2
    place=(s0^jnp.arange(streams))*R
    flag=(place>=half).astype(jnp.int32)
    nlive=jnp.clip(jnp.where(flag==1,target-(place-half),source-place),0,R).astype(jnp.int32)
    info=jnp.stack([flag,nlive],1)
    tdim=stamp_rows*total; halfway=tdim//2
    t_ids=(((order^group)[:,None,None]*unit+jnp.arange(unit)[None,:,None])*stamp_rows+jnp.arange(SMALL)[None,None,:])
    valid=(jnp.arange(SMALL)<stamp_rows)[None,None,:]
    t_ids=jnp.where(valid,t_ids,0).reshape(-1)
    rates=jnp.exp(-math.log(10000.0)*(t_ids%halfway).astype(F32)/halfway)
    angle=stamp.astype(F32)*rates
    feats=jnp.where(t_ids<halfway,jnp.sin(angle),jnp.cos(angle))
    feats=jnp.where(jnp.broadcast_to(valid,(GROUPS,unit,SMALL)).reshape(-1),feats,0.0)
    feat=jnp.broadcast_to(feats.astype(BF)[None],(8,feats.shape[0]))
    bits=far_first(unit)
    first=widen(first[None],bits[0],total)
    first,second=sync(first,second)
    second=widen(second[None],bits[0],total)
    for bit in bits[1:]: first=widen(first,bit,total)
    first=rowwise(settle(first,inner,unit),((4,shard),(1,SMALL)))
    cells=chunks_of(tokens)
    first,second,feat,info,*cells=sync(first,second,feat,info,*cells)
    for bit in bits[1:]: second=widen(second,bit,total)
    n1=[first]+[flip(first,g*unit,total) for g in (2,4,6)]
    toks=[cells[0]]+[None]*(streams-1)
    early,late=list(range(2,streams)),[1]
    for c in early: toks[c]=flip(cells[c],c,total)
    n1[1],n1[2],toks[2],second=sync(n1[1],n1[2],toks[2],second)
    second=rowwise(settle(second,inner,unit),((1,shard),(1,ff_shard),(FF//D,shard)))
    for c in late: toks[c]=flip(after(cells[c],second),c,total)
    n2=spread_start(second,unit,total)
    p1=n1+[flip(x,unit,total) for x in n1]
    *cells,_=sync(*chunks_of(cotangent),toks)
    far=[flip(n2[0],unit,total)]
    cots=[cells[0]]+[flip(cells[c],c,total) for c in range(1,streams-1)]
    mixed,inputs,q,k,v,auxk,pre,hid,vec,upb=project(me,info,feat,toks,p1,unit,FF)
    pairs=D//(2*HEAD); parts=(2,pairs-2)
    atts=[];auxq=[]
    def forward(c,q):
        a,x=attn_fwd(q,k,v,auxk,sum(parts[:c]),parts[c]); atts.append(a); auxq.append(x)
    forward(0,q)
    q,n2,far,cots,cells,atts=sync(q,n2,far,cots,cells,atts)
    cut=n+FF//GROUPS
    low=flip(n2[2][:cut],2*unit,total); high=flip(n2[1][cut:],4*unit,total)
    cots.append(flip(cells[streams-1],streams-1,total))
    far+=[flip(n2[1],unit,total),flip(n2[2],unit,total)]
    forward(1,q)
    low,high,far,atts,cots=sync(low,high,far,atts,cots)
    diag=(low,high)
    p2=n2+[diag]+far+[tuple(flip(x,unit,total) for x in diag)]
    *output,ga,gatt,auxd,mine2,theirs2,dvec,dupb=sync(*middle(me,info,mixed,cots,atts,vec,upb,p2))
    grads=[]
    def backward(c,q):
        grads.append(attn_bwd(q,k,v,gatt,auxk,auxq[c],auxd,sum(parts[:c]),parts[c],0))
    got=flip(theirs2,unit,total)
    backs=[output[0],flip(output[1],1,total)]
    backward(0,q)
    got,q,output,backs,grads=sync(got,q,output,backs,grads)
    fx,fy,fd=(flip(x,g*unit,total) for x,g in zip(sum_three(mine2,got),(2,4,6)))
    backs+=[flip(output[c],c,total) for c in range(2,streams)]
    out,*tg,rows4=attn_finish(me,info,(q,k,v,gatt,auxk,auxq[1],auxd),ga,pre,grads[0],p1,parts[0],parts[1],R)
    grads.append(out)
    def place(chunks,dtype):
        out=jnp.zeros((seqs,R,D),dtype)
        for c,part in enumerate(chunks):
            out=lax.dynamic_update_index_in_dim(out,part.astype(dtype),s0^c,0)
        return out
    tg,rows4,backs=sync(tg,rows4,backs)
    held=[flip(tg[c],c,total) for c in range(streams-2,0,-1)][::-1]
    mine1,theirs1=weight_grads(me,inputs,rows4,hid,feat,dvec,dupb,grads,unit)
    mine1,theirs1,fx,fy,fd,held=sync(mine1,theirs1,fx,fy,fd,held)
    keep2,send2=sum_own(inner,mine2,got,(fx,fy,fd),((1,shard),(1,ff_shard),(FF//D,shard)),unit)
    got1=flip(theirs1,unit,total)
    keep2,send2,tg=sync(keep2,send2,tg)
    got2=flip(send2,1,total)
    tgs=[tg[0]]+held+[flip(tg[streams-1],streams-1,total)]
    blocks=sum_three(mine1,got1)
    fx,fy,fd=(flip(x,g*unit,total) for x,g in zip(blocks,(2,4,6)))
    keep2,got2=finish2(keep2,got2,total)
    fx,fy,fd,keep2,got2,tgs=sync(fx,fy,fd,keep2,got2,tgs)
    output=place(backs,BF)
    dwo,dwd,dwu=last2(keep2,got2,shard,ff_shard,FF)
    keep1,*sends=sum_direct(inner,mine1,got1,(fx,fy,fd),((4,shard),(1,SMALL)),unit)
    given=[keep1]+[flip(x,c+1,total) for c,x in reversed(list(enumerate(sends)))]
    dwq,dwk,dwv,dwe,dws,bq,bv,bo,ag,as_,bd,fg,fs,bs,be,bu=last1(given,shard,stamp_rows,[shard]*10+[ff_shard])
    token_grad=place(tgs,F32)
    return (output,token_grad,dwq,bq,dwk,dwv,bv,dwo,bo,ag,as_,dwu,bu,dwd,bd,fg,fs,dws,bs,dwe,be)

def solution(mesh):
    cells=P("seq","stream",None); per=P("seq"); mat=P(("seq","stream"),None); row=P(("seq","stream"))
    return jax.shard_map(on_device,mesh=mesh,
        in_specs=(cells,per,per,per,cells,mat,row,mat,mat,row,mat,row,row,row,mat,row,mat,row,row,row,mat,row,mat,row),
        out_specs=(cells,cells,mat,row,mat,mat,row,mat,row,row,row,mat,row,mat,row,row,row,mat,row,mat,row),
        check_vma=False)
```
